32 devices in a mesh: dp: 8 (over z, core), expert: 4 (over y, x).
Axes of the slice: x: 2, y: 2, z: 4, core: 2. Of those that a mesh axis runs over, the one named last changes fastest.
Arguments:
- tokens: bfloat16 [1024, 2048], P(('dp', 'expert')), may hold values from -6 to 6
- routes: int32 [1024, 6], P(('dp', 'expert')), may hold values from 0 to 31, all different within a row; in each aligned block of 32 rows (0 to 31, 32 to 63, ...) at most 7 rows name the same one
- weights_fwd: float32 [1024, 6], P(('dp', 'expert')), may hold values from 0.05 to 0.45
- cotangent: bfloat16 [1024, 2048], P(('dp', 'expert')), may hold values from -6 to 6
- routes_back: int32 [1024, 6], P(('dp', 'expert')), may hold values from 0 to 31, all different within a row; in each aligned block of 32 rows (0 to 31, 32 to 63, ...) at most 7 rows name the same one
- weights_back: float32 [1024, 6], P(('dp', 'expert')), may hold values from 0.05 to 0.45
- saved_gate: bfloat16 [8, 4, 32, 7, 704], P('dp', None, 'expert'), may hold values from -5 to 5
- saved_up: bfloat16 [8, 4, 32, 7, 704], P('dp', None, 'expert'), may hold values from -5 to 5
- w_gate: bfloat16 [32, 2048, 704], P('expert'), may hold values from -0.125 to 0.125
- w_up: bfloat16 [32, 2048, 704], P('expert'), may hold values from -0.125 to 0.125
- w_down: bfloat16 [32, 704, 2048], P('expert'), may hold values from -0.21875 to 0.21875
Outputs:
- mixed: bfloat16 [1024, 2048], P(('dp', 'expert'))
- input_grad: bfloat16 [1024, 2048], P(('dp', 'expert'))
- weight_grad: float32 [1024, 6], P(('dp', 'expert'))
The draws below stay inside these ranges and needn't reach their ends.
Inputs may be any that keep to these rules, and one draw needn't show every extreme that they name: `routes`: each row names 6 different experts; among the 32 rows of one device no expert is named more than 7 times, and in every draw some expert is named exactly 7 times by one device. `routes_back`: each row names 6 different experts; among the 32 rows of one device no expert is named more than 7 times, and in every draw some expert is named exactly 7 times by one device.
All inputs are finite; a program needn't handle non-finite values.
Results may differ from the reference program's by a relative error of at most 0.0057.
Values may be sent and summed in bfloat16 or wider, within the bound.
No kernel may reach another device: no remote copies, remote signals or barrier semaphores. Data moves between devices by JAX's collectives and lax.ppermute only.
A program may use at most 128 MiB of HBM per device.

```python
import math
import jax
import jax.numpy as jnp
import numpy as np

D = 2048
FF = 704
EXPERTS = 32
TOPK = 6
TOK_DEV = 32
CAP = 7
TOKENS = 1024
N_DP = 8
N_EXPERT = 4
DEVICES = 32


def level_of(own_key, dims, split, low, high):
    def one(position, parts):
        heights = jax.random.uniform(jax.random.fold_in(jax.random.fold_in(own_key, 6), position), (parts,), jnp.float32, low / len(split), high / len(split))
        return jnp.repeat(jnp.exp(heights), dims[position] // parts).reshape((-1,) + (1,) * (len(dims) - position - 1))

    gain = one(*split[0])
    for cut in split[1:]:
        gain = gain * one(*cut)
    return gain


def deal_out(rng, own, number, rows, amount, top, limit, skew):
    order = jax.random.permutation(rng, amount)
    packed, common = portions_of(amount, rows * top, limit, skew, True), portions_of(amount, rows * top, limit, skew, False)
    places = jnp.arange(amount)

    def named(lengths, rotation):
        used = int((lengths > 0).sum())
        fixed = max(1, used // 4)
        shifted = fixed + (places - fixed + rotation * (used - fixed)) % max(1, amount - fixed)
        return jnp.zeros((amount,), jnp.int32).at[order[jnp.where(places < fixed, places, shifted)]].set(jnp.asarray(lengths, jnp.int32))

    lengths = jnp.where(number % 4 == 0, named(packed, number // 4), named(common, number - number // 4 - 1))
    mixed = jax.random.permutation(jax.random.fold_in(own, 3), amount)
    donor, sink = mixed[0:amount // 2 * 2:2], mixed[1:amount // 2 * 2:2]
    slack = jnp.minimum(lengths[donor] - 1, limit - lengths[sink]) // 2
    slack = jnp.where((donor == order[0]) | (sink == order[0]) | (lengths[sink] == 0), 0, jnp.maximum(slack, 0))
    shifted = jax.random.randint(jax.random.fold_in(own, 4), (amount // 2,), 0, 1 << 20) % (slack + 1)
    lengths = lengths.at[donor].add(-shifted).at[sink].add(shifted)
    items = jnp.searchsorted(jnp.cumsum(lengths), jnp.arange(rows * top), side="right").astype(jnp.int32)
    table = items.reshape(top, rows).T
    table = table[jax.random.permutation(jax.random.fold_in(own, 1), rows)]
    rotation = jax.random.randint(jax.random.fold_in(own, 2), (rows, 1), 0, top)
    return jnp.take_along_axis(table, (jnp.arange(top)[None, :] + rotation) % top, axis=1)


def portions_of(amount, total, limit, lean, full):
    loads = [(1 << 20) // math.isqrt(standing ** lean) + 1 for standing in range(1, amount + 1)]
    largest = limit if full else min(limit, max(-(-total // amount), total * loads[0] // sum(loads)))
    least = 1 if total - largest >= amount - 1 else 0
    holding, rest = [largest] + [least] * (amount - 1), total - largest - least * (amount - 1)
    while rest > 0:
        free = [i for i in range(1, amount) if holding[i] < largest] or [i for i in range(1, amount) if holding[i] < limit]
        pool, budget = sum([loads[i] for i in free]), rest
        for i in free:
            addition = min(limit - holding[i], max(1, budget * loads[i] // pool), rest)
            holding[i] = holding[i] + addition
            rest = rest - addition
    return np.array(holding)


def normal_values(own_key, extent, scale, most, pieces=(), kind=jnp.bfloat16):
    factor_of = level_of(own_key, extent, pieces, -0.22, 0.18) if pieces else 1.0
    drawn = jax.random.normal(own_key, extent, jnp.float32) * scale * factor_of
    return jnp.minimum(jnp.maximum(drawn, -most), most).astype(kind)


def setup_inputs(seed: int = 0) -> dict:
    arg_keys = jax.random.split(jax.random.key(seed), 12)
    tokens = normal_values(arg_keys[0], (TOKENS, D), 1.0, 6.0, ((0, 32),))
    routes_keys = jax.random.split(jax.random.fold_in(arg_keys[1], 1), TOKENS // TOK_DEV)
    routes_turns = jax.random.permutation(jax.random.fold_in(arg_keys[1], 3), TOKENS // TOK_DEV)
    routes = jax.vmap(lambda own, number: deal_out(jax.random.fold_in(arg_keys[1], 2), own, number, TOK_DEV, EXPERTS, TOPK, CAP, 2))(routes_keys, routes_turns).reshape((TOKENS, TOPK))
    weights_fwd = jnp.clip(0.05 + 0.39999999 * jax.random.uniform(arg_keys[2], (TOKENS, TOPK), jnp.float32) ** level_of(arg_keys[2], (TOKENS, TOPK), ((0, 32),), -0.2, 0.2), 0.05, 0.45)
    cotangent = normal_values(arg_keys[3], (TOKENS, D), 1.0, 6.0, ((0, 32),))
    routes_back_keys = jax.random.split(jax.random.fold_in(arg_keys[4], 1), TOKENS // TOK_DEV)
    routes_back_turns = jax.random.permutation(jax.random.fold_in(arg_keys[4], 3), TOKENS // TOK_DEV)
    routes_back = jax.vmap(lambda own, number: deal_out(jax.random.fold_in(arg_keys[4], 2), own, number, TOK_DEV, EXPERTS, TOPK, CAP, 2))(routes_back_keys, routes_back_turns).reshape((TOKENS, TOPK))
    weights_back = jnp.clip(0.05 + 0.39999999 * jax.random.uniform(arg_keys[5], (TOKENS, TOPK), jnp.float32) ** level_of(arg_keys[5], (TOKENS, TOPK), ((0, 32),), -0.2, 0.2), 0.05, 0.45)
    saved_gate = normal_values(arg_keys[6], (N_DP, N_EXPERT, EXPERTS, CAP, FF), 1.0, 5.0, ((0, 8), (2, 4)))
    saved_up = normal_values(arg_keys[7], (N_DP, N_EXPERT, EXPERTS, CAP, FF), 1.0, 5.0, ((0, 8), (2, 4)))
    w_gate = normal_values(arg_keys[8], (EXPERTS, D, FF), D ** -0.5, 0.125, ((0, 4),))
    w_up = normal_values(arg_keys[9], (EXPERTS, D, FF), D ** -0.5, 0.125, ((0, 4),))
    w_down = normal_values(arg_keys[10], (EXPERTS, FF, D), FF ** -0.5, 0.21875, ((0, 4),))
    return {"tokens": tokens, "routes": routes, "weights_fwd": weights_fwd, "cotangent": cotangent, "routes_back": routes_back, "weights_back": weights_back, "saved_gate": saved_gate, "saved_up": saved_up, "w_gate": w_gate, "w_up": w_up, "w_down": w_down}


def slot_places(ids):
    count, top = ids.shape
    flat = ids.reshape(-1)
    onehot = (flat[:, None] == jnp.arange(EXPERTS, dtype=jnp.int32)[None, :]).astype(jnp.int32)
    before = jnp.cumsum(onehot, axis=0) - onehot
    slot = jnp.sum(before * onehot, axis=1)
    return (flat * CAP + slot).reshape(count, top).astype(jnp.int32)


def dispatch(places, rows):
    count, top = places.shape
    table = (places.reshape(-1)[None, :] == jnp.arange(EXPERTS * CAP, dtype=jnp.int32)[:, None])
    table = jnp.sum(table.reshape(EXPERTS * CAP, count, top).astype(jnp.float32), axis=2)
    return jnp.dot(table, rows.astype(jnp.float32), preferred_element_type=jnp.float32).astype(jnp.bfloat16)


def combine(flat_out, places, factors):
    picked = flat_out[places].astype(jnp.float32)
    return jnp.sum(factors[:, :, None] * picked, axis=1)


def reference(tokens, routes, weights_fwd, cotangent, routes_back, weights_back, saved_gate, saved_up, w_gate, w_up, w_down):
    blocks = DEVICES
    wg = w_gate.astype(jnp.float32)
    wu = w_up.astype(jnp.float32)
    wd = w_down.astype(jnp.float32)
    places = jax.vmap(slot_places)(routes.reshape(blocks, TOK_DEV, TOPK))
    places_back = jax.vmap(slot_places)(routes_back.reshape(blocks, TOK_DEV, TOPK))
    buffer = jax.vmap(dispatch)(places, tokens.reshape(blocks, TOK_DEV, D)).reshape(blocks, EXPERTS, CAP, D)
    grad_buffer = jax.vmap(dispatch)(places_back, cotangent.reshape(blocks, TOK_DEV, D)).reshape(blocks, EXPERTS, CAP, D)
    xb = buffer.astype(jnp.float32)
    gate = jnp.einsum('becd,edf->becf', xb, wg)
    up = jnp.einsum('becd,edf->becf', xb, wu)
    hidden = (jax.nn.silu(gate) * up).astype(jnp.bfloat16)
    expert_out = jnp.einsum('becf,efd->becd', hidden.astype(jnp.float32), wd).astype(jnp.bfloat16)
    mixed = jax.vmap(combine)(expert_out.reshape(blocks, EXPERTS * CAP, D), places, weights_fwd.reshape(blocks, TOK_DEV, TOPK))
    mixed = mixed.reshape(TOKENS, D).astype(jnp.bfloat16)
    act_in = saved_gate.reshape(blocks, EXPERTS, CAP, FF).astype(jnp.float32)
    up_in = saved_up.reshape(blocks, EXPERTS, CAP, FF).astype(jnp.float32)
    grad_hidden = jnp.einsum('becd,efd->becf', grad_buffer.astype(jnp.float32), wd)
    sig = jax.nn.sigmoid(act_in)
    silu_in = act_in * sig
    score = jnp.sum(silu_in * up_in * grad_hidden, axis=3)
    grad_gate = (grad_hidden * up_in * sig * (1.0 + act_in * (1.0 - sig))).astype(jnp.bfloat16)
    grad_up = (grad_hidden * silu_in).astype(jnp.bfloat16)
    expert_grad = jnp.einsum('becf,edf->becd', grad_gate.astype(jnp.float32), wg) + jnp.einsum('becf,edf->becd', grad_up.astype(jnp.float32), wu)
    expert_grad = expert_grad.astype(jnp.bfloat16)
    input_grad = jax.vmap(combine)(expert_grad.reshape(blocks, EXPERTS * CAP, D), places_back, weights_back.reshape(blocks, TOK_DEV, TOPK))
    input_grad = input_grad.reshape(TOKENS, D).astype(jnp.bfloat16)
    weight_grad = jax.vmap(lambda flat, pl: flat[pl])(score.reshape(blocks, EXPERTS * CAP), places_back).reshape(TOKENS, TOPK)
    return mixed, input_grad, weight_grad
```

```python
import functools
import jax
import jax.numpy as jnp
from jax import lax
from jax.experimental import pallas as pl
from jax.experimental.pallas import tpu as pltpu
from jax.sharding import PartitionSpec as P

F32 = jnp.float32
BF16 = jnp.bfloat16
LANES = 128
MIB = 1 << 20


def round_up(value, unit):
    return -(-value // unit) * unit


def dot(a, b):
    return jnp.dot(a, b, preferred_element_type=F32)


def dot_tb(a, b):
    return lax.dot_general(a, b, (((1,), (1,)), ((), ())), preferred_element_type=F32)


def dot_ta(a, b):
    return lax.dot_general(a, b, (((0,), (0,)), ((), ())), preferred_element_type=F32)


def iota(shape, dim):
    return lax.broadcasted_iota(jnp.int32, shape, dim)


def vmem():
    return pl.BlockSpec(memory_space=pltpu.VMEM)


class Plan:
    def __init__(self, tokens, routes, saved_gate, w_gate):
        self.owners = lax.axis_size("expert")
        self.groups = lax.axis_size("dp")
        self.count, self.width = tokens.shape
        self.top = routes.shape[1]
        self.local = w_gate.shape[0]
        self.hidden = w_gate.shape[2]
        self.experts = self.owners * self.local
        self.cap = saved_gate.shape[3]
        self.cap_rows = round_up(self.cap, 8)
        self.split = 2 if self.groups % 2 == 0 and self.local % 2 == 0 else 1
        self.mine = self.local // self.split
        self.meta = round_up(3 * self.experts, LANES)
        self.blocks = self.split * self.owners
        self.source_rows = self.owners * self.cap_rows
        self.expert_rows = self.split * self.source_rows
        self.rows = self.mine * self.expert_rows
        self.cols = self.blocks * self.count

    def peer(self, index, step):
        if self.owners & (self.owners - 1) == 0:
            return index ^ step
        return (index + step) % self.owners

    def over_expert(self, x, step):
        pairs = [(self.peer(i, step), i) for i in range(self.owners)]
        return lax.ppermute(x, "expert", pairs)

    def back_over_expert(self, x, step):
        pairs = [(i, self.peer(i, step)) for i in range(self.owners)]
        return lax.ppermute(x, "expert", pairs)

    def over_pair(self, x):
        return lax.ppermute(x, "dp", [(i, i ^ 1) for i in range(self.groups)])


def pack_kernel(plan, x_ref, routes_ref, factors_ref, out_ref):
    experts, top = plan.experts, plan.top
    count = plan.count
    out_ref[:, : plan.width] = x_ref[...]
    lane = iota((plan.meta, count), 0)
    chosen = jnp.zeros((plan.meta, count), F32)
    parts = jnp.zeros((plan.meta, count), F32)
    for k in range(top):
        route = routes_ref[k : k + 1, :]
        factor = factors_ref[k : k + 1, :]
        high = factor.astype(BF16).astype(F32)
        low = factor - high
        chosen = chosen + jnp.where(lane == route, 1.0, 0.0)
        parts = parts + jnp.where(lane == route + experts, high, 0.0)
        parts = parts + jnp.where(lane == route + 2 * experts, low, 0.0)
    earlier = jnp.where(iota((count, count), 0) < iota((count, count), 1), 1.0, 0.0)
    before = dot(chosen.astype(BF16), earlier.astype(BF16))
    facts = (chosen * (before + 1.0) + parts).astype(BF16)
    shape = (plan.meta, plan.meta)
    same = jnp.where(iota(shape, 0) == iota(shape, 1), 1.0, 0.0).astype(BF16)
    out_ref[:, plan.width :] = dot_ta(facts, same).astype(BF16)


def pack(plan, x, routes, factors):
    return pl.pallas_call(
        functools.partial(pack_kernel, plan),
        out_shape=jax.ShapeDtypeStruct((plan.count, plan.width + plan.meta), BF16),
        in_specs=[vmem()] * 3,
        out_specs=vmem(),
        name="pack",
    )(x, routes.T, factors.T)


def first_expert(plan):
    core = lax.rem(lax.axis_index("dp"), plan.split)
    return lax.axis_index("expert") * plan.local + core * plan.mine, core * plan.mine


def tables(plan, meta, first):
    me = lax.axis_index("expert")
    row = iota((plan.rows, plan.meta), 0)
    lane = iota((plan.rows, plan.meta), 1)
    expert = first + row // plan.expert_rows
    pick_slot = jnp.where(lane == expert, 1.0, 0.0).astype(BF16)
    pick_part = jnp.where(
        (lane == expert + plan.experts) | (lane == expert + 2 * plan.experts), 1.0, 0.0
    ).astype(BF16)
    slot = dot_tb(pick_slot, meta)
    part = dot_tb(pick_part, meta)
    shape = (plan.rows, plan.cols)
    row = iota(shape, 0)
    col = iota(shape, 1)
    block = col // plan.count
    source = plan.peer(me, block % plan.owners)
    place = row % plan.expert_rows
    want = (row % plan.cap_rows + 1).astype(F32)
    same = (place // plan.cap_rows) == (block // plan.owners) * plan.owners + source
    hit = same & (slot == want)
    factor = jnp.sum(jnp.where(hit, part, 0.0), axis=1, keepdims=True)
    return jnp.where(hit, 1.0, 0.0).astype(BF16), factor


def weight_copies(plan, offset, arrays, slots, sems):
    copies = []
    for e in range(plan.mine):
        copies.append(
            [
                pltpu.make_async_copy(array.at[offset + e], slot.at[e], sems.at[e, i])
                for i, (array, slot) in enumerate(zip(arrays, slots))
            ]
        )
    for group in copies:
        for copy in group:
            copy.start()
    return copies


def forward_kernel(plan, *refs):
    blocks = refs[: plan.blocks]
    w_gate, w_up, w_down = refs[plan.blocks : plan.blocks + 3]
    outs = refs[plan.blocks + 3 : 2 * plan.blocks + 3]
    gate_s, up_s, down_s, x_s, y_s, sems = refs[2 * plan.blocks + 3 :]
    first, offset = first_expert(plan)
    copies = weight_copies(
        plan, offset, (w_gate, w_up, w_down), (gate_s, up_s, down_s), sems
    )
    meta = jnp.concatenate([b[:, plan.width :] for b in blocks], axis=0)
    rows = jnp.concatenate([b[:, : plan.width] for b in blocks], axis=0)
    table, factor = tables(plan, meta, first)
    x_s[...] = dot(table, rows).astype(BF16)
    n = plan.expert_rows
    for e in range(plan.mine):
        x = x_s[e * n : (e + 1) * n, :]
        copies[e][0].wait()
        gate = dot_tb(x, gate_s[e])
        copies[e][1].wait()
        up = dot_tb(x, up_s[e])
        hidden = (gate / (1.0 + jnp.exp(-gate)) * up).astype(BF16)
        copies[e][2].wait()
        out = dot(hidden, down_s[e])
        y_s[e * n : (e + 1) * n, :] = (out * factor[e * n : (e + 1) * n]).astype(BF16)
    mixed = dot_ta(table, y_s[...]).astype(BF16)
    for i, out in enumerate(outs):
        out[...] = mixed[i * plan.count : (i + 1) * plan.count, :]


def backward_kernel(plan, *refs):
    blocks = refs[: plan.blocks]
    refs = refs[plan.blocks :]
    saved = refs[: plan.split]
    w_gate, w_up, w_down = refs[plan.split : plan.split + 3]
    refs = refs[plan.split + 3 :]
    outs = refs[: plan.blocks]
    gate_s, up_s, down_s, x_s, y_s, score_s, sems = refs[plan.blocks :]
    first, offset = first_expert(plan)
    copies = weight_copies(
        plan, offset, (w_down, w_gate, w_up), (down_s, gate_s, up_s), sems
    )
    meta = jnp.concatenate([b[:, plan.width :] for b in blocks], axis=0)
    rows = jnp.concatenate([b[:, : plan.width] for b in blocks], axis=0)
    table, factor = tables(plan, meta, first)
    x_s[...] = dot(table, rows).astype(BF16)
    n = plan.expert_rows
    lane = iota((n, plan.meta), 1)
    for e in range(plan.mine):
        x = x_s[e * n : (e + 1) * n, :]
        act = jnp.concatenate([s[0, e] for s in saved], axis=0).astype(F32)
        up = jnp.concatenate([s[1, e] for s in saved], axis=0).astype(F32)
        sig = 1.0 / (1.0 + jnp.exp(-act))
        silu = act * sig
        copies[e][0].wait()
        grad = dot_tb(x, down_s[e])
        score = jnp.sum(silu * up * grad, axis=1, keepdims=True)
        grad_gate = (grad * up * sig * (1.0 + act * (1.0 - sig))).astype(BF16)
        grad_up = (grad * silu).astype(BF16)
        copies[e][1].wait()
        result = dot(grad_gate, gate_s[e])
        copies[e][2].wait()
        result = result + dot(grad_up, up_s[e])
        y_s[e * n : (e + 1) * n, :] = (result * factor[e * n : (e + 1) * n]).astype(BF16)
        expert = first + e
        high = score.astype(BF16).astype(F32)
        middle = (score - high).astype(BF16).astype(F32)
        low = score - high - middle
        spread = jnp.where(lane == expert, high, 0.0)
        spread = jnp.where(lane == expert + plan.experts, middle, spread)
        spread = jnp.where(lane == expert + 2 * plan.experts, low, spread)
        score_s[e * n : (e + 1) * n, :] = spread.astype(BF16)
    grads = dot_ta(table, y_s[...]).astype(BF16)
    scores = dot_ta(table, score_s[...]).astype(BF16)
    for i, out in enumerate(outs):
        out[:, : plan.width] = grads[i * plan.count : (i + 1) * plan.count, :]
        out[:, plan.width :] = scores[i * plan.count : (i + 1) * plan.count, :]


def expert_call(plan, kernel, name, width, vmem_inputs, weights, extra_scratch):
    any_spec = pl.BlockSpec(memory_space=pl.ANY)
    shape = (plan.mine, plan.hidden, plan.width)
    matrices = 3 * plan.mine
    return pl.pallas_call(
        functools.partial(kernel, plan),
        out_shape=[jax.ShapeDtypeStruct((plan.count, width), BF16)] * plan.blocks,
        in_specs=[vmem()] * len(vmem_inputs) + [any_spec] * 3,
        out_specs=[vmem()] * plan.blocks,
        scratch_shapes=[
            pltpu.VMEM(shape, BF16),
            pltpu.VMEM(shape, BF16),
            pltpu.VMEM(shape, BF16),
            pltpu.VMEM((plan.rows, plan.width), BF16),
            pltpu.VMEM((plan.rows, plan.width), BF16),
        ]
        + extra_scratch
        + [pltpu.SemaphoreType.DMA((plan.mine, 3))],
        compiler_params=pltpu.CompilerParams(vmem_limit_bytes=46 * MIB),
        cost_estimate=pl.CostEstimate(
            flops=2 * matrices * plan.expert_rows * plan.width * plan.hidden,
            bytes_accessed=2 * matrices * plan.width * plan.hidden,
            transcendentals=0,
        ),
        name=name,
    )(*vmem_inputs, *weights)


def gather(plan, block):
    own = [block] + [plan.over_expert(block, d) for d in range(1, plan.owners)]
    if plan.split == 1:
        return own
    return own + [plan.over_pair(b) for b in own]


def scatter(plan, parts):
    own = parts[: plan.owners]
    if plan.split > 1:
        other = [plan.over_pair(p) for p in parts[plan.owners :]]
        own = [
            (a.astype(F32) + b.astype(F32)).astype(BF16) if d else a
            for d, (a, b) in enumerate(zip(own, other))
        ]
    arrived = [own[0]]
    if plan.split > 1:
        arrived.append(other[0])
    return arrived + [plan.back_over_expert(own[d], d) for d in range(1, plan.owners)]


def sum_kernel(count, *refs):
    total = refs[0][...].astype(F32)
    for ref in refs[1:count]:
        total = total + ref[...].astype(F32)
    refs[count][...] = total.astype(BF16)


def sum_parts(plan, parts):
    return pl.pallas_call(
        functools.partial(sum_kernel, len(parts)),
        out_shape=jax.ShapeDtypeStruct((plan.count, plan.width), BF16),
        in_specs=[vmem()] * len(parts),
        out_specs=vmem(),
        name="sum_forward",
    )(*parts)


def sum_back_kernel(plan, count, *refs):
    routes, out, score = refs[count:]
    total = refs[0][...].astype(F32)
    for ref in refs[1:count]:
        total = total + ref[...].astype(F32)
    out[...] = total[:, : plan.width].astype(BF16)
    spread = total[:, plan.width :]
    lane = iota(spread.shape, 1)
    lane = jnp.where(lane < 3 * plan.experts, lane % plan.experts, -1)
    for k in range(plan.top):
        hit = lane == routes[:, k : k + 1]
        score[:, k : k + 1] = jnp.sum(jnp.where(hit, spread, 0.0), axis=1, keepdims=True)


def sum_back(plan, parts, routes):
    return pl.pallas_call(
        functools.partial(sum_back_kernel, plan, len(parts)),
        out_shape=(
            jax.ShapeDtypeStruct((plan.count, plan.width), BF16),
            jax.ShapeDtypeStruct((plan.count, plan.top), F32),
        ),
        in_specs=[vmem()] * (len(parts) + 1),
        out_specs=(vmem(), vmem()),
        name="sum_backward",
    )(*parts, routes)


def split_saved(plan, saved_gate, saved_up):
    both = jnp.stack([saved_gate[0], saved_up[0]])

    def part(core):
        piece = lax.dynamic_slice_in_dim(both, core * plan.mine, plan.mine, axis=2)
        piece = jnp.swapaxes(piece, 1, 2)
        short = plan.cap_rows - plan.cap
        return jnp.pad(piece, ((0, 0),) * 3 + ((0, short), (0, 0))).reshape(
            2, plan.mine, plan.source_rows, plan.hidden
        )

    if plan.split == 1:
        return [part(0)]
    core = lax.axis_index("dp") % 2
    return [part(core), plan.over_pair(part(1 - core))]


def body(
    tokens,
    routes,
    weights_fwd,
    cotangent,
    routes_back,
    weights_back,
    saved_gate,
    saved_up,
    w_gate,
    w_up,
    w_down,
):
    plan = Plan(tokens, routes, saved_gate, w_gate)
    weights = (jnp.swapaxes(w_gate, 1, 2), jnp.swapaxes(w_up, 1, 2), w_down)
    blocks = gather(plan, pack(plan, tokens, routes, weights_fwd))
    blocks_back = gather(plan, pack(plan, cotangent, routes_back, weights_back))
    saved = split_saved(plan, saved_gate, saved_up)
    parts = expert_call(plan, forward_kernel, "forward", plan.width, blocks, weights, [])
    mixed = sum_parts(plan, scatter(plan, parts))
    parts_back = expert_call(
        plan,
        backward_kernel,
        "backward",
        plan.width + plan.meta,
        [*blocks_back, *saved],
        weights,
        [pltpu.VMEM((plan.rows, plan.meta), BF16)],
    )
    input_grad, weight_grad = sum_back(plan, scatter(plan, parts_back), routes_back)
    return (mixed, input_grad, weight_grad)


def solution(mesh):
    spec = P(("dp", "expert"), None)
    saved = P("dp", None, "expert", None, None)
    weight = P("expert", None, None)
    return jax.shard_map(
        body,
        mesh=mesh,
        in_specs=(spec,) * 6 + (saved,) * 2 + (weight,) * 3,
        out_specs=(spec,) * 3,
        check_vma=False,
    )
```

```python
import functools
import jax
import jax.numpy as jnp
from jax import lax
from jax.experimental import pallas as pl
from jax.experimental.pallas import tpu as pltpu
from jax.sharding import PartitionSpec as P

F32 = jnp.float32
BF16 = jnp.bfloat16
LANES = 128
MIB = 1 << 20


def round_up(value, unit):
    return -(-value // unit) * unit


def dot(a, b):
    return jnp.dot(a, b, preferred_element_type=F32)


def dot_tb(a, b):
    return lax.dot_general(a, b, (((1,), (1,)), ((), ())), preferred_element_type=F32)


def dot_ta(a, b):
    return lax.dot_general(a, b, (((0,), (0,)), ((), ())), preferred_element_type=F32)


def iota(shape, dim):
    return lax.broadcasted_iota(jnp.int32, shape, dim)


def vmem():
    return pl.BlockSpec(memory_space=pltpu.VMEM)


class Plan:
    def __init__(self, tokens, routes, saved_gate, w_gate):
        self.owners = lax.axis_size("expert")
        self.groups = lax.axis_size("dp")
        self.count, self.width = tokens.shape
        self.top = routes.shape[1]
        self.local = w_gate.shape[0]
        self.hidden = w_gate.shape[2]
        self.experts = self.owners * self.local
        self.cap = saved_gate.shape[3]
        self.cap_rows = round_up(self.cap, 8)
        self.split = 2 if self.groups % 2 == 0 and self.local % 2 == 0 else 1
        self.mine = self.local // self.split
        self.meta = round_up(3 * self.experts, LANES)
        self.blocks = self.split * self.owners
        self.source_rows = self.owners * self.cap_rows
        self.expert_rows = self.split * self.source_rows
        self.rows = self.mine * self.expert_rows
        self.cols = self.blocks * self.count

    def peer(self, index, step):
        if self.owners & (self.owners - 1) == 0:
            return index ^ step
        return (index + step) % self.owners

    def over_expert(self, x, step):
        pairs = [(self.peer(i, step), i) for i in range(self.owners)]
        return lax.ppermute(x, "expert", pairs)

    def back_over_expert(self, x, step):
        pairs = [(i, self.peer(i, step)) for i in range(self.owners)]
        return lax.ppermute(x, "expert", pairs)

    def over_pair(self, x):
        return lax.ppermute(x, "dp", [(i, i ^ 1) for i in range(self.groups)])


def pack_kernel(plan, x_ref, routes_ref, factors_ref, out_ref):
    experts, top = plan.experts, plan.top
    count = plan.count
    out_ref[:, : plan.width] = x_ref[...]
    lane = iota((plan.meta, count), 0)
    chosen = jnp.zeros((plan.meta, count), F32)
    parts = jnp.zeros((plan.meta, count), F32)
    for k in range(top):
        route = routes_ref[k : k + 1, :]
        factor = factors_ref[k : k + 1, :]
        high = factor.astype(BF16).astype(F32)
        low = factor - high
        chosen = chosen + jnp.where(lane == route, 1.0, 0.0)
        parts = parts + jnp.where(lane == route + experts, high, 0.0)
        parts = parts + jnp.where(lane == route + 2 * experts, low, 0.0)
    earlier = jnp.where(iota((count, count), 0) < iota((count, count), 1), 1.0, 0.0)
    before = dot(chosen.astype(BF16), earlier.astype(BF16))
    facts = (chosen * (before + 1.0) + parts).astype(BF16)
    shape = (plan.meta, plan.meta)
    same = jnp.where(iota(shape, 0) == iota(shape, 1), 1.0, 0.0).astype(BF16)
    out_ref[:, plan.width :] = dot_ta(facts, same).astype(BF16)


def pack(plan, x, routes, factors):
    return pl.pallas_call(
        functools.partial(pack_kernel, plan),
        out_shape=jax.ShapeDtypeStruct((plan.count, plan.width + plan.meta), BF16),
        in_specs=[vmem()] * 3,
        out_specs=vmem(),
        compiler_params=pltpu.CompilerParams(vmem_limit_bytes=4 * MIB),
        name="pack",
    )(x, routes.T, factors.T)


def first_expert(plan):
    core = lax.rem(lax.axis_index("dp"), plan.split)
    return lax.axis_index("expert") * plan.local + core * plan.mine, core * plan.mine


def whole_block(plan, index):
    core = lax.rem(lax.axis_index("dp"), plan.split)
    group, step = index // plan.owners, index % plan.owners
    return (group ^ core) * plan.owners + plan.peer(lax.axis_index("expert"), step)


def tables(plan, meta, first, whole):
    me = lax.axis_index("expert")
    core = lax.rem(lax.axis_index("dp"), plan.split)
    row = iota((plan.rows, plan.meta), 0)
    lane = iota((plan.rows, plan.meta), 1)
    expert = first + row // plan.expert_rows
    pick_slot = jnp.where(lane == expert, 1.0, 0.0).astype(BF16)
    pick_part = jnp.where(
        (lane == expert + plan.experts) | (lane == expert + 2 * plan.experts), 1.0, 0.0
    ).astype(BF16)
    slot = dot_tb(pick_slot, meta)
    part = dot_tb(pick_part, meta)
    shape = (plan.rows, plan.cols)
    row = iota(shape, 0)
    col = iota(shape, 1)
    block = col // plan.count
    source = block % plan.owners
    group = block // plan.owners
    if whole:
        group = group ^ core
    else:
        source = plan.peer(me, source)
    place = row % plan.expert_rows
    want = (row % plan.cap_rows + 1).astype(F32)
    same = (place // plan.cap_rows) == group * plan.owners + source
    hit = same & (slot == want)
    factor = jnp.sum(jnp.where(hit, part, 0.0), axis=1, keepdims=True)
    return jnp.where(hit, 1.0, 0.0).astype(BF16), factor


def weight_copies(plan, offset, arrays, slots, sems):
    copies = []
    for e in range(plan.mine):
        copies.append(
            [
                pltpu.make_async_copy(array.at[offset + e], slot.at[e], sems.at[e, i])
                for i, (array, slot) in enumerate(zip(arrays, slots))
            ]
        )
    for group in copies:
        for copy in group:
            copy.start()
    return copies


def forward_kernel(plan, *refs):
    blocks = refs[: plan.blocks]
    w_gate, w_up, w_down = refs[plan.blocks : plan.blocks + 3]
    out_ref, gate_s, up_s, down_s, x_s, y_s, sems = refs[plan.blocks + 3 :]
    first, offset = first_expert(plan)
    copies = weight_copies(
        plan, offset, (w_gate, w_up, w_down), (gate_s, up_s, down_s), sems
    )
    meta = jnp.concatenate([b[:, plan.width :] for b in blocks], axis=0)
    rows = jnp.concatenate([b[:, : plan.width] for b in blocks], axis=0)
    table, factor = tables(plan, meta, first, False)
    x_s[...] = dot(table, rows).astype(BF16)
    n = plan.expert_rows
    for e in range(plan.mine):
        x = x_s[e * n : (e + 1) * n, :]
        copies[e][0].wait()
        gate = dot_tb(gate_s[e], x)
        copies[e][1].wait()
        up = dot_tb(up_s[e], x)
        hidden = (gate / (1.0 + jnp.exp(-gate)) * up).astype(BF16)
        copies[e][2].wait()
        out = dot_ta(hidden, down_s[e])
        y_s[e * n : (e + 1) * n, :] = (out * factor[e * n : (e + 1) * n]).astype(BF16)
    mixed = dot_ta(table, y_s[...]).astype(BF16)
    for i in range(plan.blocks):
        start = pl.multiple_of(whole_block(plan, i) * plan.count, plan.count)
        out_ref[pl.ds(start, plan.count), :] = mixed[i * plan.count : (i + 1) * plan.count, :]


def backward_kernel(plan, *refs):
    block_ref, refs = refs[0], refs[1:]
    saved = refs[: plan.split]
    w_gate, w_up, w_down = refs[plan.split : plan.split + 3]
    refs = refs[plan.split + 3 :]
    outs = refs[: plan.blocks]
    gate_s, up_s, down_s, x_s, y_s, score_s, grad_s, sems = refs[plan.blocks :]
    first, offset = first_expert(plan)
    copies = weight_copies(
        plan, offset, (w_down, w_gate, w_up), (down_s, gate_s, up_s), sems
    )
    table, factor = tables(plan, block_ref[:, plan.width :], first, True)
    x_s[...] = dot(table, block_ref[:, : plan.width]).astype(BF16)
    n = plan.expert_rows
    lane = iota((n, plan.meta), 1)
    for e in range(plan.mine):
        x = x_s[e * n : (e + 1) * n, :]
        act = jnp.concatenate([s[0, e] for s in saved], axis=0).astype(F32)
        up = jnp.concatenate([s[1, e] for s in saved], axis=0).astype(F32)
        sig = 1.0 / (1.0 + jnp.exp(-act))
        silu = act * sig
        copies[e][0].wait()
        grad = dot_tb(x, down_s[e])
        score = jnp.sum(silu * up * grad, axis=1, keepdims=True)
        grad_gate = (grad * up * sig * (1.0 + act * (1.0 - sig))).astype(BF16)
        grad_up = (grad * silu).astype(BF16)
        copies[e][1].wait()
        result = dot(grad_gate, gate_s[e])
        copies[e][2].wait()
        result = result + dot(grad_up, up_s[e])
        y_s[e * n : (e + 1) * n, :] = (result * factor[e * n : (e + 1) * n]).astype(BF16)
        expert = first + e
        high = score.astype(BF16).astype(F32)
        middle = (score - high).astype(BF16).astype(F32)
        low = score - high - middle
        spread = jnp.where(lane == expert, high, 0.0)
        spread = jnp.where(lane == expert + plan.experts, middle, spread)
        spread = jnp.where(lane == expert + 2 * plan.experts, low, spread)
        score_s[e * n : (e + 1) * n, :] = spread.astype(BF16)
    grad_s[:, : plan.width] = dot_ta(table, y_s[...]).astype(BF16)
    grad_s[:, plan.width :] = dot_ta(table, score_s[...]).astype(BF16)
    for i, out in enumerate(outs):
        start = pl.multiple_of(whole_block(plan, i) * plan.count, plan.count)
        out[...] = grad_s[pl.ds(start, plan.count), :]


def expert_call(plan, kernel, name, out_shape, vmem_inputs, weights, extra_scratch):
    any_spec = pl.BlockSpec(memory_space=pl.ANY)
    shape = (plan.mine, plan.hidden, plan.width)
    matrices = 3 * plan.mine
    return pl.pallas_call(
        functools.partial(kernel, plan),
        out_shape=out_shape,
        in_specs=[vmem()] * len(vmem_inputs) + [any_spec] * 3,
        out_specs=[vmem()] * len(out_shape),
        scratch_shapes=[
            pltpu.VMEM(shape, BF16),
            pltpu.VMEM(shape, BF16),
            pltpu.VMEM(shape, BF16),
            pltpu.VMEM((plan.rows, plan.width), BF16),
            pltpu.VMEM((plan.rows, plan.width), BF16),
        ]
        + extra_scratch
        + [pltpu.SemaphoreType.DMA((plan.mine, 3))],
        compiler_params=pltpu.CompilerParams(vmem_limit_bytes=46 * MIB),
        cost_estimate=pl.CostEstimate(
            flops=2 * matrices * plan.expert_rows * plan.width * plan.hidden,
            bytes_accessed=2 * matrices * plan.width * plan.hidden,
            transcendentals=0,
        ),
        name=name,
    )(*vmem_inputs, *weights)


def pair_groups(plan):
    size = plan.blocks
    return [
        list(range(start, start + size))
        for start in range(0, plan.groups * plan.owners, size)
    ]


def gather(plan, block):
    own = [block] + [plan.over_expert(block, d) for d in range(1, plan.owners)]
    if plan.split == 1:
        return own
    return own + [plan.over_pair(b) for b in own]


def gather_whole(plan, block):
    axes = ("dp", "expert")
    return lax.all_gather(block, axes, axis_index_groups=pair_groups(plan), tiled=True)


def scatter_whole(plan, parts):
    axes = ("dp", "expert")
    groups = pair_groups(plan)
    return lax.psum_scatter(parts, axes, axis_index_groups=groups, tiled=True)


def scatter(plan, parts):
    own = parts[: plan.owners]
    arrived = [own[0]]
    if plan.split > 1:
        other = [plan.over_pair(p) for p in parts[plan.owners :]]
        arrived.append(other[0])
        own = [(a.astype(F32) + b.astype(F32)).astype(BF16) for a, b in zip(own, other)]
    return arrived + [plan.back_over_expert(own[d], d) for d in range(1, plan.owners)]


def finish_back(plan, parts, routes):
    total = sum(p.astype(F32) for p in parts)
    spread = total[:, plan.width : plan.width + 3 * plan.experts]
    spread = jnp.sum(spread.reshape(plan.count, 3, plan.experts), axis=1)
    lane = iota((plan.top, plan.count, plan.experts), 2)
    hit = lane == routes.T[:, :, None]
    score = jnp.sum(jnp.where(hit, spread[None], 0.0), axis=2).T
    return total[:, : plan.width].astype(BF16), score


def split_saved(plan, saved_gate, saved_up):
    def piece(array, core):
        rows = lax.dynamic_slice_in_dim(array[0], core * plan.mine, plan.mine, axis=1)
        short = plan.cap_rows - plan.cap
        rows = jnp.pad(jnp.swapaxes(rows, 0, 1), ((0, 0), (0, 0), (0, short), (0, 0)))
        return rows.reshape(1, plan.mine, plan.source_rows, plan.hidden)

    def part(core):
        return jnp.concatenate([piece(saved_gate, core), piece(saved_up, core)])

    if plan.split == 1:
        return [part(0)]
    core = lax.axis_index("dp") % 2
    return [part(core), plan.over_pair(part(1 - core))]


def body(
    tokens,
    routes,
    weights_fwd,
    cotangent,
    routes_back,
    weights_back,
    saved_gate,
    saved_up,
    w_gate,
    w_up,
    w_down,
):
    plan = Plan(tokens, routes, saved_gate, w_gate)
    weights = (jnp.swapaxes(w_gate, 1, 2), jnp.swapaxes(w_up, 1, 2), w_down)
    packed = pack(plan, tokens, routes, weights_fwd)
    packed, cotangent = lax.optimization_barrier((packed, cotangent))
    packed_back = pack(plan, cotangent, routes_back, weights_back)
    blocks = gather(plan, packed)
    whole_back = gather_whole(plan, packed_back)
    saved = split_saved(plan, saved_gate, saved_up)
    whole_shape = jax.ShapeDtypeStruct((plan.cols, plan.width), BF16)
    (partial,) = expert_call(
        plan, forward_kernel, "forward", [whole_shape], blocks, weights, []
    )
    partial, saved = lax.optimization_barrier((partial, saved))
    mixed = scatter_whole(plan, partial)
    block_shape = jax.ShapeDtypeStruct((plan.count, plan.width + plan.meta), BF16)
    parts_back = expert_call(
        plan,
        backward_kernel,
        "backward",
        [block_shape] * plan.blocks,
        [whole_back, *saved],
        weights,
        [
            pltpu.VMEM((plan.rows, plan.meta), BF16),
            pltpu.VMEM((plan.cols, plan.width + plan.meta), BF16),
        ],
    )
    parts_back, mixed = lax.optimization_barrier((parts_back, mixed))
    input_grad, weight_grad = finish_back(plan, scatter(plan, parts_back), routes_back)
    return (mixed, input_grad, weight_grad)


def solution(mesh):
    spec = P(("dp", "expert"), None)
    saved = P("dp", None, "expert", None, None)
    weight = P("expert", None, None)
    return jax.shard_map(
        body,
        mesh=mesh,
        in_specs=(spec,) * 6 + (saved,) * 2 + (weight,) * 3,
        out_specs=(spec,) * 3,
        check_vma=False,
    )
```

```python
import functools
import jax
import jax.numpy as jnp
from jax import lax
from jax.experimental import pallas as pl
from jax.experimental.pallas import tpu as pltpu
from jax.sharding import PartitionSpec as P

F32 = jnp.float32
BF16 = jnp.bfloat16
LANES = 128
MIB = 1 << 20


def round_up(value, unit):
    return -(-value // unit) * unit


def dot(a, b):
    return jnp.dot(a, b, preferred_element_type=F32)


def dot_tb(a, b):
    return lax.dot_general(a, b, (((1,), (1,)), ((), ())), preferred_element_type=F32)


def dot_ta(a, b):
    return lax.dot_general(a, b, (((0,), (0,)), ((), ())), preferred_element_type=F32)


def iota(shape, dim):
    return lax.broadcasted_iota(jnp.int32, shape, dim)


def vmem():
    return pl.BlockSpec(memory_space=pltpu.VMEM)


def hbm():
    return pl.BlockSpec(memory_space=pltpu.HBM)


def in_vmem(x):
    return pltpu.with_memory_space_constraint(x, pltpu.VMEM)


def in_hbm(x):
    return pltpu.with_memory_space_constraint(x, pltpu.HBM)


class Plan:
    def __init__(self, tokens, routes, saved_gate, w_gate):
        self.owners = lax.axis_size("expert")
        self.groups = lax.axis_size("dp")
        self.count, self.width = tokens.shape
        self.top = routes.shape[1]
        self.local = w_gate.shape[0]
        self.hidden = w_gate.shape[2]
        self.experts = self.owners * self.local
        self.cap = saved_gate.shape[3]
        self.cap_rows = round_up(self.cap, 8)
        self.split = 2 if self.groups % 2 == 0 and self.local % 2 == 0 else 1
        self.mine = self.local // self.split
        self.meta = round_up(3 * self.experts, LANES)
        self.blocks = self.split * self.owners
        self.source_rows = self.owners * self.cap_rows
        self.expert_rows = self.split * self.source_rows
        self.rows = self.mine * self.expert_rows
        self.cols = self.blocks * self.count

    def peer(self, index, step):
        if self.owners & (self.owners - 1) == 0:
            return index ^ step
        return (index + step) % self.owners

    def over_expert(self, x, step):
        pairs = [(self.peer(i, step), i) for i in range(self.owners)]
        return lax.ppermute(x, "expert", pairs)

    def back_over_expert(self, x, step):
        pairs = [(i, self.peer(i, step)) for i in range(self.owners)]
        return lax.ppermute(x, "expert", pairs)

    def over_pair(self, x):
        return lax.ppermute(x, "dp", [(i, i ^ 1) for i in range(self.groups)])


def pack_kernel(plan, x_hbm, routes_hbm, factors_hbm, out_ref, routes_ref, factors_ref, sems):
    experts, top = plan.experts, plan.top
    count = plan.count
    x_copy = pltpu.make_async_copy(x_hbm, out_ref.at[:, : plan.width], sems.at[0])
    small = [
        pltpu.make_async_copy(routes_hbm, routes_ref, sems.at[1]),
        pltpu.make_async_copy(factors_hbm, factors_ref, sems.at[2]),
    ]
    for copy in (*small, x_copy):
        copy.start()
    for copy in small:
        copy.wait()
    lane = iota((plan.meta, count), 0)
    chosen = jnp.zeros((plan.meta, count), F32)
    parts = jnp.zeros((plan.meta, count), F32)
    for k in range(top):
        route = routes_ref[k : k + 1, :]
        factor = factors_ref[k : k + 1, :]
        high = factor.astype(BF16).astype(F32)
        low = factor - high
        chosen = chosen + jnp.where(lane == route, 1.0, 0.0)
        parts = parts + jnp.where(lane == route + experts, high, 0.0)
        parts = parts + jnp.where(lane == route + 2 * experts, low, 0.0)
    earlier = jnp.where(iota((count, count), 0) < iota((count, count), 1), 1.0, 0.0)
    before = dot(chosen.astype(BF16), earlier.astype(BF16))
    facts = (chosen * (before + 1.0) + parts).astype(BF16)
    shape = (plan.meta, plan.meta)
    same = jnp.where(iota(shape, 0) == iota(shape, 1), 1.0, 0.0).astype(BF16)
    out_ref[:, plan.width :] = dot_ta(facts, same).astype(BF16)
    x_copy.wait()


def pack(plan, x, routes, factors):
    return pl.pallas_call(
        functools.partial(pack_kernel, plan),
        out_shape=jax.ShapeDtypeStruct((plan.count, plan.width + plan.meta), BF16),
        in_specs=[hbm()] * 3,
        out_specs=vmem(),
        scratch_shapes=[
            pltpu.VMEM((plan.top, plan.count), jnp.int32),
            pltpu.VMEM((plan.top, plan.count), F32),
            pltpu.SemaphoreType.DMA((3,)),
        ],
        compiler_params=pltpu.CompilerParams(vmem_limit_bytes=4 * MIB),
        name="pack",
    )(in_hbm(x), in_hbm(routes.T), in_hbm(factors.T))


def first_expert(plan):
    core = lax.rem(lax.axis_index("dp"), plan.split)
    return lax.axis_index("expert") * plan.local + core * plan.mine, core * plan.mine


def tables(plan, meta, first):
    me = lax.axis_index("expert")
    row = iota((plan.rows, plan.meta), 0)
    lane = iota((plan.rows, plan.meta), 1)
    expert = first + row // plan.expert_rows
    pick_slot = jnp.where(lane == expert, 1.0, 0.0).astype(BF16)
    pick_part = jnp.where(
        (lane == expert + plan.experts) | (lane == expert + 2 * plan.experts), 1.0, 0.0
    ).astype(BF16)
    slot = dot_tb(pick_slot, meta)
    part = dot_tb(pick_part, meta)
    shape = (plan.rows, plan.cols)
    row = iota(shape, 0)
    col = iota(shape, 1)
    block = col // plan.count
    source = plan.peer(me, block % plan.owners)
    group = block // plan.owners
    place = row % plan.expert_rows
    want = (row % plan.cap_rows + 1).astype(F32)
    same = (place // plan.cap_rows) == group * plan.owners + source
    hit = same & (slot == want)
    factor = jnp.sum(jnp.where(hit, part, 0.0), axis=1, keepdims=True)
    return jnp.where(hit, 1.0, 0.0).astype(BF16), factor


def fetch_kernel(plan, gate_hbm, up_hbm, after, gate_ref, up_ref, done_ref, sems):
    done_ref[...] = jnp.zeros_like(done_ref)
    offset = first_expert(plan)[1]
    copies = []
    for i, (array, ref) in enumerate(((gate_hbm, gate_ref), (up_hbm, up_ref))):
        for e in range(plan.mine):
            copies.append(
                pltpu.make_async_copy(array.at[offset + e], ref.at[e], sems.at[i, e])
            )
    for copy in copies:
        copy.start()
    for copy in copies:
        copy.wait()


def fetch(plan, w_gate, w_up, after):
    shape = pltpu.VMEM((plan.mine, plan.hidden, plan.width), BF16)
    return pl.pallas_call(
        functools.partial(fetch_kernel, plan),
        out_shape=(shape, shape, jax.ShapeDtypeStruct((8, LANES), F32)),
        in_specs=[hbm(), hbm(), pl.BlockSpec(memory_space=pl.ANY)],
        out_specs=(vmem(), vmem(), vmem()),
        scratch_shapes=[pltpu.SemaphoreType.DMA((2, plan.mine))],
        compiler_params=pltpu.CompilerParams(vmem_limit_bytes=MIB),
        cost_estimate=pl.CostEstimate(
            flops=0,
            bytes_accessed=4 * plan.mine * plan.hidden * plan.width * 2,
            transcendentals=0,
        ),
        name="fetch",
    )(in_hbm(w_gate), in_hbm(w_up), after)


def forward_kernel(plan, count, *refs):
    blocks, refs = refs[:count], refs[count:]
    gate_ref, up_ref, down_hbm, *refs = refs
    outs, (kept_ref, rest_ref, x_s, y_s, sems) = refs[:-5], refs[-5:]
    first, offset = first_expert(plan)
    downs = [kept_ref.at[0]] + [rest_ref.at[e - 1] for e in range(1, plan.mine)]
    copies = [
        pltpu.make_async_copy(down_hbm.at[offset + e], down, sems.at[e])
        for e, down in enumerate(downs)
    ]
    for copy in copies:
        copy.start()
    meta = jnp.concatenate([b[:, plan.width :] for b in blocks], axis=0)
    rows = jnp.concatenate([b[:, : plan.width] for b in blocks], axis=0)
    table, factor = tables(plan, meta, first)
    x_s[...] = dot(table, rows).astype(BF16)
    n = plan.expert_rows
    hiddens = []
    for e in range(plan.mine):
        x = x_s[e * n : (e + 1) * n, :]
        gate = dot_tb(x, gate_ref[e])
        up = dot_tb(x, up_ref[e])
        hiddens.append((gate / (1.0 + jnp.exp(-gate)) * up).astype(BF16))
    for e in range(plan.mine):
        copies[e].wait()
        out = dot(hiddens[e], downs[e][...])
        y_s[e * n : (e + 1) * n, :] = (out * factor[e * n : (e + 1) * n]).astype(BF16)
    put_rows(plan, outs, slice(None), dot_ta(table, y_s[...]).astype(BF16))


def put_rows(plan, outs, columns, rows):
    start = 0
    for out in outs:
        stop = start + out.shape[0]
        out[:, columns] = rows[start:stop, :]
        start = stop


def backward_kernel(plan, count, *refs):
    blocks, refs = refs[:count], refs[count:]
    saved, refs = refs[: plan.split], refs[plan.split :]
    gate_ref, up_ref, kept_ref, down_hbm, *refs = refs
    outs, (rest_ref, x_s, y_s, score_s, sems) = refs[:-5], refs[-5:]
    first, offset = first_expert(plan)
    downs = [kept_ref.at[0]] + [rest_ref.at[e - 1] for e in range(1, plan.mine)]
    copies = [
        pltpu.make_async_copy(down_hbm.at[offset + e], downs[e], sems.at[e])
        for e in range(1, plan.mine)
    ]
    for copy in copies:
        copy.start()
    meta = jnp.concatenate([b[:, plan.width :] for b in blocks], axis=0)
    rows = jnp.concatenate([b[:, : plan.width] for b in blocks], axis=0)
    table, factor = tables(plan, meta, first)
    x_s[...] = dot(table, rows).astype(BF16)
    n = plan.expert_rows
    lane = iota((n, plan.meta), 1)
    for e in range(plan.mine):
        x = x_s[e * n : (e + 1) * n, :]
        act = jnp.concatenate([s[0, e] for s in saved], axis=0).astype(F32)
        up = jnp.concatenate([s[1, e] for s in saved], axis=0).astype(F32)
        sig = 1.0 / (1.0 + jnp.exp(-act))
        silu = act * sig
        if e > 0:
            copies[e - 1].wait()
        grad = dot_tb(x, downs[e][...])
        score = jnp.sum(silu * up * grad, axis=1, keepdims=True)
        grad_gate = (grad * up * sig * (1.0 + act * (1.0 - sig))).astype(BF16)
        grad_up = (grad * silu).astype(BF16)
        result = dot(grad_gate, gate_ref[e]) + dot(grad_up, up_ref[e])
        y_s[e * n : (e + 1) * n, :] = (result * factor[e * n : (e + 1) * n]).astype(BF16)
        expert = first + e
        high = score.astype(BF16).astype(F32)
        middle = (score - high).astype(BF16).astype(F32)
        low = score - high - middle
        spread = jnp.where(lane == expert, high, 0.0)
        spread = jnp.where(lane == expert + plan.experts, middle, spread)
        spread = jnp.where(lane == expert + 2 * plan.experts, low, spread)
        score_s[e * n : (e + 1) * n, :] = spread.astype(BF16)
    put_rows(plan, outs, slice(0, plan.width), dot_ta(table, y_s[...]).astype(BF16))
    scores = dot_ta(table, score_s[...]).astype(BF16)
    put_rows(plan, outs, slice(plan.width, plan.width + plan.meta), scores)


def part_shapes(plan, width):
    block = jax.ShapeDtypeStruct((plan.count, width), BF16)
    other = jax.ShapeDtypeStruct((plan.owners * plan.count, width), BF16)
    return [block] * plan.owners + [other] * (plan.split - 1)


def expert_params(plan, matrices):
    held = 2 * plan.mine * plan.width * plan.hidden * 2
    return dict(
        compiler_params=pltpu.CompilerParams(vmem_limit_bytes=40 * MIB - held),
        cost_estimate=pl.CostEstimate(
            flops=2 * 3 * plan.mine * plan.expert_rows * plan.width * plan.hidden,
            bytes_accessed=2 * matrices * plan.mine * plan.width * plan.hidden,
            transcendentals=0,
        ),
    )


def forward(plan, blocks, gate, up, w_down):
    kept = pltpu.VMEM((1, plan.hidden, plan.width), BF16)
    shapes = part_shapes(plan, plan.width) + [kept]
    *parts, kept = pl.pallas_call(
        functools.partial(forward_kernel, plan, len(blocks)),
        out_shape=shapes,
        in_specs=[vmem()] * (len(blocks) + 2) + [hbm()],
        out_specs=[vmem()] * len(shapes),
        scratch_shapes=[
            rest_shape(plan),
            pltpu.VMEM((plan.rows, plan.width), BF16),
            pltpu.VMEM((plan.rows, plan.width), BF16),
            pltpu.SemaphoreType.DMA((plan.mine,)),
        ],
        name="forward",
        **expert_params(plan, 1),
    )(*blocks, in_vmem(gate), in_vmem(up), in_hbm(w_down))
    return parts, kept


def rest_shape(plan):
    return pltpu.VMEM((max(plan.mine - 1, 1), plan.hidden, plan.width), BF16)


def backward(plan, blocks, saved, weights, w_down):
    shapes = part_shapes(plan, plan.width + plan.meta)
    return pl.pallas_call(
        functools.partial(backward_kernel, plan, len(blocks)),
        out_shape=shapes,
        in_specs=[vmem()] * (len(blocks) + len(saved) + 3) + [hbm()],
        out_specs=[vmem()] * len(shapes),
        scratch_shapes=[
            rest_shape(plan),
            pltpu.VMEM((plan.rows, plan.width), BF16),
            pltpu.VMEM((plan.rows, plan.width), BF16),
            pltpu.VMEM((plan.rows, plan.meta), BF16),
            pltpu.SemaphoreType.DMA((plan.mine,)),
        ],
        name="backward",
        **expert_params(plan, 1),
    )(*blocks, *saved, *[in_vmem(w) for w in weights], in_hbm(w_down))


def gather_group(plan, block):
    return [block] + [plan.over_expert(block, d) for d in range(1, plan.owners)]


def sum_pair(plan, parts):
    own = [[p] for p in parts[: plan.owners]]
    if plan.split > 1:
        other = plan.over_pair(parts[plan.owners])
        for d in range(plan.owners):
            own[d].append(other[d * plan.count : (d + 1) * plan.count])
    return own


def total(terms):
    return sum(t.astype(F32) for t in terms)


def scatter_group(plan, own):
    sent = [total(own[d]).astype(BF16) for d in range(1, plan.owners)]
    return own[0] + [plan.back_over_expert(x, d) for d, x in enumerate(sent, 1)]


def finish_back(plan, parts, routes):
    whole = total(parts)
    spread = whole[:, plan.width : plan.width + 3 * plan.experts]
    spread = jnp.sum(spread.reshape(plan.count, 3, plan.experts), axis=1)
    lane = iota((plan.top, plan.count, plan.experts), 2)
    hit = lane == routes.T[:, :, None]
    score = jnp.sum(jnp.where(hit, spread[None], 0.0), axis=2).T
    return whole[:, : plan.width].astype(BF16), score


def split_saved(plan, saved_gate, saved_up):
    def piece(array, core):
        rows = lax.dynamic_slice_in_dim(array[0], core * plan.mine, plan.mine, axis=1)
        short = plan.cap_rows - plan.cap
        rows = jnp.pad(jnp.swapaxes(rows, 0, 1), ((0, 0), (0, 0), (0, short), (0, 0)))
        return rows.reshape(1, plan.mine, plan.source_rows, plan.hidden)

    def part(core):
        return jnp.concatenate([piece(saved_gate, core), piece(saved_up, core)])

    if plan.split == 1:
        return [part(0)]
    core = lax.axis_index("dp") % 2
    return [part(core), plan.over_pair(part(1 - core))]


def body(
    tokens,
    routes,
    weights_fwd,
    cotangent,
    routes_back,
    weights_back,
    saved_gate,
    saved_up,
    w_gate,
    w_up,
    w_down,
):
    plan = Plan(tokens, routes, saved_gate, w_gate)
    packed = pack(plan, tokens, routes, weights_fwd)
    packed, cotangent = lax.optimization_barrier((packed, cotangent))
    packed_back = pack(plan, cotangent, routes_back, weights_back)
    gate, up, done = fetch(
        plan, jnp.swapaxes(w_gate, 1, 2), jnp.swapaxes(w_up, 1, 2), packed_back
    )
    blocks = gather_group(plan, packed)
    saved = split_saved(plan, saved_gate, saved_up)
    blocks_back = gather_group(plan, packed_back)
    if plan.split > 1:
        zero = done[0, 0].astype(BF16)
        blocks = blocks + [plan.over_pair(b + zero) for b in blocks]
    parts, kept = forward(plan, blocks, gate, up, w_down)
    parts, blocks_back, saved = lax.optimization_barrier((parts, blocks_back, saved))
    if plan.split > 1:
        blocks_back = blocks_back + [plan.over_pair(jnp.concatenate(blocks_back))]
    terms = scatter_group(plan, sum_pair(plan, parts))
    parts_back = backward(plan, blocks_back, saved, (gate, up, kept), w_down)
    parts_back, terms = lax.optimization_barrier((parts_back, terms))
    mixed = total(terms).astype(BF16)
    terms_back = scatter_group(plan, sum_pair(plan, parts_back))
    input_grad, weight_grad = finish_back(plan, terms_back, routes_back)
    return (mixed, input_grad, weight_grad)


def solution(mesh):
    spec = P(("dp", "expert"), None)
    saved = P("dp", None, "expert", None, None)
    weight = P("expert", None, None)
    return jax.shard_map(
        body,
        mesh=mesh,
        in_specs=(spec,) * 6 + (saved,) * 2 + (weight,) * 3,
        out_specs=(spec,) * 3,
        check_vma=False,
    )
```

```python
import functools
import jax
import jax.numpy as jnp
from jax import lax
from jax.experimental import pallas as pl
from jax.experimental.pallas import tpu as pltpu
from jax.sharding import PartitionSpec as P

F32 = jnp.float32
BF16 = jnp.bfloat16
LANES = 128
MIB = 1 << 20


def round_up(value, unit):
    return -(-value // unit) * unit


def dot(a, b):
    return jnp.dot(a, b, preferred_element_type=F32)


def dot_tb(a, b):
    return lax.dot_general(a, b, (((1,), (1,)), ((), ())), preferred_element_type=F32)


def dot_ta(a, b):
    return lax.dot_general(a, b, (((0,), (0,)), ((), ())), preferred_element_type=F32)


def iota(shape, dim):
    return lax.broadcasted_iota(jnp.int32, shape, dim)


def vmem():
    return pl.BlockSpec(memory_space=pltpu.VMEM)


def hbm():
    return pl.BlockSpec(memory_space=pltpu.HBM)


def in_vmem(x):
    return pltpu.with_memory_space_constraint(x, pltpu.VMEM)


def in_hbm(x):
    return pltpu.with_memory_space_constraint(x, pltpu.HBM)


class Plan:
    def __init__(self, tokens, routes, saved_gate, w_gate):
        self.owners = lax.axis_size("expert")
        self.groups = lax.axis_size("dp")
        self.count, self.width = tokens.shape
        self.top = routes.shape[1]
        self.local = w_gate.shape[0]
        self.hidden = w_gate.shape[2]
        self.experts = self.owners * self.local
        self.cap = saved_gate.shape[3]
        self.cap_rows = round_up(self.cap, 8)
        self.split = 2 if self.groups % 2 == 0 and self.local % 2 == 0 else 1
        self.mine = self.local // self.split
        self.meta = round_up(3 * self.experts, LANES)
        self.blocks = self.split * self.owners
        self.source_rows = self.owners * self.cap_rows
        self.expert_rows = self.split * self.source_rows
        self.paired = self.owners & (self.owners - 1) == 0
        self.sent = self.width + self.meta
        self.rows = self.mine * self.expert_rows
        self.cols = self.blocks * self.count

    def peer(self, index, step, core):
        bits = self.owners.bit_length() - 1
        if self.owners != 1 << bits:
            return (index + step) % self.owners
        turned = sum(((step >> i) & 1) << (bits - 1 - i) for i in range(bits))
        return index ^ (step + (turned - step) * core)

    def over_expert(self, x, step, back=False):
        pairs = []
        for group in range(self.groups):
            for i in range(self.owners):
                near = group * self.owners + i
                far = self.peer(i, step, group % self.split) + group * self.owners
                pairs.append((near, far) if back else (far, near))
        return lax.ppermute(x, ("dp", "expert"), pairs)

    def over_pair(self, x):
        return lax.ppermute(x, "dp", [(i, i ^ 1) for i in range(self.groups)])


def pack_body(plan, x_hbm, routes_hbm, factors_hbm, out_ref, routes_ref, factors_ref, sems):
    experts, count = plan.experts, plan.count
    x_copy = pltpu.make_async_copy(x_hbm, out_ref.at[:, : plan.width], sems.at[0])
    small = [
        pltpu.make_async_copy(routes_hbm, routes_ref, sems.at[1]),
        pltpu.make_async_copy(factors_hbm, factors_ref, sems.at[2]),
    ]
    for copy in (*small, x_copy):
        copy.start()
    for copy in small:
        copy.wait()
    lane = iota((plan.meta, count), 0)
    chosen = jnp.zeros((plan.meta, count), F32)
    parts = jnp.zeros((plan.meta, count), F32)
    for k in range(plan.top):
        route = routes_ref[k : k + 1, :]
        factor = factors_ref[k : k + 1, :]
        high = factor.astype(BF16).astype(F32)
        low = factor - high
        chosen = chosen + jnp.where(lane == route, 1.0, 0.0)
        parts = parts + jnp.where(lane == route + experts, high, 0.0)
        parts = parts + jnp.where(lane == route + 2 * experts, low, 0.0)
    earlier = jnp.where(iota((count, count), 0) < iota((count, count), 1), 1.0, 0.0)
    before = dot(chosen.astype(BF16), earlier.astype(BF16))
    facts = (chosen * (before + 1.0) + parts).astype(BF16)
    shape = (plan.meta, plan.meta)
    same = jnp.where(iota(shape, 0) == iota(shape, 1), 1.0, 0.0).astype(BF16)
    out_ref[:, plan.width :] = dot_ta(facts, same).astype(BF16)
    x_copy.wait()


def pack_scratch(plan):
    return [
        pltpu.VMEM((plan.top, plan.count), jnp.int32),
        pltpu.VMEM((plan.top, plan.count), F32),
        pltpu.SemaphoreType.DMA((3,)),
    ]


def pack(plan, x, routes, factors):
    return pl.pallas_call(
        functools.partial(pack_body, plan),
        out_shape=jax.ShapeDtypeStruct((plan.count, plan.width + plan.meta), BF16),
        in_specs=[hbm()] * 3,
        out_specs=vmem(),
        scratch_shapes=pack_scratch(plan),
        compiler_params=pltpu.CompilerParams(vmem_limit_bytes=4 * MIB),
        name="pack",
    )(in_hbm(x), in_hbm(routes.T), in_hbm(factors.T))


def first_expert(plan):
    core = lax.rem(lax.axis_index("dp"), plan.split)
    return lax.axis_index("expert") * plan.local + core * plan.mine, core * plan.mine


def tables(plan, meta, first):
    me = lax.axis_index("expert")
    core = lax.rem(lax.axis_index("dp"), plan.split)
    row = iota((plan.rows, plan.meta), 0)
    lane = iota((plan.rows, plan.meta), 1)
    expert = first + row // plan.expert_rows
    pick_slot = jnp.where(lane == expert, 1.0, 0.0).astype(BF16)
    pick_part = jnp.where(
        (lane == expert + plan.experts) | (lane == expert + 2 * plan.experts), 1.0, 0.0
    ).astype(BF16)
    slot = dot_tb(pick_slot, meta)
    part = dot_tb(pick_part, meta)
    shape = (plan.rows, plan.cols)
    row = iota(shape, 0)
    col = iota(shape, 1)
    block = col // plan.count
    group = block // plan.owners
    source = plan.peer(me, block % plan.owners, core ^ group)
    place = row % plan.expert_rows
    want = (row % plan.cap_rows + 1).astype(F32)
    same = (place // plan.cap_rows) == group * plan.owners + source
    hit = same & (slot == want)
    factor = jnp.sum(jnp.where(hit, part, 0.0), axis=1, keepdims=True)
    return jnp.where(hit, 1.0, 0.0).astype(BF16), factor


def weight_copies(plan, array, ref, sems):
    offset = first_expert(plan)[1]
    copies = [
        pltpu.make_async_copy(array.at[offset + e], ref.at[e], sems.at[e])
        for e in range(plan.mine)
    ]
    for copy in copies:
        copy.start()
    return copies


def prepare_kernel(plan, x_hbm, routes_hbm, factors_hbm, gate_hbm, up_hbm, after, *refs):
    packed_ref, done_ref, own_ref = refs[:3]
    other_ref = refs[3] if plan.split > 1 else None
    gate_s, up_s, saved_sems, routes_ref, factors_ref, pack_sems = refs[plan.split + 2 :]
    done_ref[...] = jnp.zeros_like(done_ref)
    saved = [
        pltpu.make_async_copy(gate_hbm, gate_s, saved_sems.at[0]),
        pltpu.make_async_copy(up_hbm, up_s, saved_sems.at[1]),
    ]
    for copy in saved:
        copy.start()
    pack_body(
        plan, x_hbm, routes_hbm, factors_hbm, packed_ref, routes_ref, factors_ref, pack_sems
    )
    _, offset = first_expert(plan)
    shape = (plan.mine * plan.source_rows, gate_s.shape[0])
    row, col = iota(shape, 0), iota(shape, 1)
    slot = row % plan.cap_rows
    source = row % plan.source_rows // plan.cap_rows
    place = (source * plan.cap + slot) * plan.local + row // plan.source_rows
    place = jnp.where(slot < plan.cap, place, -plan.local)

    def pick(start, ref):
        table = jnp.where(col == place + start, 1.0, 0.0).astype(BF16)
        return dot(table, ref[...]).astype(BF16)

    for copy in saved:
        copy.wait()
    own_ref[0] = pick(offset, gate_s)
    own_ref[1] = pick(offset, up_s)
    if other_ref is not None:
        other_ref[0] = pick(plan.mine - offset, gate_s)
        other_ref[1] = pick(plan.mine - offset, up_s)


def prepare(plan, x, routes, factors, saved_gate, saved_up, after):
    flat = (plan.owners * plan.cap * plan.local, plan.hidden)

    def flatten(saved):
        return in_hbm(jnp.swapaxes(saved[0], 1, 2).reshape(flat))

    part = jax.ShapeDtypeStruct((2, plan.mine * plan.source_rows, plan.hidden), BF16)
    packed_shape = jax.ShapeDtypeStruct((plan.count, plan.sent), BF16)
    done_shape = jax.ShapeDtypeStruct((16, plan.sent), BF16)
    out_shape = [packed_shape, done_shape] + [part] * plan.split
    packed, done, *saved = pl.pallas_call(
        functools.partial(prepare_kernel, plan),
        out_shape=out_shape,
        in_specs=[hbm()] * 5 + [pl.BlockSpec(memory_space=pl.ANY)],
        out_specs=[vmem()] * len(out_shape),
        scratch_shapes=[
            pltpu.VMEM(flat, BF16),
            pltpu.VMEM(flat, BF16),
            pltpu.SemaphoreType.DMA((2,)),
            *pack_scratch(plan),
        ],
        compiler_params=pltpu.CompilerParams(vmem_limit_bytes=8 * MIB),
        cost_estimate=pl.CostEstimate(
            flops=0, bytes_accessed=plan.owners * plan.width * plan.sent, transcendentals=0
        ),
        name="prepare",
    )(
        in_hbm(x),
        in_hbm(routes.T),
        in_hbm(factors.T),
        flatten(saved_gate),
        flatten(saved_up),
        after,
    )
    return packed, saved, done


def fetch_kernel(plan, w_hbm, after, w_ref, done_ref, sems):
    copies = weight_copies(plan, w_hbm, w_ref, sems)
    done_ref[...] = jnp.zeros_like(done_ref)
    for copy in copies:
        copy.wait()


def fetch(plan, w, after):
    return pl.pallas_call(
        functools.partial(fetch_kernel, plan),
        out_shape=(
            pltpu.VMEM((plan.mine, plan.hidden, plan.width), BF16),
            jax.ShapeDtypeStruct((16, plan.sent), BF16),
        ),
        in_specs=[hbm(), pl.BlockSpec(memory_space=pl.ANY)],
        out_specs=(vmem(), vmem()),
        scratch_shapes=[pltpu.SemaphoreType.DMA((plan.mine,))],
        compiler_params=pltpu.CompilerParams(vmem_limit_bytes=MIB),
        cost_estimate=pl.CostEstimate(
            flops=0,
            bytes_accessed=2 * plan.mine * plan.hidden * plan.width * 2,
            transcendentals=0,
        ),
        name="fetch",
    )(in_hbm(w), after)


def arrived(plan, blocks, first):
    left, metas, rows = plan.cols, [], []
    for block in blocks:
        count = min(left, block.shape[0])
        metas.append(block[:count, plan.width :])
        rows.append(block[:count, : plan.width])
        left -= count
    table, factor = tables(plan, jnp.concatenate(metas, axis=0), first)
    return table, factor, jnp.concatenate(rows, axis=0)


def forward_kernel(plan, count, *refs):
    blocks, refs = refs[:count], refs[count:]
    gate_ref, up_hbm, down_hbm, *refs = refs
    outs, (up_s, down_s, x_s, y_s, gate_s, sems) = refs[:-6], refs[-6:]
    first, _ = first_expert(plan)
    up_copies = weight_copies(plan, up_hbm, up_s, sems.at[0])
    down_copies = weight_copies(plan, down_hbm, down_s, sems.at[1])
    table, factor, rows = arrived(plan, blocks, first)
    x_s[...] = dot(table, rows).astype(BF16)
    n = plan.expert_rows
    for e in range(plan.mine):
        gate_s[e] = dot_tb(x_s[e * n : (e + 1) * n, :], gate_ref[e])
    for e in range(plan.mine):
        up_copies[e].wait()
        up = dot_tb(x_s[e * n : (e + 1) * n, :], up_s[e])
        gate = gate_s[e]
        hidden = (gate / (1.0 + jnp.exp(-gate)) * up).astype(BF16)
        down_copies[e].wait()
        out = dot(hidden, down_s[e])
        y_s[e * n : (e + 1) * n, :] = (out * factor[e * n : (e + 1) * n]).astype(BF16)
    put_rows(plan, outs, slice(None), dot_ta(table, y_s[...]).astype(BF16))


def put_rows(plan, outs, columns, rows):
    start = 0
    for out in outs:
        stop = start + out.shape[0]
        out[:, columns] = rows[start:stop, :]
        start = stop


def backward_kernel(plan, count, *refs):
    blocks, refs = refs[:count], refs[count:]
    saved_ref, other_ref, refs = refs[0], refs[plan.split - 1], refs[plan.split :]
    gate_ref, up_hbm, down_hbm, *refs = refs
    held = plan.source_rows
    outs, (up_s, down_s, x_s, y_s, score_s, sems) = refs[:-6], refs[-6:]
    first, offset = first_expert(plan)
    copies = []
    for e in range(plan.mine):
        for i, (array, slot) in enumerate(((down_hbm, down_s), (up_hbm, up_s))):
            copy = pltpu.make_async_copy(array.at[offset + e], slot.at[e], sems.at[i, e])
            copy.start()
            copies.append(copy)
    table, factor, rows = arrived(plan, blocks, first)
    x_s[...] = dot(table, rows).astype(BF16)
    n = plan.expert_rows
    lane = iota((n, plan.meta), 1)
    for e in range(plan.mine):
        x = x_s[e * n : (e + 1) * n, :]
        own = slice(e * held, (e + 1) * held)
        act, up = saved_ref[0, own, :], saved_ref[1, own, :]
        if plan.split > 1:
            act = jnp.concatenate([act, other_ref[0, own, :]], axis=0)
            up = jnp.concatenate([up, other_ref[1, own, :]], axis=0)
        act, up = act.astype(F32), up.astype(F32)
        sig = 1.0 / (1.0 + jnp.exp(-act))
        silu = act * sig
        copies[2 * e].wait()
        grad = dot_tb(x, down_s[e])
        score = jnp.sum(silu * up * grad, axis=1, keepdims=True)
        grad_gate = (grad * up * sig * (1.0 + act * (1.0 - sig))).astype(BF16)
        grad_up = (grad * silu).astype(BF16)
        result = dot(grad_gate, gate_ref[e])
        copies[2 * e + 1].wait()
        result = result + dot(grad_up, up_s[e])
        y_s[e * n : (e + 1) * n, :] = (result * factor[e * n : (e + 1) * n]).astype(BF16)
        expert = first + e
        high = score.astype(BF16).astype(F32)
        middle = (score - high).astype(BF16).astype(F32)
        low = score - high - middle
        spread = jnp.where(lane == expert, high, 0.0)
        spread = jnp.where(lane == expert + plan.experts, middle, spread)
        spread = jnp.where(lane == expert + 2 * plan.experts, low, spread)
        score_s[e * n : (e + 1) * n, :] = spread.astype(BF16)
    put_rows(plan, outs, slice(0, plan.width), dot_ta(table, y_s[...]).astype(BF16))
    scores = dot_ta(table, score_s[...]).astype(BF16)
    put_rows(plan, outs, slice(plan.width, plan.width + plan.meta), scores)


def part_shapes(plan, width):
    block = jax.ShapeDtypeStruct((plan.count, width), BF16)
    other = jax.ShapeDtypeStruct((plan.owners * plan.count, width), BF16)
    return [block] * plan.owners + [other] * (plan.split - 1)


def expert_call(plan, kernel, name, inputs, gate, up_hbm, down_hbm, width, scratch):
    shapes = part_shapes(plan, width)
    weight = pltpu.VMEM((plan.mine, plan.hidden, plan.width), BF16)
    rows = pltpu.VMEM((plan.rows, plan.width), BF16)
    return pl.pallas_call(
        kernel,
        out_shape=shapes,
        in_specs=[vmem()] * (len(inputs) + 1) + [hbm()] * 2,
        out_specs=[vmem()] * len(shapes),
        scratch_shapes=[
            *[weight, weight, rows, rows],
            scratch,
            pltpu.SemaphoreType.DMA((2, plan.mine)),
        ],
        compiler_params=pltpu.CompilerParams(vmem_limit_bytes=36 * MIB),
        cost_estimate=pl.CostEstimate(
            flops=2 * 3 * plan.mine * plan.expert_rows * plan.width * plan.hidden,
            bytes_accessed=2 * 2 * plan.mine * plan.width * plan.hidden,
            transcendentals=0,
        ),
        name=name,
    )(*inputs, in_vmem(gate), in_hbm(up_hbm), in_hbm(down_hbm))


def forward(plan, blocks, *weights):
    kernel = functools.partial(forward_kernel, plan, len(blocks))
    gates = pltpu.VMEM((plan.mine, plan.expert_rows, plan.hidden), F32)
    return expert_call(plan, kernel, "forward", blocks, *weights, plan.width, gates)


def backward(plan, blocks, saved, *weights):
    kernel = functools.partial(backward_kernel, plan, len(blocks))
    scores = pltpu.VMEM((plan.rows, plan.meta), BF16)
    inputs = [*blocks, *saved]
    return expert_call(plan, kernel, "backward", inputs, *weights, plan.sent, scores)


def gather_group(plan, block):
    return [block] + [plan.over_expert(block, d) for d in range(1, plan.owners)]


def sum_pair(plan, parts):
    own = [[p] for p in parts[: plan.owners]]
    if plan.split > 1:
        other = plan.over_pair(parts[plan.owners])
        for d in range(plan.owners):
            own[d].append(other[d * plan.count : (d + 1) * plan.count])
    return own


def total(terms):
    return sum(t.astype(F32) for t in terms)


def scatter_group(plan, own):
    sent = [total(own[d]).astype(BF16) for d in range(1, plan.owners)]
    return own[0] + [plan.over_expert(x, d, True) for d, x in enumerate(sent, 1)]


def scatter_steps(plan, own):
    if not plan.paired:
        return scatter_group(plan, own)
    step = 1
    while step < plan.owners:
        away = [d for d in range(0, plan.owners, step) if d & step]
        sent = jnp.concatenate([total(own[d]).astype(BF16) for d in away])
        back = plan.over_expert(sent, step, True)
        for i, d in enumerate(away):
            own[d ^ step].append(back[i * plan.count : (i + 1) * plan.count])
        step *= 2
    return own[0]


def finish_kernel(plan, count, *refs):
    parts, (routes_ref, out_hbm, score_hbm, out_s, score_s, sems) = refs[:count], refs[count:]
    whole = parts[0][: plan.count, :].astype(F32)
    for part in parts[1:]:
        whole = whole + part[: plan.count, :].astype(F32)
    out_s[...] = whole[:, : plan.width].astype(BF16)
    out_copy = pltpu.make_async_copy(out_s, out_hbm, sems.at[0])
    out_copy.start()
    shape = (plan.meta, plan.meta)
    same = jnp.where(iota(shape, 0) == iota(shape, 1), 1.0, 0.0).astype(BF16)
    spread = dot_tb(same, whole[:, plan.width :].astype(BF16))
    experts = plan.experts
    score = spread[:experts] + spread[experts : 2 * experts] + spread[2 * experts : 3 * experts]
    row = iota((experts, plan.count), 0)
    for k in range(plan.top):
        hit = row == routes_ref[k : k + 1, :]
        score_s[k : k + 1, :] = jnp.sum(jnp.where(hit, score, 0.0), axis=0, keepdims=True)
    score_copy = pltpu.make_async_copy(score_s, score_hbm, sems.at[1])
    score_copy.start()
    out_copy.wait()
    score_copy.wait()


def finish_back(plan, parts, routes):
    out, score = pl.pallas_call(
        functools.partial(finish_kernel, plan, len(parts)),
        out_shape=(
            jax.ShapeDtypeStruct((plan.count, plan.width), BF16),
            jax.ShapeDtypeStruct((plan.top, plan.count), F32),
        ),
        in_specs=[vmem()] * (len(parts) + 1),
        out_specs=(hbm(), hbm()),
        scratch_shapes=[
            pltpu.VMEM((plan.count, plan.width), BF16),
            pltpu.VMEM((plan.top, plan.count), F32),
            pltpu.SemaphoreType.DMA((2,)),
        ],
        compiler_params=pltpu.CompilerParams(vmem_limit_bytes=8 * MIB),
        name="finish",
    )(*parts, routes.T)
    return out, score.T


def body(
    tokens,
    routes,
    weights_fwd,
    cotangent,
    routes_back,
    weights_back,
    saved_gate,
    saved_up,
    w_gate,
    w_up,
    w_down,
):
    plan = Plan(tokens, routes, saved_gate, w_gate)
    packed = pack(plan, tokens, routes, weights_fwd)
    packed_back, saved, ready = prepare(
        plan, cotangent, routes_back, weights_back, saved_gate, saved_up, packed
    )
    gate_hbm, up_hbm = jnp.swapaxes(w_gate, 1, 2), jnp.swapaxes(w_up, 1, 2)
    if plan.paired and plan.owners > 1:
        blocks = [packed, plan.over_expert(packed, 1)]
        gate, done = fetch(plan, gate_hbm, blocks[1])
        step = 2
        while step < plan.owners:
            blocks.append(plan.over_expert(jnp.concatenate(blocks) + ready[:1], step))
            step *= 2
    else:
        blocks = gather_group(plan, packed)
        gate, done = fetch(plan, gate_hbm, packed)
    if plan.split > 1:
        blocks.append(plan.over_pair(jnp.concatenate(blocks) + done[:1]))
    blocks_back = gather_group(plan, packed_back)
    parts = forward(plan, blocks, gate, up_hbm, w_down)
    parts, blocks_back = lax.optimization_barrier((parts, blocks_back))
    if plan.split > 1:
        blocks_back = blocks_back + [plan.over_pair(jnp.concatenate(blocks_back))]
        saved[1] = plan.over_pair(saved[1])
    terms = scatter_group(plan, sum_pair(plan, parts))
    parts_back = backward(plan, blocks_back, saved, gate, up_hbm, w_down)
    parts_back, terms = lax.optimization_barrier((parts_back, terms))
    mixed = total(terms).astype(BF16)
    terms_back = scatter_steps(plan, sum_pair(plan, parts_back))
    input_grad, weight_grad = finish_back(plan, terms_back, routes_back)
    return (mixed, input_grad, weight_grad)


def solution(mesh):
    spec = P(("dp", "expert"), None)
    saved = P("dp", None, "expert", None, None)
    weight = P("expert", None, None)
    return jax.shard_map(
        body,
        mesh=mesh,
        in_specs=(spec,) * 6 + (saved,) * 2 + (weight,) * 3,
        out_specs=(spec,) * 3,
        check_vma=False,
    )
```

```python
import functools
import jax
import jax.numpy as jnp
from jax import lax
from jax.experimental import pallas as pl
from jax.experimental.pallas import tpu as pltpu
from jax.sharding import PartitionSpec as P

F32 = jnp.float32
BF16 = jnp.bfloat16
LANES = 128
MIB = 1 << 20


def round_up(value, unit):
    return -(-value // unit) * unit


def dot(a, b):
    return jnp.dot(a, b, preferred_element_type=F32)


def dot_tb(a, b):
    return lax.dot_general(a, b, (((1,), (1,)), ((), ())), preferred_element_type=F32)


def dot_ta(a, b):
    return lax.dot_general(a, b, (((0,), (0,)), ((), ())), preferred_element_type=F32)


def iota(shape, dim):
    return lax.broadcasted_iota(jnp.int32, shape, dim)


def vmem():
    return pl.BlockSpec(memory_space=pltpu.VMEM)


def hbm():
    return pl.BlockSpec(memory_space=pltpu.HBM)


def in_vmem(x):
    return pltpu.with_memory_space_constraint(x, pltpu.VMEM)


def in_hbm(x):
    return pltpu.with_memory_space_constraint(x, pltpu.HBM)


class Plan:
    def __init__(self, tokens, routes, saved_gate, w_gate):
        self.owners = lax.axis_size("expert")
        self.groups = lax.axis_size("dp")
        self.count, self.width = tokens.shape
        self.top = routes.shape[1]
        self.local = w_gate.shape[0]
        self.hidden = w_gate.shape[2]
        self.experts = self.owners * self.local
        self.cap = saved_gate.shape[3]
        self.cap_rows = round_up(self.cap, 8)
        self.split = 2 if self.groups % 2 == 0 and self.local % 2 == 0 else 1
        self.mine = self.local // self.split
        self.meta = round_up(3 * self.experts, LANES)
        self.blocks = self.split * self.owners
        self.source_rows = self.owners * self.cap_rows
        self.expert_rows = self.split * self.source_rows
        self.paired = self.owners & (self.owners - 1) == 0
        self.sent = self.width + self.meta
        self.half = round_up(self.width // 2, LANES)
        self.rows = self.mine * self.expert_rows
        self.cols = self.blocks * self.count

    def peer(self, index, step, core):
        bits = self.owners.bit_length() - 1
        if self.owners != 1 << bits:
            return (index + step) % self.owners
        turned = sum(((step >> i) & 1) << (bits - 1 - i) for i in range(bits))
        return index ^ (step + (turned - step) * core)

    def over_expert(self, x, step, back=False):
        pairs = []
        for group in range(self.groups):
            for i in range(self.owners):
                near = group * self.owners + i
                far = self.peer(i, step, group % self.split) + group * self.owners
                pairs.append((near, far) if back else (far, near))
        return lax.ppermute(x, ("dp", "expert"), pairs)

    def over_pair(self, x):
        return lax.ppermute(x, "dp", [(i, i ^ 1) for i in range(self.groups)])


def pack_body(plan, x_hbm, routes_hbm, factors_hbm, out_ref, routes_ref, factors_ref, sems):
    experts, count = plan.experts, plan.count
    x_copy = pltpu.make_async_copy(x_hbm, out_ref.at[:, : plan.width], sems.at[0])
    small = [
        pltpu.make_async_copy(routes_hbm, routes_ref, sems.at[1]),
        pltpu.make_async_copy(factors_hbm, factors_ref, sems.at[2]),
    ]
    for copy in (*small, x_copy):
        copy.start()
    for copy in small:
        copy.wait()
    lane = iota((plan.meta, count), 0)
    chosen = jnp.zeros((plan.meta, count), F32)
    parts = jnp.zeros((plan.meta, count), F32)
    for k in range(plan.top):
        route = routes_ref[k : k + 1, :]
        factor = factors_ref[k : k + 1, :]
        high = factor.astype(BF16).astype(F32)
        low = factor - high
        chosen = chosen + jnp.where(lane == route, 1.0, 0.0)
        parts = parts + jnp.where(lane == route + experts, high, 0.0)
        parts = parts + jnp.where(lane == route + 2 * experts, low, 0.0)
    earlier = jnp.where(iota((count, count), 0) < iota((count, count), 1), 1.0, 0.0)
    before = dot(chosen.astype(BF16), earlier.astype(BF16))
    facts = (chosen * (before + 1.0) + parts).astype(BF16)
    shape = (plan.meta, plan.meta)
    same = jnp.where(iota(shape, 0) == iota(shape, 1), 1.0, 0.0).astype(BF16)
    out_ref[:, plan.width :] = dot_ta(facts, same).astype(BF16)
    x_copy.wait()


def pack_scratch(plan):
    return [
        pltpu.VMEM((plan.top, plan.count), jnp.int32),
        pltpu.VMEM((plan.top, plan.count), F32),
        pltpu.SemaphoreType.DMA((3,)),
    ]


def pack(plan, x, routes, factors):
    return pl.pallas_call(
        functools.partial(pack_body, plan),
        out_shape=jax.ShapeDtypeStruct((plan.count, plan.width + plan.meta), BF16),
        in_specs=[hbm()] * 3,
        out_specs=vmem(),
        scratch_shapes=pack_scratch(plan),
        compiler_params=pltpu.CompilerParams(vmem_limit_bytes=4 * MIB),
        name="pack",
    )(in_hbm(x), in_hbm(routes.T), in_hbm(factors.T))


def first_expert(plan):
    core = lax.rem(lax.axis_index("dp"), plan.split)
    return lax.axis_index("expert") * plan.local + core * plan.mine, core * plan.mine


def tables(plan, meta, first):
    me = lax.axis_index("expert")
    core = lax.rem(lax.axis_index("dp"), plan.split)
    row = iota((plan.rows, plan.meta), 0)
    lane = iota((plan.rows, plan.meta), 1)
    expert = first + row // plan.expert_rows
    pick_slot = jnp.where(lane == expert, 1.0, 0.0).astype(BF16)
    pick_part = jnp.where(
        (lane == expert + plan.experts) | (lane == expert + 2 * plan.experts), 1.0, 0.0
    ).astype(BF16)
    slot = dot_tb(pick_slot, meta)
    part = dot_tb(pick_part, meta)
    shape = (plan.rows, plan.cols)
    row = iota(shape, 0)
    col = iota(shape, 1)
    block = col // plan.count
    group = block // plan.owners
    source = plan.peer(me, block % plan.owners, core ^ group)
    place = row % plan.expert_rows
    want = (row % plan.cap_rows + 1).astype(F32)
    same = (place // plan.cap_rows) == group * plan.owners + source
    hit = same & (slot == want)
    factor = jnp.sum(jnp.where(hit, part, 0.0), axis=1, keepdims=True)
    return jnp.where(hit, 1.0, 0.0).astype(BF16), factor


def weight_copies(plan, array, ref, sems):
    offset = first_expert(plan)[1]
    return [
        pltpu.make_async_copy(array.at[offset + e], ref.at[e], sems.at[e])
        for e in range(plan.mine)
    ]


def prepare_kernel(plan, x_hbm, routes_hbm, factors_hbm, gate_hbm, up_hbm, after, *refs):
    packed_ref, done_ref, own_ref = refs[:3]
    other_ref = refs[3] if plan.split > 1 else None
    gate_s, up_s, saved_sems, routes_ref, factors_ref, pack_sems = refs[plan.split + 2 :]
    done_ref[...] = jnp.zeros_like(done_ref)
    saved = [
        pltpu.make_async_copy(gate_hbm, gate_s, saved_sems.at[0]),
        pltpu.make_async_copy(up_hbm, up_s, saved_sems.at[1]),
    ]
    for copy in saved:
        copy.start()
    pack_body(
        plan, x_hbm, routes_hbm, factors_hbm, packed_ref, routes_ref, factors_ref, pack_sems
    )
    _, offset = first_expert(plan)
    shape = (plan.mine * plan.source_rows, gate_s.shape[0])
    row, col = iota(shape, 0), iota(shape, 1)
    slot = row % plan.cap_rows
    source = row % plan.source_rows // plan.cap_rows
    place = (source * plan.cap + slot) * plan.local + row // plan.source_rows
    place = jnp.where(slot < plan.cap, place, -plan.local)

    def pick(start, ref):
        table = jnp.where(col == place + start, 1.0, 0.0).astype(BF16)
        return dot(table, ref[...]).astype(BF16)

    for copy in saved:
        copy.wait()
    own_ref[0] = pick(offset, gate_s)
    own_ref[1] = pick(offset, up_s)
    if other_ref is not None:
        other_ref[0] = pick(plan.mine - offset, gate_s)
        other_ref[1] = pick(plan.mine - offset, up_s)


def prepare(plan, x, routes, factors, saved_gate, saved_up, after):
    flat = (plan.owners * plan.cap * plan.local, plan.hidden)

    def flatten(saved):
        return in_hbm(jnp.swapaxes(saved[0], 1, 2).reshape(flat))

    part = jax.ShapeDtypeStruct((2, plan.mine * plan.source_rows, plan.hidden), BF16)
    packed_shape = jax.ShapeDtypeStruct((plan.count, plan.sent), BF16)
    done_shape = jax.ShapeDtypeStruct((16, plan.sent), BF16)
    out_shape = [packed_shape, done_shape] + [part] * plan.split
    packed, done, *saved = pl.pallas_call(
        functools.partial(prepare_kernel, plan),
        out_shape=out_shape,
        in_specs=[hbm()] * 5 + [pl.BlockSpec(memory_space=pl.ANY)],
        out_specs=[vmem()] * len(out_shape),
        scratch_shapes=[
            pltpu.VMEM(flat, BF16),
            pltpu.VMEM(flat, BF16),
            pltpu.SemaphoreType.DMA((2,)),
            *pack_scratch(plan),
        ],
        compiler_params=pltpu.CompilerParams(vmem_limit_bytes=8 * MIB),
        cost_estimate=pl.CostEstimate(
            flops=0, bytes_accessed=plan.owners * plan.width * plan.sent, transcendentals=0
        ),
        name="prepare",
    )(
        in_hbm(x),
        in_hbm(routes.T),
        in_hbm(factors.T),
        flatten(saved_gate),
        flatten(saved_up),
        after,
    )
    return packed, saved, done


def fetch_kernel(plan, w_hbm, after, w_ref, done_ref, sems):
    copies = weight_copies(plan, w_hbm, w_ref, sems)
    for copy in copies:
        copy.start()
    done_ref[...] = jnp.zeros_like(done_ref)
    for copy in copies:
        copy.wait()


def fetch(plan, w, after):
    return pl.pallas_call(
        functools.partial(fetch_kernel, plan),
        out_shape=(
            pltpu.VMEM((plan.mine, plan.hidden, plan.width), BF16),
            jax.ShapeDtypeStruct((16, plan.sent), BF16),
        ),
        in_specs=[hbm(), pl.BlockSpec(memory_space=pl.ANY)],
        out_specs=(vmem(), vmem()),
        scratch_shapes=[pltpu.SemaphoreType.DMA((plan.mine,))],
        compiler_params=pltpu.CompilerParams(vmem_limit_bytes=MIB),
        cost_estimate=pl.CostEstimate(
            flops=0,
            bytes_accessed=2 * plan.mine * plan.hidden * plan.width * 2,
            transcendentals=0,
        ),
        name="fetch",
    )(in_hbm(w), after)


def arrived(plan, blocks, first):
    left, metas, rows = plan.cols, [], []
    for block in blocks:
        count = min(left, block.shape[0])
        metas.append(block[:count, plan.width :])
        rows.append(block[:count, : plan.width])
        left -= count
    table, factor = tables(plan, jnp.concatenate(metas, axis=0), first)
    return table, factor, jnp.concatenate(rows, axis=0)


def forward_kernel(plan, count, *refs):
    blocks, refs = refs[:count], refs[count:]
    gate_ref, up_hbm, down_hbm, *refs = refs
    outs, (up_s, down_s, x_s, y_s, gate_s, sems) = refs[:-6], refs[-6:]
    first, _ = first_expert(plan)
    up_copies = weight_copies(plan, up_hbm, up_s, sems.at[0])
    down_copies = weight_copies(plan, down_hbm, down_s, sems.at[1])
    up_copies[0].start()
    down_copies[0].start()
    table, factor, rows = arrived(plan, blocks, first)
    x_s[...] = dot(table, rows).astype(BF16)
    n = plan.expert_rows
    for e in range(plan.mine):
        gate_s[e] = dot_tb(x_s[e * n : (e + 1) * n, :], gate_ref[e])
        if e + 1 < plan.mine:
            up_copies[e + 1].start()
            down_copies[e + 1].start()
    for e in range(plan.mine):
        up_copies[e].wait()
        up = dot_tb(x_s[e * n : (e + 1) * n, :], up_s[e])
        gate = gate_s[e]
        hidden = (gate / (1.0 + jnp.exp(-gate)) * up).astype(BF16)
        down_copies[e].wait()
        out = dot(hidden, down_s[e])
        y_s[e * n : (e + 1) * n, :] = (out * factor[e * n : (e + 1) * n]).astype(BF16)
    put_rows(outs, slice(None), dot_ta(table, y_s[...]).astype(BF16))


def put_rows(outs, columns, rows):
    start = 0
    for out in outs:
        stop = start + out.shape[0]
        out[:, columns] = rows[start:stop, :]
        start = stop


def backward_kernel(plan, count, *refs):
    blocks, refs = refs[:count], refs[count:]
    saved_ref, other_ref, refs = refs[0], refs[plan.split - 1], refs[plan.split :]
    gate_ref, up_hbm, down_hbm, *refs = refs
    held = plan.source_rows
    outs, (up_s, down_s, x_s, y_s, score_s, sems) = refs[:-6], refs[-6:]
    first, _ = first_expert(plan)
    up_copies = weight_copies(plan, up_hbm, up_s, sems.at[0])
    down_copies = weight_copies(plan, down_hbm, down_s, sems.at[1])
    down_copies[0].start()
    table, factor, rows = arrived(plan, blocks, first)
    up_copies[0].start()
    x_s[...] = dot(table, rows).astype(BF16)
    n = plan.expert_rows
    lane = iota((n, plan.meta), 1)
    for e in range(plan.mine):
        x = x_s[e * n : (e + 1) * n, :]
        own = slice(e * held, (e + 1) * held)
        act, up = saved_ref[0, own, :], saved_ref[1, own, :]
        if plan.split > 1:
            act = jnp.concatenate([act, other_ref[0, own, :]], axis=0)
            up = jnp.concatenate([up, other_ref[1, own, :]], axis=0)
        act, up = act.astype(F32), up.astype(F32)
        sig = 1.0 / (1.0 + jnp.exp(-act))
        silu = act * sig
        down_copies[e].wait()
        if e + 1 < plan.mine:
            down_copies[e + 1].start()
            up_copies[e + 1].start()
        grad = dot_tb(x, down_s[e])
        score = jnp.sum(silu * up * grad, axis=1, keepdims=True)
        grad_gate = (grad * up * sig * (1.0 + act * (1.0 - sig))).astype(BF16)
        grad_up = (grad * silu).astype(BF16)
        result = dot(grad_gate, gate_ref[e])
        up_copies[e].wait()
        result = result + dot(grad_up, up_s[e])
        y_s[e * n : (e + 1) * n, :] = (result * factor[e * n : (e + 1) * n]).astype(BF16)
        expert = first + e
        high = score.astype(BF16).astype(F32)
        middle = (score - high).astype(BF16).astype(F32)
        low = score - high - middle
        spread = jnp.where(lane == expert, high, 0.0)
        spread = jnp.where(lane == expert + plan.experts, middle, spread)
        spread = jnp.where(lane == expert + 2 * plan.experts, low, spread)
        score_s[e * n : (e + 1) * n, :] = spread.astype(BF16)
    half, near = plan.half, outs[: len(outs) // 2]
    far = outs[len(outs) // 2 :]
    put_rows(near, slice(0, half), dot_ta(table, y_s[:, :half]).astype(BF16))
    rest = plan.width - half
    put_rows(far, slice(0, rest), dot_ta(table, y_s[:, half:]).astype(BF16))
    scores = dot_ta(table, score_s[...]).astype(BF16)
    put_rows(far, slice(rest, rest + plan.meta), scores)


def part_shapes(plan, width):
    block = jax.ShapeDtypeStruct((plan.count, width), BF16)
    other = jax.ShapeDtypeStruct((plan.owners * plan.count, width), BF16)
    return [block] * plan.owners + [other] * (plan.split - 1)


def expert_call(plan, kernel, name, inputs, gate, up_hbm, down_hbm, widths, scratch):
    shapes = [shape for width in widths for shape in part_shapes(plan, width)]
    weight = pltpu.VMEM((plan.mine, plan.hidden, plan.width), BF16)
    rows = pltpu.VMEM((plan.rows, plan.width), BF16)
    return pl.pallas_call(
        kernel,
        out_shape=shapes,
        in_specs=[vmem()] * (len(inputs) + 1) + [hbm()] * 2,
        out_specs=[vmem()] * len(shapes),
        scratch_shapes=[
            *[weight, weight, rows, rows],
            scratch,
            pltpu.SemaphoreType.DMA((2, plan.mine)),
        ],
        compiler_params=pltpu.CompilerParams(vmem_limit_bytes=36 * MIB),
        cost_estimate=pl.CostEstimate(
            flops=2 * 3 * plan.mine * plan.expert_rows * plan.width * plan.hidden,
            bytes_accessed=2 * 2 * plan.mine * plan.width * plan.hidden,
            transcendentals=0,
        ),
        name=name,
    )(*inputs, in_vmem(gate), in_hbm(up_hbm), in_hbm(down_hbm))


def forward(plan, blocks, *weights):
    kernel = functools.partial(forward_kernel, plan, len(blocks))
    gates = pltpu.VMEM((plan.mine, plan.expert_rows, plan.hidden), F32)
    return expert_call(plan, kernel, "forward", blocks, *weights, [plan.width], gates)


def backward(plan, blocks, saved, *weights):
    kernel = functools.partial(backward_kernel, plan, len(blocks))
    scores = pltpu.VMEM((plan.rows, plan.meta), BF16)
    widths = [plan.half, plan.sent - plan.half]
    inputs = [*blocks, *saved]
    parts = expert_call(plan, kernel, "backward", inputs, *weights, widths, scores)
    return parts[: len(parts) // 2], parts[len(parts) // 2 :]


def gather_group(plan, block):
    return [block] + [plan.over_expert(block, d) for d in range(1, plan.owners)]


def sum_pair(plan, parts):
    own = [[p] for p in parts[: plan.owners]]
    if plan.split > 1:
        other = plan.over_pair(parts[plan.owners])
        for d in range(plan.owners):
            own[d].append(other[d * plan.count : (d + 1) * plan.count])
    return own


def total(terms):
    return sum(t.astype(F32) for t in terms)


def scatter_group(plan, own):
    sent = [total(own[d]).astype(BF16) for d in range(1, plan.owners)]
    return own[0] + [plan.over_expert(x, d, True) for d, x in enumerate(sent, 1)]


def scatter_steps(plan, owns):
    if not plan.paired:
        return [scatter_group(plan, own) for own in owns]
    step = 1
    while step < plan.owners:
        away = [d for d in range(0, plan.owners, step) if d & step]
        for own in owns:
            sent = jnp.concatenate([total(own[d]).astype(BF16) for d in away])
            back = plan.over_expert(sent, step, True)
            for i, d in enumerate(away):
                own[d ^ step].append(back[i * plan.count : (i + 1) * plan.count])
        step *= 2
    return [own[0] for own in owns]


def finish_kernel(plan, count, *refs):
    parts, (routes_ref, out_hbm, score_hbm, out_s, score_s, sems) = refs[:count], refs[count:]
    half, rest = plan.half, plan.width - plan.half
    near = total([part[...] for part in parts[: count // 2]])
    far = total([part[...] for part in parts[count // 2 :]])
    out_s[:, :half] = near.astype(BF16)
    out_s[:, half:] = far[:, :rest].astype(BF16)
    out_copy = pltpu.make_async_copy(out_s, out_hbm, sems.at[0])
    out_copy.start()
    shape = (plan.meta, plan.meta)
    same = jnp.where(iota(shape, 0) == iota(shape, 1), 1.0, 0.0).astype(BF16)
    spread = dot_tb(same, far[:, rest:].astype(BF16))
    experts = plan.experts
    score = spread[:experts] + spread[experts : 2 * experts] + spread[2 * experts : 3 * experts]
    row = iota((experts, plan.count), 0)
    for k in range(plan.top):
        hit = row == routes_ref[k : k + 1, :]
        score_s[k : k + 1, :] = jnp.sum(jnp.where(hit, score, 0.0), axis=0, keepdims=True)
    score_copy = pltpu.make_async_copy(score_s, score_hbm, sems.at[1])
    score_copy.start()
    out_copy.wait()
    score_copy.wait()


def finish_back(plan, parts, routes):
    out, score = pl.pallas_call(
        functools.partial(finish_kernel, plan, len(parts)),
        out_shape=(
            jax.ShapeDtypeStruct((plan.count, plan.width), BF16),
            jax.ShapeDtypeStruct((plan.top, plan.count), F32),
        ),
        in_specs=[vmem()] * (len(parts) + 1),
        out_specs=(hbm(), hbm()),
        scratch_shapes=[
            pltpu.VMEM((plan.count, plan.width), BF16),
            pltpu.VMEM((plan.top, plan.count), F32),
            pltpu.SemaphoreType.DMA((2,)),
        ],
        compiler_params=pltpu.CompilerParams(vmem_limit_bytes=8 * MIB),
        name="finish",
    )(*parts, routes.T)
    return out, score.T


def body(
    tokens,
    routes,
    weights_fwd,
    cotangent,
    routes_back,
    weights_back,
    saved_gate,
    saved_up,
    w_gate,
    w_up,
    w_down,
):
    plan = Plan(tokens, routes, saved_gate, w_gate)
    packed = pack(plan, tokens, routes, weights_fwd)
    packed_back, saved, ready = prepare(
        plan, cotangent, routes_back, weights_back, saved_gate, saved_up, packed
    )
    gate_hbm, up_hbm = jnp.swapaxes(w_gate, 1, 2), jnp.swapaxes(w_up, 1, 2)
    if plan.paired and plan.owners > 1:
        blocks = [packed, plan.over_expert(packed, 1)]
        gate, done = fetch(plan, gate_hbm, blocks[1])
        step = 2
        while step < plan.owners:
            blocks.append(plan.over_expert(jnp.concatenate(blocks) + ready[:1], step))
            step *= 2
    else:
        blocks = gather_group(plan, packed)
        gate, done = fetch(plan, gate_hbm, packed)
    if plan.split > 1:
        blocks.append(plan.over_pair(jnp.concatenate(blocks) + done[:1]))
    blocks_back = gather_group(plan, packed_back)
    parts = forward(plan, blocks, gate, up_hbm, w_down)
    parts, blocks_back = lax.optimization_barrier((parts, blocks_back))
    if plan.split > 1:
        blocks_back = blocks_back + [plan.over_pair(jnp.concatenate(blocks_back))]
        saved[1] = plan.over_pair(saved[1])
    terms = scatter_group(plan, sum_pair(plan, parts))
    parts_back = backward(plan, blocks_back, saved, gate, up_hbm, w_down)
    parts_back, terms = lax.optimization_barrier((parts_back, terms))
    mixed = total(terms).astype(BF16)
    near, far = scatter_steps(plan, [sum_pair(plan, parts) for parts in parts_back])
    input_grad, weight_grad = finish_back(plan, near + far, routes_back)
    return (mixed, input_grad, weight_grad)


def solution(mesh):
    spec = P(("dp", "expert"), None)
    saved = P("dp", None, "expert", None, None)
    weight = P("expert", None, None)
    return jax.shard_map(
        body,
        mesh=mesh,
        in_specs=(spec,) * 6 + (saved,) * 2 + (weight,) * 3,
        out_specs=(spec,) * 3,
        check_vma=False,
    )
```

```python
import functools
import jax
import jax.numpy as jnp
from jax import lax
from jax.experimental import pallas as pl
from jax.experimental.pallas import tpu as pltpu
from jax.sharding import PartitionSpec as P

F32 = jnp.float32
BF16 = jnp.bfloat16
LANES = 128
MIB = 1 << 20


def round_up(value, unit):
    return -(-value // unit) * unit


def dot(a, b):
    return jnp.dot(a, b, preferred_element_type=F32)


def dot_tb(a, b):
    return lax.dot_general(a, b, (((1,), (1,)), ((), ())), preferred_element_type=F32)


def dot_ta(a, b):
    return lax.dot_general(a, b, (((0,), (0,)), ((), ())), preferred_element_type=F32)


def iota(shape, dim):
    return lax.broadcasted_iota(jnp.int32, shape, dim)


def vmem():
    return pl.BlockSpec(memory_space=pltpu.VMEM)


def hbm():
    return pl.BlockSpec(memory_space=pltpu.HBM)


def in_vmem(x):
    return pltpu.with_memory_space_constraint(x, pltpu.VMEM)


def in_hbm(x):
    return pltpu.with_memory_space_constraint(x, pltpu.HBM)


class Plan:
    def __init__(self, tokens, routes, saved_gate, w_gate):
        self.owners = lax.axis_size("expert")
        self.groups = lax.axis_size("dp")
        self.count, self.width = tokens.shape
        self.top = routes.shape[1]
        self.local = w_gate.shape[0]
        self.hidden = w_gate.shape[2]
        self.experts = self.owners * self.local
        self.cap = saved_gate.shape[3]
        self.cap_rows = round_up(self.cap, 8)
        self.split = 2 if self.groups % 2 == 0 and self.local % 2 == 0 else 1
        self.mine = self.local // self.split
        self.meta = round_up(3 * self.experts, LANES)
        self.blocks = self.split * self.owners
        self.source_rows = self.owners * self.cap_rows
        self.expert_rows = self.split * self.source_rows
        self.paired = self.owners & (self.owners - 1) == 0
        self.sent = self.width + self.meta
        self.half = round_up(self.width // 2, LANES)
        self.rows = self.mine * self.expert_rows
        self.cols = self.blocks * self.count

    def peer(self, index, step, core):
        bits = self.owners.bit_length() - 1
        if self.owners != 1 << bits:
            return (index + step) % self.owners
        turned = sum(((step >> i) & 1) << (bits - 1 - i) for i in range(bits))
        return index ^ (step + (turned - step) * core)

    def over_expert(self, x, step, back=False):
        pairs = []
        for group in range(self.groups):
            for i in range(self.owners):
                near = group * self.owners + i
                far = self.peer(i, step, group % self.split) + group * self.owners
                pairs.append((near, far) if back else (far, near))
        return lax.ppermute(x, ("dp", "expert"), pairs)

    def over_pair(self, x):
        return lax.ppermute(x, "dp", [(i, i ^ 1) for i in range(self.groups)])


def pack_body(plan, x_hbm, routes_hbm, factors_hbm, out_ref, routes_ref, factors_ref, sems):
    experts, count = plan.experts, plan.count
    x_copy = pltpu.make_async_copy(x_hbm, out_ref.at[:, : plan.width], sems.at[0])
    small = [
        pltpu.make_async_copy(routes_hbm, routes_ref, sems.at[1]),
        pltpu.make_async_copy(factors_hbm, factors_ref, sems.at[2]),
    ]
    for copy in (*small, x_copy):
        copy.start()
    for copy in small:
        copy.wait()
    lane = iota((plan.meta, count), 0)
    chosen = jnp.zeros((plan.meta, count), F32)
    parts = jnp.zeros((plan.meta, count), F32)
    for k in range(plan.top):
        route = routes_ref[k : k + 1, :]
        factor = factors_ref[k : k + 1, :]
        high = factor.astype(BF16).astype(F32)
        low = factor - high
        chosen = chosen + jnp.where(lane == route, 1.0, 0.0)
        parts = parts + jnp.where(lane == route + experts, high, 0.0)
        parts = parts + jnp.where(lane == route + 2 * experts, low, 0.0)
    earlier = jnp.where(iota((count, count), 0) < iota((count, count), 1), 1.0, 0.0)
    before = dot(chosen.astype(BF16), earlier.astype(BF16))
    facts = (chosen * (before + 1.0) + parts).astype(BF16)
    shape = (plan.meta, plan.meta)
    same = jnp.where(iota(shape, 0) == iota(shape, 1), 1.0, 0.0).astype(BF16)
    out_ref[:, plan.width :] = dot_ta(facts, same).astype(BF16)
    x_copy.wait()


def pack_scratch(plan):
    return [
        pltpu.VMEM((plan.top, plan.count), jnp.int32),
        pltpu.VMEM((plan.top, plan.count), F32),
        pltpu.SemaphoreType.DMA((3,)),
    ]


def pack(plan, x, routes, factors):
    return pl.pallas_call(
        functools.partial(pack_body, plan),
        out_shape=jax.ShapeDtypeStruct((plan.count, plan.width + plan.meta), BF16),
        in_specs=[hbm()] * 3,
        out_specs=vmem(),
        scratch_shapes=pack_scratch(plan),
        compiler_params=pltpu.CompilerParams(vmem_limit_bytes=4 * MIB),
        name="pack",
    )(in_hbm(x), in_hbm(routes.T), in_hbm(factors.T))


def first_expert(plan):
    core = lax.rem(lax.axis_index("dp"), plan.split)
    return lax.axis_index("expert") * plan.local + core * plan.mine, core * plan.mine


def tables(plan, meta, first):
    me = lax.axis_index("expert")
    core = lax.rem(lax.axis_index("dp"), plan.split)
    row = iota((plan.rows, plan.meta), 0)
    lane = iota((plan.rows, plan.meta), 1)
    expert = first + row // plan.expert_rows
    pick_slot = jnp.where(lane == expert, 1.0, 0.0).astype(BF16)
    pick_part = jnp.where(
        (lane == expert + plan.experts) | (lane == expert + 2 * plan.experts), 1.0, 0.0
    ).astype(BF16)
    slot = dot_tb(pick_slot, meta)
    part = dot_tb(pick_part, meta)
    shape = (plan.rows, plan.cols)
    row = iota(shape, 0)
    col = iota(shape, 1)
    block = col // plan.count
    group = block // plan.owners
    source = plan.peer(me, block % plan.owners, core ^ group)
    place = row % plan.expert_rows
    want = (row % plan.cap_rows + 1).astype(F32)
    same = (place // plan.cap_rows) == group * plan.owners + source
    hit = same & (slot == want)
    factor = jnp.sum(jnp.where(hit, part, 0.0), axis=1, keepdims=True)
    return jnp.where(hit, 1.0, 0.0).astype(BF16), factor


def weight_copies(plan, array, ref, sems):
    offset = first_expert(plan)[1]
    return [
        pltpu.make_async_copy(array.at[offset + e], ref.at[e], sems.at[e])
        for e in range(plan.mine)
    ]


def prepare_kernel(plan, x_hbm, routes_hbm, factors_hbm, gate_hbm, up_hbm, after, *refs):
    packed_ref, done_ref, own_ref = refs[:3]
    other_ref = refs[3] if plan.split > 1 else None
    gate_s, up_s, saved_sems, routes_ref, factors_ref, pack_sems = refs[plan.split + 2 :]
    done_ref[...] = jnp.zeros_like(done_ref)
    saved = [
        pltpu.make_async_copy(gate_hbm, gate_s, saved_sems.at[0]),
        pltpu.make_async_copy(up_hbm, up_s, saved_sems.at[1]),
    ]
    for copy in saved:
        copy.start()
    pack_body(
        plan, x_hbm, routes_hbm, factors_hbm, packed_ref, routes_ref, factors_ref, pack_sems
    )
    _, offset = first_expert(plan)
    shape = (plan.mine * plan.source_rows, gate_s.shape[0])
    row, col = iota(shape, 0), iota(shape, 1)
    slot = row % plan.cap_rows
    source = row % plan.source_rows // plan.cap_rows
    place = (source * plan.cap + slot) * plan.local + row // plan.source_rows
    place = jnp.where(slot < plan.cap, place, -plan.local)

    def pick(start, ref):
        table = jnp.where(col == place + start, 1.0, 0.0).astype(BF16)
        return dot(table, ref[...]).astype(BF16)

    for copy in saved:
        copy.wait()
    own_ref[0] = pick(offset, gate_s)
    own_ref[1] = pick(offset, up_s)
    if other_ref is not None:
        other_ref[0] = pick(plan.mine - offset, gate_s)
        other_ref[1] = pick(plan.mine - offset, up_s)


def prepare(plan, x, routes, factors, saved_gate, saved_up, after):
    flat = (plan.owners * plan.cap * plan.local, plan.hidden)

    def flatten(saved):
        return in_hbm(jnp.swapaxes(saved[0], 1, 2).reshape(flat))

    part = jax.ShapeDtypeStruct((2, plan.mine * plan.source_rows, plan.hidden), BF16)
    packed_shape = jax.ShapeDtypeStruct((plan.count, plan.sent), BF16)
    done_shape = jax.ShapeDtypeStruct((16, plan.sent), BF16)
    out_shape = [packed_shape, done_shape] + [part] * plan.split
    packed, done, *saved = pl.pallas_call(
        functools.partial(prepare_kernel, plan),
        out_shape=out_shape,
        in_specs=[hbm()] * 5 + [pl.BlockSpec(memory_space=pl.ANY)],
        out_specs=[vmem()] * len(out_shape),
        scratch_shapes=[
            pltpu.VMEM(flat, BF16),
            pltpu.VMEM(flat, BF16),
            pltpu.SemaphoreType.DMA((2,)),
            *pack_scratch(plan),
        ],
        compiler_params=pltpu.CompilerParams(vmem_limit_bytes=8 * MIB),
        cost_estimate=pl.CostEstimate(
            flops=0, bytes_accessed=plan.owners * plan.width * plan.sent, transcendentals=0
        ),
        name="prepare",
    )(
        in_hbm(x),
        in_hbm(routes.T),
        in_hbm(factors.T),
        flatten(saved_gate),
        flatten(saved_up),
        after,
    )
    return packed, saved, done


def fetch_kernel(plan, w_hbm, after, w_ref, done_ref, sems):
    copies = weight_copies(plan, w_hbm, w_ref, sems)
    for copy in copies:
        copy.start()
    done_ref[...] = jnp.zeros_like(done_ref)
    for copy in copies:
        copy.wait()


def fetch(plan, w, after):
    return pl.pallas_call(
        functools.partial(fetch_kernel, plan),
        out_shape=(
            pltpu.VMEM((plan.mine, plan.hidden, plan.width), BF16),
            jax.ShapeDtypeStruct((16, plan.sent), BF16),
        ),
        in_specs=[hbm(), pl.BlockSpec(memory_space=pl.ANY)],
        out_specs=(vmem(), vmem()),
        scratch_shapes=[pltpu.SemaphoreType.DMA((plan.mine,))],
        compiler_params=pltpu.CompilerParams(vmem_limit_bytes=MIB),
        cost_estimate=pl.CostEstimate(
            flops=0,
            bytes_accessed=2 * plan.mine * plan.hidden * plan.width * 2,
            transcendentals=0,
        ),
        name="fetch",
    )(in_hbm(w), after)


def arrived(plan, blocks, first):
    left, metas, rows = plan.cols, [], []
    for block in blocks:
        count = min(left, block.shape[0])
        metas.append(block[:count, plan.width :])
        rows.append(block[:count, : plan.width])
        left -= count
    table, factor = tables(plan, jnp.concatenate(metas, axis=0), first)
    return table, factor, jnp.concatenate(rows, axis=0)


class Queue:
    def __init__(self, copies, ahead):
        self.copies, self.ahead, self.started, self.taken = copies, ahead, 0, 0

    def fill(self):
        limit = min(self.taken + self.ahead, len(self.copies))
        while self.started < limit:
            self.copies[self.started].start()
            self.started += 1

    def take(self):
        self.fill()
        self.copies[self.taken].wait()
        self.taken += 1
        self.fill()


def forward_kernel(plan, count, *refs):
    blocks, refs = refs[:count], refs[count:]
    gate_ref, up_hbm, down_hbm, *refs = refs
    outs, (up_s, down_s, x_s, y_s, gate_s, hidden_s, sems) = refs[:-7], refs[-7:]
    first, _ = first_expert(plan)
    copies = weight_copies(plan, up_hbm, up_s, sems.at[0])
    copies += weight_copies(plan, down_hbm, down_s, sems.at[1])
    queue = Queue(copies, 3)
    queue.fill()
    table, factor, rows = arrived(plan, blocks, first)
    x_s[...] = dot(table, rows).astype(BF16)
    n = plan.expert_rows
    parts = [slice(e * n, (e + 1) * n) for e in range(plan.mine)]
    for e, part in enumerate(parts):
        gate_s[e] = dot_tb(x_s[part, :], gate_ref[e])
    up = None
    for e, part in enumerate(parts):
        queue.take()
        last, up = up, dot_tb(x_s[part, :], up_s[e])
        if e:
            gate = gate_s[e - 1]
            hidden_s[e - 1] = (gate / (1.0 + jnp.exp(-gate)) * last).astype(BF16)
    gate = gate_s[plan.mine - 1]
    hidden_s[plan.mine - 1] = (gate / (1.0 + jnp.exp(-gate)) * up).astype(BF16)
    for e, part in enumerate(parts):
        queue.take()
        out = dot(hidden_s[e], down_s[e])
        y_s[part, :] = (out * factor[part]).astype(BF16)
    put_rows(outs, slice(None), dot_ta(table, y_s[...]).astype(BF16))


def put_rows(outs, columns, rows):
    start = 0
    for out in outs:
        stop = start + out.shape[0]
        out[:, columns] = rows[start:stop, :]
        start = stop


def backward_kernel(plan, count, *refs):
    blocks, refs = refs[:count], refs[count:]
    saved_ref, other_ref, refs = refs[0], refs[plan.split - 1], refs[plan.split :]
    gate_ref, up_hbm, down_hbm, *refs = refs
    outs, (up_s, down_s, x_s, y_s, score_s, grads_s, sems) = refs[:-7], refs[-7:]
    first, _ = first_expert(plan)
    copies = weight_copies(plan, down_hbm, down_s, sems.at[0])
    copies += weight_copies(plan, up_hbm, up_s, sems.at[1])
    queue = Queue(copies, 2)
    queue.fill()
    table, factor, rows = arrived(plan, blocks, first)
    x_s[...] = dot(table, rows).astype(BF16)
    n, held = plan.expert_rows, plan.source_rows
    lane = iota((n, plan.meta), 1)
    parts = [slice(e * n, (e + 1) * n) for e in range(plan.mine)]

    def through_activation(e, grad):
        own = slice(e * held, (e + 1) * held)
        act, up = saved_ref[0, own, :], saved_ref[1, own, :]
        if plan.split > 1:
            act = jnp.concatenate([act, other_ref[0, own, :]], axis=0)
            up = jnp.concatenate([up, other_ref[1, own, :]], axis=0)
        act, up = act.astype(F32), up.astype(F32)
        sig = 1.0 / (1.0 + jnp.exp(-act))
        silu = act * sig
        score = jnp.sum(silu * up * grad, axis=1, keepdims=True)
        grads_s[0, e] = (grad * up * sig * (1.0 + act * (1.0 - sig))).astype(BF16)
        grads_s[1, e] = (grad * silu).astype(BF16)
        expert = first + e
        high = score.astype(BF16).astype(F32)
        middle = (score - high).astype(BF16).astype(F32)
        low = score - high - middle
        spread = jnp.where(lane == expert, high, 0.0)
        spread = jnp.where(lane == expert + plan.experts, middle, spread)
        spread = jnp.where(lane == expert + 2 * plan.experts, low, spread)
        score_s[parts[e], :] = spread.astype(BF16)

    grad = None
    for e, part in enumerate(parts):
        queue.take()
        last, grad = grad, dot_tb(x_s[part, :], down_s[e])
        if e:
            through_activation(e - 1, last)
    through_activation(plan.mine - 1, grad)
    for e, part in enumerate(parts):
        queue.take()
        result = dot(grads_s[0, e], gate_ref[e]) + dot(grads_s[1, e], up_s[e])
        y_s[part, :] = (result * factor[part]).astype(BF16)
    half, near = plan.half, outs[: len(outs) // 2]
    far = outs[len(outs) // 2 :]
    put_rows(near, slice(0, half), dot_ta(table, y_s[:, :half]).astype(BF16))
    rest = plan.width - half
    put_rows(far, slice(0, rest), dot_ta(table, y_s[:, half:]).astype(BF16))
    scores = dot_ta(table, score_s[...]).astype(BF16)
    put_rows(far, slice(rest, rest + plan.meta), scores)


def part_shapes(plan, width):
    block = jax.ShapeDtypeStruct((plan.count, width), BF16)
    other = jax.ShapeDtypeStruct((plan.owners * plan.count, width), BF16)
    return [block] * plan.owners + [other] * (plan.split - 1)


def expert_call(plan, kernel, name, inputs, gate, up_hbm, down_hbm, widths, scratch):
    shapes = [shape for width in widths for shape in part_shapes(plan, width)]
    weight = pltpu.VMEM((plan.mine, plan.hidden, plan.width), BF16)
    rows = pltpu.VMEM((plan.rows, plan.width), BF16)
    return pl.pallas_call(
        kernel,
        out_shape=shapes,
        in_specs=[vmem()] * (len(inputs) + 1) + [hbm()] * 2,
        out_specs=[vmem()] * len(shapes),
        scratch_shapes=[
            *[weight, weight, rows, rows],
            *scratch,
            pltpu.SemaphoreType.DMA((2, plan.mine)),
        ],
        compiler_params=pltpu.CompilerParams(vmem_limit_bytes=36 * MIB),
        cost_estimate=pl.CostEstimate(
            flops=2 * 3 * plan.mine * plan.expert_rows * plan.width * plan.hidden,
            bytes_accessed=2 * 2 * plan.mine * plan.width * plan.hidden,
            transcendentals=0,
        ),
        name=name,
    )(*inputs, in_vmem(gate), in_hbm(up_hbm), in_hbm(down_hbm))


def forward(plan, blocks, *weights):
    kernel = functools.partial(forward_kernel, plan, len(blocks))
    shape = (plan.mine, plan.expert_rows, plan.hidden)
    scratch = [pltpu.VMEM(shape, F32), pltpu.VMEM(shape, BF16)]
    return expert_call(plan, kernel, "forward", blocks, *weights, [plan.width], scratch)


def backward(plan, blocks, saved, *weights):
    kernel = functools.partial(backward_kernel, plan, len(blocks))
    scratch = [
        pltpu.VMEM((plan.rows, plan.meta), BF16),
        pltpu.VMEM((2, plan.mine, plan.expert_rows, plan.hidden), BF16),
    ]
    widths = [plan.half, plan.sent - plan.half]
    inputs = [*blocks, *saved]
    parts = expert_call(plan, kernel, "backward", inputs, *weights, widths, scratch)
    return parts[: len(parts) // 2], parts[len(parts) // 2 :]


def gather_group(plan, block):
    return [block] + [plan.over_expert(block, d) for d in range(1, plan.owners)]


def sum_pair(plan, parts):
    own = [[p] for p in parts[: plan.owners]]
    if plan.split > 1:
        other = plan.over_pair(parts[plan.owners])
        for d in range(plan.owners):
            own[d].append(other[d * plan.count : (d + 1) * plan.count])
    return own


def total(terms):
    return sum(t.astype(F32) for t in terms)


def scatter_group(plan, own):
    sent = [total(own[d]).astype(BF16) for d in range(1, plan.owners)]
    return own[0] + [plan.over_expert(x, d, True) for d, x in enumerate(sent, 1)]


def scatter_steps(plan, owns):
    if not plan.paired:
        return [scatter_group(plan, own) for own in owns]
    step = 1
    while step < plan.owners:
        away = [d for d in range(0, plan.owners, step) if d & step]
        for own in owns:
            sent = jnp.concatenate([total(own[d]).astype(BF16) for d in away])
            back = plan.over_expert(sent, step, True)
            for i, d in enumerate(away):
                own[d ^ step].append(back[i * plan.count : (i + 1) * plan.count])
        step *= 2
    return [own[0] for own in owns]


def finish_kernel(plan, count, *refs):
    parts, (routes_ref, out_hbm, score_hbm, out_s, score_s, sems) = refs[:count], refs[count:]
    half, rest = plan.half, plan.width - plan.half
    near = total([part[...] for part in parts[: count // 2]])
    far = total([part[...] for part in parts[count // 2 :]])
    out_s[:, :half] = near.astype(BF16)
    out_s[:, half:] = far[:, :rest].astype(BF16)
    out_copy = pltpu.make_async_copy(out_s, out_hbm, sems.at[0])
    out_copy.start()
    shape = (plan.meta, plan.meta)
    same = jnp.where(iota(shape, 0) == iota(shape, 1), 1.0, 0.0).astype(BF16)
    spread = dot_tb(same, far[:, rest:].astype(BF16))
    experts = plan.experts
    score = spread[:experts] + spread[experts : 2 * experts] + spread[2 * experts : 3 * experts]
    row = iota((experts, plan.count), 0)
    for k in range(plan.top):
        hit = row == routes_ref[k : k + 1, :]
        score_s[k : k + 1, :] = jnp.sum(jnp.where(hit, score, 0.0), axis=0, keepdims=True)
    score_copy = pltpu.make_async_copy(score_s, score_hbm, sems.at[1])
    score_copy.start()
    out_copy.wait()
    score_copy.wait()


def finish_back(plan, parts, routes):
    out, score = pl.pallas_call(
        functools.partial(finish_kernel, plan, len(parts)),
        out_shape=(
            jax.ShapeDtypeStruct((plan.count, plan.width), BF16),
            jax.ShapeDtypeStruct((plan.top, plan.count), F32),
        ),
        in_specs=[vmem()] * (len(parts) + 1),
        out_specs=(hbm(), hbm()),
        scratch_shapes=[
            pltpu.VMEM((plan.count, plan.width), BF16),
            pltpu.VMEM((plan.top, plan.count), F32),
            pltpu.SemaphoreType.DMA((2,)),
        ],
        compiler_params=pltpu.CompilerParams(vmem_limit_bytes=8 * MIB),
        name="finish",
    )(*parts, routes.T)
    return out, score.T


def body(
    tokens,
    routes,
    weights_fwd,
    cotangent,
    routes_back,
    weights_back,
    saved_gate,
    saved_up,
    w_gate,
    w_up,
    w_down,
):
    plan = Plan(tokens, routes, saved_gate, w_gate)
    packed = pack(plan, tokens, routes, weights_fwd)
    packed_back, saved, ready = prepare(
        plan, cotangent, routes_back, weights_back, saved_gate, saved_up, packed
    )
    gate_hbm, up_hbm = jnp.swapaxes(w_gate, 1, 2), jnp.swapaxes(w_up, 1, 2)
    if plan.paired and plan.owners > 1:
        blocks = [packed, plan.over_expert(packed, 1)]
        gate, done = fetch(plan, gate_hbm, blocks[1])
        step = 2
        while step < plan.owners:
            blocks.append(plan.over_expert(jnp.concatenate(blocks) + ready[:1], step))
            step *= 2
    else:
        blocks = gather_group(plan, packed)
        gate, done = fetch(plan, gate_hbm, packed)
    if plan.split > 1:
        blocks.append(plan.over_pair(jnp.concatenate(blocks) + done[:1]))
    blocks_back = gather_group(plan, packed_back)
    parts = forward(plan, blocks, gate, up_hbm, w_down)
    parts, blocks_back = lax.optimization_barrier((parts, blocks_back))
    if plan.split > 1:
        blocks_back = blocks_back + [plan.over_pair(jnp.concatenate(blocks_back))]
        saved[1] = plan.over_pair(saved[1])
    terms = scatter_group(plan, sum_pair(plan, parts))
    parts_back = backward(plan, blocks_back, saved, gate, up_hbm, w_down)
    parts_back, terms = lax.optimization_barrier((parts_back, terms))
    mixed = total(terms).astype(BF16)
    near, far = scatter_steps(plan, [sum_pair(plan, parts) for parts in parts_back])
    input_grad, weight_grad = finish_back(plan, near + far, routes_back)
    return (mixed, input_grad, weight_grad)


def solution(mesh):
    spec = P(("dp", "expert"), None)
    saved = P("dp", None, "expert", None, None)
    weight = P("expert", None, None)
    return jax.shard_map(
        body,
        mesh=mesh,
        in_specs=(spec,) * 6 + (saved,) * 2 + (weight,) * 3,
        out_specs=(spec,) * 3,
        check_vma=False,
    )
```

```python
import functools
import jax
import jax.numpy as jnp
from jax import lax
from jax.experimental import pallas as pl
from jax.experimental.pallas import tpu as pltpu
from jax.sharding import PartitionSpec as P

F32 = jnp.float32
BF16 = jnp.bfloat16
LANES = 128
MIB = 1 << 20


def round_up(value, unit):
    return -(-value // unit) * unit


def dot(a, b):
    return jnp.dot(a, b, preferred_element_type=F32)


def dot_tb(a, b):
    return lax.dot_general(a, b, (((1,), (1,)), ((), ())), preferred_element_type=F32)


def dot_ta(a, b):
    return lax.dot_general(a, b, (((0,), (0,)), ((), ())), preferred_element_type=F32)


def iota(shape, dim):
    return lax.broadcasted_iota(jnp.int32, shape, dim)


def vmem():
    return pl.BlockSpec(memory_space=pltpu.VMEM)


def hbm():
    return pl.BlockSpec(memory_space=pltpu.HBM)


def in_vmem(x):
    return pltpu.with_memory_space_constraint(x, pltpu.VMEM)


def in_hbm(x):
    return pltpu.with_memory_space_constraint(x, pltpu.HBM)


class Plan:
    def __init__(self, tokens, routes, saved_gate, w_gate):
        self.owners = lax.axis_size("expert")
        self.groups = lax.axis_size("dp")
        self.count, self.width = tokens.shape
        self.top = routes.shape[1]
        self.local = w_gate.shape[0]
        self.hidden = w_gate.shape[2]
        self.experts = self.owners * self.local
        self.cap = saved_gate.shape[3]
        self.cap_rows = round_up(self.cap, 8)
        self.split = 2 if self.groups % 2 == 0 and self.local % 2 == 0 else 1
        self.mine = self.local // self.split
        self.meta = round_up(3 * self.experts, LANES)
        self.blocks = self.split * self.owners
        self.source_rows = self.owners * self.cap_rows
        self.expert_rows = self.split * self.source_rows
        self.paired = self.owners & (self.owners - 1) == 0
        self.sent = self.width + self.meta
        self.half = round_up(self.width // 2, LANES)
        self.kept = min(self.mine, 2)
        self.rows = self.mine * self.expert_rows
        self.cols = self.blocks * self.count

    def peer(self, index, step, core):
        bits = self.owners.bit_length() - 1
        if self.owners != 1 << bits:
            return (index + step) % self.owners
        turned = sum(((step >> i) & 1) << (bits - 1 - i) for i in range(bits))
        return index ^ (step + (turned - step) * core)

    def over_expert(self, x, step, back=False):
        pairs = []
        for group in range(self.groups):
            for i in range(self.owners):
                near = group * self.owners + i
                far = self.peer(i, step, group % self.split) + group * self.owners
                pairs.append((near, far) if back else (far, near))
        return lax.ppermute(x, ("dp", "expert"), pairs)

    def over_pair(self, x):
        return lax.ppermute(x, "dp", [(i, i ^ 1) for i in range(self.groups)])


def pack_body(plan, sources, near_ref, far_ref, routes_ref, factors_ref, sems):
    x_hbm, routes_hbm, factors_hbm = sources
    experts, count, half = plan.experts, plan.count, plan.half
    rest = plan.width - half
    rows = [
        pltpu.make_async_copy(x_hbm.at[:, :half], near_ref, sems.at[0]),
        pltpu.make_async_copy(x_hbm.at[:, half:], far_ref.at[:, :rest], sems.at[3]),
    ]
    small = [
        pltpu.make_async_copy(routes_hbm, routes_ref, sems.at[1]),
        pltpu.make_async_copy(factors_hbm, factors_ref, sems.at[2]),
    ]
    for copy in (*small, *rows):
        copy.start()
    for copy in small:
        copy.wait()
    lane = iota((plan.meta, count), 0)
    chosen = jnp.zeros((plan.meta, count), F32)
    parts = jnp.zeros((plan.meta, count), F32)
    for k in range(plan.top):
        route = routes_ref[k : k + 1, :]
        factor = factors_ref[k : k + 1, :]
        high = factor.astype(BF16).astype(F32)
        low = factor - high
        chosen = chosen + jnp.where(lane == route, 1.0, 0.0)
        parts = parts + jnp.where(lane == route + experts, high, 0.0)
        parts = parts + jnp.where(lane == route + 2 * experts, low, 0.0)
    earlier = jnp.where(iota((count, count), 0) < iota((count, count), 1), 1.0, 0.0)
    before = dot(chosen.astype(BF16), earlier.astype(BF16))
    facts = (chosen * (before + 1.0) + parts).astype(BF16)
    shape = (plan.meta, plan.meta)
    same = jnp.where(iota(shape, 0) == iota(shape, 1), 1.0, 0.0).astype(BF16)
    far_ref[:, rest:] = dot_ta(facts, same).astype(BF16)
    for copy in rows:
        copy.wait()


def pack_scratch(plan):
    return [
        pltpu.VMEM((plan.top, plan.count), jnp.int32),
        pltpu.VMEM((plan.top, plan.count), F32),
        pltpu.SemaphoreType.DMA((4,)),
    ]


def pack_kernel(plan, *refs):
    pack_body(plan, refs[:3], *refs[3:])


def pack(plan, x, routes, factors):
    return pl.pallas_call(
        functools.partial(pack_kernel, plan),
        out_shape=(
            jax.ShapeDtypeStruct((plan.count, plan.half), BF16),
            jax.ShapeDtypeStruct((plan.count, plan.sent - plan.half), BF16),
        ),
        in_specs=[hbm()] * 3,
        out_specs=(vmem(), vmem()),
        scratch_shapes=pack_scratch(plan),
        compiler_params=pltpu.CompilerParams(vmem_limit_bytes=4 * MIB),
        name="pack",
    )(in_hbm(x), in_hbm(routes.T), in_hbm(factors.T))


def first_expert(plan):
    core = lax.rem(lax.axis_index("dp"), plan.split)
    return lax.axis_index("expert") * plan.local + core * plan.mine, core * plan.mine


def tables(plan, meta, first):
    me = lax.axis_index("expert")
    core = lax.rem(lax.axis_index("dp"), plan.split)
    row = iota((plan.rows, plan.meta), 0)
    lane = iota((plan.rows, plan.meta), 1)
    expert = first + row // plan.expert_rows
    pick_slot = jnp.where(lane == expert, 1.0, 0.0).astype(BF16)
    pick_part = jnp.where(
        (lane == expert + plan.experts) | (lane == expert + 2 * plan.experts), 1.0, 0.0
    ).astype(BF16)
    slot = dot_tb(pick_slot, meta)
    part = dot_tb(pick_part, meta)
    shape = (plan.rows, plan.cols)
    row = iota(shape, 0)
    col = iota(shape, 1)
    block = col // plan.count
    group = block // plan.owners
    source = plan.peer(me, block % plan.owners, core ^ group)
    place = row % plan.expert_rows
    want = (row % plan.cap_rows + 1).astype(F32)
    same = (place // plan.cap_rows) == group * plan.owners + source
    hit = same & (slot == want)
    factor = jnp.sum(jnp.where(hit, part, 0.0), axis=1, keepdims=True)
    return jnp.where(hit, 1.0, 0.0).astype(BF16), factor


def weight_copies(plan, array, slots, sems):
    offset = first_expert(plan)[1]
    return [
        pltpu.make_async_copy(array.at[offset + e], slot, sems.at[e])
        for e, slot in enumerate(slots)
    ]


def weight_slots(plan, *refs):
    return [ref.at[e] for ref in refs for e in range(ref.shape[0])][: plan.mine]


def prepare_kernel(plan, x_hbm, routes_hbm, factors_hbm, gate_hbm, up_hbm, after, *refs):
    packed_ref, done_ref, own_ref = refs[:3]
    other_ref = refs[3] if plan.split > 1 else None
    gate_s, up_s, saved_sems, routes_ref, factors_ref, pack_sems = refs[plan.split + 2 :]
    done_ref[...] = jnp.zeros_like(done_ref)
    saved = [
        pltpu.make_async_copy(gate_hbm, gate_s, saved_sems.at[0]),
        pltpu.make_async_copy(up_hbm, up_s, saved_sems.at[1]),
    ]
    for copy in saved:
        copy.start()
    halves = packed_ref.at[:, : plan.half], packed_ref.at[:, plan.half :]
    sources = x_hbm, routes_hbm, factors_hbm
    pack_body(plan, sources, *halves, routes_ref, factors_ref, pack_sems)
    _, offset = first_expert(plan)
    shape = (plan.mine * plan.source_rows, gate_s.shape[0])
    row, col = iota(shape, 0), iota(shape, 1)
    slot = row % plan.cap_rows
    source = row % plan.source_rows // plan.cap_rows
    place = (source * plan.cap + slot) * plan.local + row // plan.source_rows
    place = jnp.where(slot < plan.cap, place, -plan.local)

    def pick(start, ref):
        table = jnp.where(col == place + start, 1.0, 0.0).astype(BF16)
        return dot(table, ref[...]).astype(BF16)

    for copy in saved:
        copy.wait()
    own_ref[0] = pick(offset, gate_s)
    own_ref[1] = pick(offset, up_s)
    if other_ref is not None:
        other_ref[0] = pick(plan.mine - offset, gate_s)
        other_ref[1] = pick(plan.mine - offset, up_s)


def prepare(plan, x, routes, factors, saved_gate, saved_up, after):
    flat = (plan.owners * plan.cap * plan.local, plan.hidden)

    def flatten(saved):
        return in_hbm(jnp.swapaxes(saved[0], 1, 2).reshape(flat))

    part = jax.ShapeDtypeStruct((2, plan.mine * plan.source_rows, plan.hidden), BF16)
    packed_shape = jax.ShapeDtypeStruct((plan.count, plan.sent), BF16)
    done_shape = jax.ShapeDtypeStruct((16, plan.sent), BF16)
    out_shape = [packed_shape, done_shape] + [part] * plan.split
    packed, done, *saved = pl.pallas_call(
        functools.partial(prepare_kernel, plan),
        out_shape=out_shape,
        in_specs=[hbm()] * 5 + [pl.BlockSpec(memory_space=pl.ANY)],
        out_specs=[vmem()] * len(out_shape),
        scratch_shapes=[
            pltpu.VMEM(flat, BF16),
            pltpu.VMEM(flat, BF16),
            pltpu.SemaphoreType.DMA((2,)),
            *pack_scratch(plan),
        ],
        compiler_params=pltpu.CompilerParams(vmem_limit_bytes=8 * MIB),
        cost_estimate=pl.CostEstimate(
            flops=0, bytes_accessed=plan.owners * plan.width * plan.sent, transcendentals=0
        ),
        name="prepare",
    )(
        in_hbm(x),
        in_hbm(routes.T),
        in_hbm(factors.T),
        flatten(saved_gate),
        flatten(saved_up),
        after,
    )
    return packed, saved, done


def fetch_kernel(plan, w_hbm, after, also_after, w_ref, done_ref, sems):
    copies = weight_copies(plan, w_hbm, weight_slots(plan, w_ref), sems)
    for copy in copies:
        copy.start()
    done_ref[...] = jnp.zeros_like(done_ref)
    for copy in copies:
        copy.wait()


def fetch(plan, w, after, also_after):
    return pl.pallas_call(
        functools.partial(fetch_kernel, plan),
        out_shape=(
            pltpu.VMEM((plan.mine, plan.hidden, plan.width), BF16),
            jax.ShapeDtypeStruct((16, plan.sent), BF16),
        ),
        in_specs=[hbm()] + [pl.BlockSpec(memory_space=pl.ANY)] * 2,
        out_specs=(vmem(), vmem()),
        scratch_shapes=[pltpu.SemaphoreType.DMA((plan.mine,))],
        compiler_params=pltpu.CompilerParams(vmem_limit_bytes=MIB),
        cost_estimate=pl.CostEstimate(
            flops=0,
            bytes_accessed=2 * plan.mine * plan.hidden * plan.width * 2,
            transcendentals=0,
        ),
        name="fetch",
    )(in_hbm(w), after, also_after)


def arrived(plan, nears, fars, first, x_s):
    half, rest = plan.half, plan.width - plan.half
    metas = jnp.concatenate([far[:, rest:] for far in fars], axis=0)
    table, factor = tables(plan, metas, first)
    near = jnp.concatenate([near[...] for near in nears], axis=0)
    x_s[:, :half] = dot(table, near).astype(BF16)
    far = jnp.concatenate([far[:, :rest] for far in fars], axis=0)
    x_s[:, half:] = dot(table, far).astype(BF16)
    return table, factor


class Queue:
    def __init__(self, copies, ahead):
        self.copies, self.ahead, self.started, self.taken = copies, ahead, 0, 0

    def fill(self):
        limit = min(self.taken + self.ahead, len(self.copies))
        while self.started < limit:
            self.copies[self.started].start()
            self.started += 1

    def take(self):
        self.fill()
        self.copies[self.taken].wait()
        self.taken += 1
        self.fill()


def forward_kernel(plan, count, *refs):
    blocks, refs = refs[:count], refs[count:]
    gate_ref, up_hbm, down_hbm, *refs = refs
    outs, (kept_ref, up_s, down_s, x_s, y_s, gate_s, hidden_s, sems) = refs[:-8], refs[-8:]
    first, _ = first_expert(plan)
    downs = weight_slots(plan, kept_ref, down_s)
    copies = weight_copies(plan, up_hbm, weight_slots(plan, up_s), sems.at[0])
    copies += weight_copies(plan, down_hbm, downs, sems.at[1])
    queue = Queue(copies, 3)
    queue.fill()
    nears, fars = blocks[: count // 2], blocks[count // 2 :]
    table, factor = arrived(plan, nears, fars, first, x_s)
    n = plan.expert_rows
    parts = [slice(e * n, (e + 1) * n) for e in range(plan.mine)]
    for e, part in enumerate(parts):
        gate_s[e] = dot_tb(x_s[part, :], gate_ref[e])
    up = None
    for e, part in enumerate(parts):
        queue.take()
        last, up = up, dot_tb(x_s[part, :], up_s[e])
        if e:
            gate = gate_s[e - 1]
            hidden_s[e - 1] = (gate / (1.0 + jnp.exp(-gate)) * last).astype(BF16)
    gate = gate_s[plan.mine - 1]
    hidden_s[plan.mine - 1] = (gate / (1.0 + jnp.exp(-gate)) * up).astype(BF16)
    for e, part in enumerate(parts):
        queue.take()
        out = dot(hidden_s[e], downs[e][...])
        y_s[part, :] = (out * factor[part]).astype(BF16)
    put_rows(outs, slice(None), dot_ta(table, y_s[...]).astype(BF16))


def put_rows(outs, columns, rows):
    start = 0
    for out in outs:
        stop = start + out.shape[0]
        out[:, columns] = rows[start:stop, :]
        start = stop


def backward_kernel(plan, count, *refs):
    blocks, refs = refs[:count], refs[count:]
    saved_ref, other_ref, refs = refs[0], refs[plan.split - 1], refs[plan.split :]
    gate_ref, kept_ref, up_hbm, down_hbm, *refs = refs
    outs, (up_s, down_s, x_s, y_s, score_s, grads_s, sems) = refs[:-7], refs[-7:]
    first, _ = first_expert(plan)
    downs = weight_slots(plan, kept_ref, down_s)
    copies = weight_copies(plan, down_hbm, downs, sems.at[0])[plan.kept :]
    copies += weight_copies(plan, up_hbm, weight_slots(plan, up_s), sems.at[1])
    queue = Queue(copies, 3)
    queue.fill()
    nears = [block.at[:, : plan.half] for block in blocks]
    fars = [block.at[:, plan.half :] for block in blocks]
    table, factor = arrived(plan, nears, fars, first, x_s)
    n, held = plan.expert_rows, plan.source_rows
    lane = iota((n, plan.meta), 1)
    parts = [slice(e * n, (e + 1) * n) for e in range(plan.mine)]

    def through_activation(e, grad):
        own = slice(e * held, (e + 1) * held)
        act, up = saved_ref[0, own, :], saved_ref[1, own, :]
        if plan.split > 1:
            act = jnp.concatenate([act, other_ref[0, own, :]], axis=0)
            up = jnp.concatenate([up, other_ref[1, own, :]], axis=0)
        act, up = act.astype(F32), up.astype(F32)
        sig = 1.0 / (1.0 + jnp.exp(-act))
        silu = act * sig
        score = jnp.sum(silu * up * grad, axis=1, keepdims=True)
        grads_s[0, e] = (grad * up * sig * (1.0 + act * (1.0 - sig))).astype(BF16)
        grads_s[1, e] = (grad * silu).astype(BF16)
        expert = first + e
        high = score.astype(BF16).astype(F32)
        middle = (score - high).astype(BF16).astype(F32)
        low = score - high - middle
        spread = jnp.where(lane == expert, high, 0.0)
        spread = jnp.where(lane == expert + plan.experts, middle, spread)
        spread = jnp.where(lane == expert + 2 * plan.experts, low, spread)
        score_s[parts[e], :] = spread.astype(BF16)

    grad = None
    for e, part in enumerate(parts):
        if e >= plan.kept:
            queue.take()
        last, grad = grad, dot_tb(x_s[part, :], downs[e][...])
        if e:
            through_activation(e - 1, last)
    through_activation(plan.mine - 1, grad)
    for e, part in enumerate(parts):
        queue.take()
        result = dot(grads_s[0, e], gate_ref[e]) + dot(grads_s[1, e], up_s[e])
        y_s[part, :] = (result * factor[part]).astype(BF16)
    half, near = plan.half, outs[: len(outs) // 2]
    far = outs[len(outs) // 2 :]
    put_rows(near, slice(0, half), dot_ta(table, y_s[:, :half]).astype(BF16))
    rest = plan.width - half
    put_rows(far, slice(0, rest), dot_ta(table, y_s[:, half:]).astype(BF16))
    scores = dot_ta(table, score_s[...]).astype(BF16)
    put_rows(far, slice(rest, rest + plan.meta), scores)


def part_shapes(plan, width):
    block = jax.ShapeDtypeStruct((plan.count, width), BF16)
    other = jax.ShapeDtypeStruct((plan.owners * plan.count, width), BF16)
    return [block] * plan.owners + [other] * (plan.split - 1)


def expert_call(plan, kernel, name, inputs, up_hbm, down_hbm, shapes, scratch):
    def weight(count):
        return pltpu.VMEM((count, plan.hidden, plan.width), BF16)

    rows = pltpu.VMEM((plan.rows, plan.width), BF16)
    return pl.pallas_call(
        kernel,
        out_shape=shapes,
        in_specs=[vmem()] * len(inputs) + [hbm()] * 2,
        out_specs=[vmem()] * len(shapes),
        scratch_shapes=[
            *[weight(plan.mine), weight(max(plan.mine - plan.kept, 1)), rows, rows],
            *scratch,
            pltpu.SemaphoreType.DMA((2, plan.mine)),
        ],
        compiler_params=pltpu.CompilerParams(vmem_limit_bytes=31 * MIB),
        cost_estimate=pl.CostEstimate(
            flops=2 * 3 * plan.mine * plan.expert_rows * plan.width * plan.hidden,
            bytes_accessed=2 * 2 * plan.mine * plan.width * plan.hidden,
            transcendentals=0,
        ),
        name=name,
    )(*inputs, in_hbm(up_hbm), in_hbm(down_hbm))


def forward(plan, nears, fars, gate, up_hbm, down_hbm):
    kernel = functools.partial(forward_kernel, plan, 2 * len(nears))
    shape = (plan.mine, plan.expert_rows, plan.hidden)
    scratch = [pltpu.VMEM(shape, F32), pltpu.VMEM(shape, BF16)]
    kept = pltpu.VMEM((plan.kept, plan.hidden, plan.width), BF16)
    shapes = part_shapes(plan, plan.width) + [kept]
    inputs = [*nears, *fars, in_vmem(gate)]
    *parts, kept = expert_call(
        plan, kernel, "forward", inputs, up_hbm, down_hbm, shapes, scratch
    )
    return parts, kept


def backward(plan, blocks, saved, gate, kept, up_hbm, down_hbm):
    kernel = functools.partial(backward_kernel, plan, len(blocks))
    scratch = [
        pltpu.VMEM((plan.rows, plan.meta), BF16),
        pltpu.VMEM((2, plan.mine, plan.expert_rows, plan.hidden), BF16),
    ]
    shapes = part_shapes(plan, plan.half) + part_shapes(plan, plan.sent - plan.half)
    inputs = [*blocks, *saved, in_vmem(gate), in_vmem(kept)]
    parts = expert_call(
        plan, kernel, "backward", inputs, up_hbm, down_hbm, shapes, scratch
    )
    return parts[: len(parts) // 2], parts[len(parts) // 2 :]


def gather_group(plan, block):
    return [block] + [plan.over_expert(block, d) for d in range(1, plan.owners)]


def sum_pair(plan, parts):
    own = [[p] for p in parts[: plan.owners]]
    if plan.split > 1:
        other = plan.over_pair(parts[plan.owners])
        for d in range(plan.owners):
            own[d].append(other[d * plan.count : (d + 1) * plan.count])
    return own


def total(terms):
    return sum(t.astype(F32) for t in terms)


def scatter_group(plan, own):
    sent = [total(own[d]).astype(BF16) for d in range(1, plan.owners)]
    return own[0] + [plan.over_expert(x, d, True) for d, x in enumerate(sent, 1)]


def scatter_steps(plan, owns):
    if not plan.paired:
        return [scatter_group(plan, own) for own in owns]
    step = 1
    while step < plan.owners:
        away = [d for d in range(0, plan.owners, step) if d & step]
        for own in owns:
            sent = jnp.concatenate([total(own[d]).astype(BF16) for d in away])
            back = plan.over_expert(sent, step, True)
            for i, d in enumerate(away):
                own[d ^ step].append(back[i * plan.count : (i + 1) * plan.count])
        step *= 2
    return [own[0] for own in owns]


def finish_kernel(plan, count, *refs):
    parts, (routes_ref, out_hbm, score_hbm, out_s, score_s, sems) = refs[:count], refs[count:]
    half, rest = plan.half, plan.width - plan.half
    near = total([part[...] for part in parts[: count // 2]])
    far = total([part[...] for part in parts[count // 2 :]])
    out_s[:, :half] = near.astype(BF16)
    out_s[:, half:] = far[:, :rest].astype(BF16)
    out_copy = pltpu.make_async_copy(out_s, out_hbm, sems.at[0])
    out_copy.start()
    shape = (plan.meta, plan.meta)
    same = jnp.where(iota(shape, 0) == iota(shape, 1), 1.0, 0.0).astype(BF16)
    spread = dot_tb(same, far[:, rest:].astype(BF16))
    experts = plan.experts
    score = spread[:experts] + spread[experts : 2 * experts] + spread[2 * experts : 3 * experts]
    row = iota((experts, plan.count), 0)
    for k in range(plan.top):
        hit = row == routes_ref[k : k + 1, :]
        score_s[k : k + 1, :] = jnp.sum(jnp.where(hit, score, 0.0), axis=0, keepdims=True)
    score_copy = pltpu.make_async_copy(score_s, score_hbm, sems.at[1])
    score_copy.start()
    out_copy.wait()
    score_copy.wait()


def finish_back(plan, parts, routes):
    out, score = pl.pallas_call(
        functools.partial(finish_kernel, plan, len(parts)),
        out_shape=(
            jax.ShapeDtypeStruct((plan.count, plan.width), BF16),
            jax.ShapeDtypeStruct((plan.top, plan.count), F32),
        ),
        in_specs=[vmem()] * (len(parts) + 1),
        out_specs=(hbm(), hbm()),
        scratch_shapes=[
            pltpu.VMEM((plan.count, plan.width), BF16),
            pltpu.VMEM((plan.top, plan.count), F32),
            pltpu.SemaphoreType.DMA((2,)),
        ],
        compiler_params=pltpu.CompilerParams(vmem_limit_bytes=8 * MIB),
        name="finish",
    )(*parts, routes.T)
    return out, score.T


def body(
    tokens,
    routes,
    weights_fwd,
    cotangent,
    routes_back,
    weights_back,
    saved_gate,
    saved_up,
    w_gate,
    w_up,
    w_down,
):
    plan = Plan(tokens, routes, saved_gate, w_gate)
    near, far = pack(plan, tokens, routes, weights_fwd)
    packed_back, saved, ready = prepare(
        plan, cotangent, routes_back, weights_back, saved_gate, saved_up, far
    )
    gate_hbm, up_hbm = jnp.swapaxes(w_gate, 1, 2), jnp.swapaxes(w_up, 1, 2)
    if plan.paired and plan.owners > 1:
        fars = [far, plan.over_expert(far, 1)]
        nears = [near, plan.over_expert(near + ready[:1, : plan.half], 1)]
        gate, done = fetch(plan, gate_hbm, nears[1], fars[1])
        step = 2
        while step < plan.owners:
            fars.append(plan.over_expert(jnp.concatenate(fars), step))
            nears.append(plan.over_expert(jnp.concatenate(nears), step))
            step *= 2
    else:
        nears, fars = gather_group(plan, near), gather_group(plan, far)
        gate, done = fetch(plan, gate_hbm, near, far)
    if plan.split > 1:
        nears.append(plan.over_pair(jnp.concatenate(nears) + done[:1, : plan.half]))
        fars.append(plan.over_pair(jnp.concatenate(fars)))
    blocks_back = gather_group(plan, packed_back)
    parts, kept = forward(plan, nears, fars, gate, up_hbm, w_down)
    parts, blocks_back = lax.optimization_barrier((parts, blocks_back))
    if plan.split > 1:
        blocks_back = blocks_back + [plan.over_pair(jnp.concatenate(blocks_back))]
        saved[1] = plan.over_pair(saved[1])
    terms = scatter_group(plan, sum_pair(plan, parts))
    parts_back = backward(plan, blocks_back, saved, gate, kept, up_hbm, w_down)
    parts_back, terms = lax.optimization_barrier((parts_back, terms))
    mixed = total(terms).astype(BF16)
    near, far = scatter_steps(plan, [sum_pair(plan, parts) for parts in parts_back])
    input_grad, weight_grad = finish_back(plan, near + far, routes_back)
    return (mixed, input_grad, weight_grad)


def solution(mesh):
    spec = P(("dp", "expert"), None)
    saved = P("dp", None, "expert", None, None)
    weight = P("expert", None, None)
    return jax.shard_map(
        body,
        mesh=mesh,
        in_specs=(spec,) * 6 + (saved,) * 2 + (weight,) * 3,
        out_specs=(spec,) * 3,
        check_vma=False,
    )
```

```python
import functools
import jax
import jax.numpy as jnp
from jax import lax
from jax.experimental import pallas as pl
from jax.experimental.pallas import tpu as pltpu
from jax.sharding import PartitionSpec as P

F32 = jnp.float32
BF16 = jnp.bfloat16
LANES = 128
MIB = 1 << 20


def round_up(value, unit):
    return -(-value // unit) * unit


def dot(a, b):
    return jnp.dot(a, b, preferred_element_type=F32)


def dot_tb(a, b):
    return lax.dot_general(a, b, (((1,), (1,)), ((), ())), preferred_element_type=F32)


def dot_ta(a, b):
    return lax.dot_general(a, b, (((0,), (0,)), ((), ())), preferred_element_type=F32)


def iota(shape, dim):
    return lax.broadcasted_iota(jnp.int32, shape, dim)


def vmem():
    return pl.BlockSpec(memory_space=pltpu.VMEM)


def hbm():
    return pl.BlockSpec(memory_space=pltpu.HBM)


def in_vmem(x):
    return pltpu.with_memory_space_constraint(x, pltpu.VMEM)


def in_hbm(x):
    return pltpu.with_memory_space_constraint(x, pltpu.HBM)


class Plan:
    def __init__(self, tokens, routes, saved_gate, w_gate):
        self.owners = lax.axis_size("expert")
        self.groups = lax.axis_size("dp")
        self.count, self.width = tokens.shape
        self.top = routes.shape[1]
        self.local = w_gate.shape[0]
        self.hidden = w_gate.shape[2]
        self.experts = self.owners * self.local
        self.cap = saved_gate.shape[3]
        self.cap_rows = round_up(self.cap, 8)
        self.split = 2 if self.groups % 2 == 0 and self.local % 2 == 0 else 1
        self.mine = self.local // self.split
        self.meta = round_up(3 * self.experts, LANES)
        self.blocks = self.split * self.owners
        self.source_rows = self.owners * self.cap_rows
        self.expert_rows = self.split * self.source_rows
        self.paired = self.owners & (self.owners - 1) == 0
        self.sent = self.width + self.meta
        self.half = round_up(self.width // 2, LANES)
        self.kept = min(self.mine, 2)
        self.rows = self.mine * self.expert_rows
        self.cols = self.blocks * self.count

    def peer(self, index, step, core):
        bits = self.owners.bit_length() - 1
        if self.owners != 1 << bits:
            return (index + step) % self.owners
        turned = sum(((step >> i) & 1) << (bits - 1 - i) for i in range(bits))
        return index ^ (step + (turned - step) * core)

    def over_expert(self, x, step, back=False):
        pairs = []
        for group in range(self.groups):
            for i in range(self.owners):
                near = group * self.owners + i
                far = self.peer(i, step, group % self.split) + group * self.owners
                pairs.append((near, far) if back else (far, near))
        return lax.ppermute(x, ("dp", "expert"), pairs)

    def over_pair(self, x):
        return lax.ppermute(x, "dp", [(i, i ^ 1) for i in range(self.groups)])


def pack_body(plan, sources, out_ref, routes_ref, factors_ref, sems):
    x_hbm, routes_hbm, factors_hbm = sources
    experts, count = plan.experts, plan.count
    rows = pltpu.make_async_copy(x_hbm, out_ref.at[:, : plan.width], sems.at[0])
    small = [
        pltpu.make_async_copy(routes_hbm, routes_ref, sems.at[1]),
        pltpu.make_async_copy(factors_hbm, factors_ref, sems.at[2]),
    ]
    for copy in (*small, rows):
        copy.start()
    for copy in small:
        copy.wait()
    lane = iota((plan.meta, count), 0)
    chosen = jnp.zeros((plan.meta, count), F32)
    parts = jnp.zeros((plan.meta, count), F32)
    for k in range(plan.top):
        route = routes_ref[k : k + 1, :]
        factor = factors_ref[k : k + 1, :]
        high = factor.astype(BF16).astype(F32)
        low = factor - high
        chosen = chosen + jnp.where(lane == route, 1.0, 0.0)
        parts = parts + jnp.where(lane == route + experts, high, 0.0)
        parts = parts + jnp.where(lane == route + 2 * experts, low, 0.0)
    earlier = jnp.where(iota((count, count), 0) < iota((count, count), 1), 1.0, 0.0)
    before = dot(chosen.astype(BF16), earlier.astype(BF16))
    facts = (chosen * (before + 1.0) + parts).astype(BF16)
    shape = (plan.meta, plan.meta)
    same = jnp.where(iota(shape, 0) == iota(shape, 1), 1.0, 0.0).astype(BF16)
    out_ref[:, plan.width :] = dot_ta(facts, same).astype(BF16)
    rows.wait()


def pack_scratch(plan):
    return [
        pltpu.VMEM((plan.top, plan.count), jnp.int32),
        pltpu.VMEM((plan.top, plan.count), F32),
        pltpu.SemaphoreType.DMA((3,)),
    ]


def pack_kernel(plan, *refs):
    pack_body(plan, refs[:3], *refs[3:])


def pack(plan, x, routes, factors):
    return pl.pallas_call(
        functools.partial(pack_kernel, plan),
        out_shape=jax.ShapeDtypeStruct((plan.count, plan.sent), BF16),
        in_specs=[hbm()] * 3,
        out_specs=vmem(),
        scratch_shapes=pack_scratch(plan),
        compiler_params=pltpu.CompilerParams(vmem_limit_bytes=4 * MIB),
        name="pack",
    )(in_hbm(x), in_hbm(routes.T), in_hbm(factors.T))


def first_expert(plan):
    core = lax.rem(lax.axis_index("dp"), plan.split)
    return lax.axis_index("expert") * plan.local + core * plan.mine, core * plan.mine


def tables(plan, meta, first):
    me = lax.axis_index("expert")
    core = lax.rem(lax.axis_index("dp"), plan.split)
    row = iota((plan.rows, 1), 0)
    place = row % plan.expert_rows
    expert = first + row // plan.expert_rows
    wanted_slot = (row % plan.cap_rows + 1).astype(F32)
    wanted_block = place // plan.cap_rows
    lane = iota((1, plan.meta), 1)
    pick_slot = jnp.where(lane == expert, 1.0, 0.0).astype(BF16)
    pick_part = (lane == expert + plan.experts) | (lane == expert + 2 * plan.experts)
    slot = dot_tb(pick_slot, meta)
    part = dot_tb(jnp.where(pick_part, 1.0, 0.0).astype(BF16), meta)
    block = iota((1, plan.cols), 1) // plan.count
    group = block // plan.owners
    source = plan.peer(me, block % plan.owners, core ^ group)
    hit = (wanted_block == group * plan.owners + source) & (slot == wanted_slot)
    factor = jnp.sum(jnp.where(hit, part, 0.0), axis=1, keepdims=True)
    return jnp.where(hit, 1.0, 0.0).astype(BF16), factor


def weight_copies(plan, array, slots, sems):
    offset = first_expert(plan)[1]
    return [
        pltpu.make_async_copy(array.at[offset + e], slot, sems.at[e])
        for e, slot in enumerate(slots)
    ]


def weight_slots(plan, *refs):
    return [ref.at[e] for ref in refs for e in range(ref.shape[0])][: plan.mine]


def prepare_kernel(plan, x_hbm, routes_hbm, factors_hbm, gate_hbm, up_hbm, after, *refs):
    packed_ref, done_ref, own_ref = refs[:3]
    other_ref = refs[3] if plan.split > 1 else None
    gate_s, up_s, saved_sems, routes_ref, factors_ref, pack_sems = refs[plan.split + 2 :]
    done_ref[...] = jnp.zeros_like(done_ref)
    saved = [
        pltpu.make_async_copy(gate_hbm, gate_s, saved_sems.at[0]),
        pltpu.make_async_copy(up_hbm, up_s, saved_sems.at[1]),
    ]
    for copy in saved:
        copy.start()
    sources = x_hbm, routes_hbm, factors_hbm
    pack_body(plan, sources, packed_ref, routes_ref, factors_ref, pack_sems)
    _, offset = first_expert(plan)
    shape = (plan.mine * plan.source_rows, gate_s.shape[0])
    row, col = iota(shape, 0), iota(shape, 1)
    slot = row % plan.cap_rows
    source = row % plan.source_rows // plan.cap_rows
    place = (source * plan.cap + slot) * plan.local + row // plan.source_rows
    place = jnp.where(slot < plan.cap, place, -plan.local)

    def pick(start, ref):
        table = jnp.where(col == place + start, 1.0, 0.0).astype(BF16)
        return dot(table, ref[...]).astype(BF16)

    for copy in saved:
        copy.wait()
    own_ref[0] = pick(offset, gate_s)
    own_ref[1] = pick(offset, up_s)
    if other_ref is not None:
        other_ref[0] = pick(plan.mine - offset, gate_s)
        other_ref[1] = pick(plan.mine - offset, up_s)


def prepare(plan, x, routes, factors, saved_gate, saved_up, after):
    flat = (plan.owners * plan.cap * plan.local, plan.hidden)

    def flatten(saved):
        return in_hbm(jnp.swapaxes(saved[0], 1, 2).reshape(flat))

    part = jax.ShapeDtypeStruct((2, plan.mine * plan.source_rows, plan.hidden), BF16)
    packed_shape = jax.ShapeDtypeStruct((plan.count, plan.sent), BF16)
    done_shape = jax.ShapeDtypeStruct((16, plan.sent), BF16)
    out_shape = [packed_shape, done_shape] + [part] * plan.split
    packed, done, *saved = pl.pallas_call(
        functools.partial(prepare_kernel, plan),
        out_shape=out_shape,
        in_specs=[hbm()] * 5 + [pl.BlockSpec(memory_space=pl.ANY)],
        out_specs=[vmem()] * len(out_shape),
        scratch_shapes=[
            pltpu.VMEM(flat, BF16),
            pltpu.VMEM(flat, BF16),
            pltpu.SemaphoreType.DMA((2,)),
            *pack_scratch(plan),
        ],
        compiler_params=pltpu.CompilerParams(vmem_limit_bytes=8 * MIB),
        cost_estimate=pl.CostEstimate(
            flops=0, bytes_accessed=plan.owners * plan.width * plan.sent, transcendentals=0
        ),
        name="prepare",
    )(
        in_hbm(x),
        in_hbm(routes.T),
        in_hbm(factors.T),
        flatten(saved_gate),
        flatten(saved_up),
        after,
    )
    return packed, saved, done


def fetch_kernel(plan, w_hbm, after, w_ref, done_ref, sems):
    copies = weight_copies(plan, w_hbm, weight_slots(plan, w_ref), sems)
    for copy in copies:
        copy.start()
    done_ref[...] = jnp.zeros_like(done_ref)
    for copy in copies:
        copy.wait()


def fetch(plan, w, after):
    return pl.pallas_call(
        functools.partial(fetch_kernel, plan),
        out_shape=(
            pltpu.VMEM((plan.mine, plan.hidden, plan.width), BF16),
            jax.ShapeDtypeStruct((16, plan.sent), BF16),
        ),
        in_specs=[hbm(), pl.BlockSpec(memory_space=pl.ANY)],
        out_specs=(vmem(), vmem()),
        scratch_shapes=[pltpu.SemaphoreType.DMA((plan.mine,))],
        compiler_params=pltpu.CompilerParams(vmem_limit_bytes=MIB),
        cost_estimate=pl.CostEstimate(
            flops=0,
            bytes_accessed=2 * plan.mine * plan.hidden * plan.width * 2,
            transcendentals=0,
        ),
        name="fetch",
    )(in_hbm(w), after)


def arrived(plan, blocks, first, x_s):
    metas = jnp.concatenate([block[:, plan.width :] for block in blocks], axis=0)
    table, factor = tables(plan, metas, first)
    rows = jnp.concatenate([block[:, : plan.width] for block in blocks], axis=0)
    x_s[...] = dot(table, rows).astype(BF16)
    return table, factor


class Queue:
    def __init__(self, copies, ahead):
        self.copies, self.ahead, self.started, self.taken = copies, ahead, 0, 0

    def fill(self):
        limit = min(self.taken + self.ahead, len(self.copies))
        while self.started < limit:
            self.copies[self.started].start()
            self.started += 1

    def take(self):
        self.fill()
        self.copies[self.taken].wait()
        self.taken += 1
        self.fill()


def forward_kernel(plan, count, *refs):
    blocks, refs = refs[:count], refs[count:]
    gate_ref, up_hbm, down_hbm, *refs = refs
    outs, (kept_ref, up_s, down_s, x_s, y_s, gate_s, hidden_s, sems) = refs[:-8], refs[-8:]
    first, _ = first_expert(plan)
    downs = weight_slots(plan, kept_ref, down_s)
    copies = weight_copies(plan, up_hbm, weight_slots(plan, up_s), sems.at[0])
    copies += weight_copies(plan, down_hbm, downs, sems.at[1])
    queue = Queue(copies, 3)
    queue.fill()
    table, factor = arrived(plan, blocks, first, x_s)
    n = plan.expert_rows
    parts = [slice(e * n, (e + 1) * n) for e in range(plan.mine)]
    for e, part in enumerate(parts):
        gate_s[e] = dot_tb(x_s[part, :], gate_ref[e])
    up = None
    for e, part in enumerate(parts):
        queue.take()
        last, up = up, dot_tb(x_s[part, :], up_s[e])
        if e:
            gate = gate_s[e - 1]
            hidden_s[e - 1] = (gate / (1.0 + jnp.exp(-gate)) * last).astype(BF16)
    gate = gate_s[plan.mine - 1]
    hidden_s[plan.mine - 1] = (gate / (1.0 + jnp.exp(-gate)) * up).astype(BF16)
    for e, part in enumerate(parts):
        queue.take()
        out = dot(hidden_s[e], downs[e][...])
        y_s[part, :] = (out * factor[part]).astype(BF16)
    put_rows(outs, slice(None), dot_ta(table, y_s[...]).astype(BF16))


def put_rows(outs, columns, rows):
    start = 0
    for out in outs:
        stop = start + out.shape[0]
        out[:, columns] = rows[start:stop, :]
        start = stop


def backward_kernel(plan, count, *refs):
    blocks, refs = refs[:count], refs[count:]
    saved_ref, other_ref, refs = refs[0], refs[plan.split - 1], refs[plan.split :]
    gate_ref, kept_ref, up_hbm, down_hbm, *refs = refs
    outs, (up_s, down_s, x_s, y_s, score_s, grads_s, sems) = refs[:-7], refs[-7:]
    first, _ = first_expert(plan)
    downs = weight_slots(plan, kept_ref, down_s)
    copies = weight_copies(plan, down_hbm, downs, sems.at[0])[plan.kept :]
    copies += weight_copies(plan, up_hbm, weight_slots(plan, up_s), sems.at[1])
    queue = Queue(copies, 3)
    queue.fill()
    table, factor = arrived(plan, blocks, first, x_s)
    n, held = plan.expert_rows, plan.source_rows
    lane = iota((n, plan.meta), 1)
    parts = [slice(e * n, (e + 1) * n) for e in range(plan.mine)]

    def through_activation(e, grad):
        own = slice(e * held, (e + 1) * held)
        act, up = saved_ref[0, own, :], saved_ref[1, own, :]
        if plan.split > 1:
            act = jnp.concatenate([act, other_ref[0, own, :]], axis=0)
            up = jnp.concatenate([up, other_ref[1, own, :]], axis=0)
        act, up = act.astype(F32), up.astype(F32)
        sig = 1.0 / (1.0 + jnp.exp(-act))
        silu = act * sig
        score = jnp.sum(silu * up * grad, axis=1, keepdims=True)
        grads_s[0, e] = (grad * up * sig * (1.0 + act * (1.0 - sig))).astype(BF16)
        grads_s[1, e] = (grad * silu).astype(BF16)
        expert = first + e
        high = score.astype(BF16).astype(F32)
        middle = (score - high).astype(BF16).astype(F32)
        low = score - high - middle
        spread = jnp.where(lane == expert, high, 0.0)
        spread = jnp.where(lane == expert + plan.experts, middle, spread)
        spread = jnp.where(lane == expert + 2 * plan.experts, low, spread)
        score_s[parts[e], :] = spread.astype(BF16)

    grad = None
    for e, part in enumerate(parts):
        if e >= plan.kept:
            queue.take()
        last, grad = grad, dot_tb(x_s[part, :], downs[e][...])
        if e:
            through_activation(e - 1, last)
    through_activation(plan.mine - 1, grad)
    for e, part in enumerate(parts):
        queue.take()
        result = dot(grads_s[0, e], gate_ref[e]) + dot(grads_s[1, e], up_s[e])
        y_s[part, :] = (result * factor[part]).astype(BF16)
    half, near = plan.half, outs[: len(outs) // 2]
    far = outs[len(outs) // 2 :]
    put_rows(near, slice(0, half), dot_ta(table, y_s[:, :half]).astype(BF16))
    rest = plan.width - half
    put_rows(far, slice(0, rest), dot_ta(table, y_s[:, half:]).astype(BF16))
    scores = dot_ta(table, score_s[...]).astype(BF16)
    put_rows(far, slice(rest, rest + plan.meta), scores)


def part_shapes(plan, width, pieces=1):
    block = jax.ShapeDtypeStruct((plan.count, width), BF16)
    pieces = pieces if plan.owners % pieces == 0 else 1
    rows = plan.owners * plan.count // pieces
    other = jax.ShapeDtypeStruct((rows, width), BF16)
    return [block] * plan.owners + [other] * ((plan.split - 1) * pieces)


def expert_call(plan, kernel, name, inputs, up_hbm, down_hbm, shapes, scratch):
    def weight(count):
        return pltpu.VMEM((count, plan.hidden, plan.width), BF16)

    rows = pltpu.VMEM((plan.rows, plan.width), BF16)
    return pl.pallas_call(
        kernel,
        out_shape=shapes,
        in_specs=[vmem()] * len(inputs) + [hbm()] * 2,
        out_specs=[vmem()] * len(shapes),
        scratch_shapes=[
            *[weight(plan.mine), weight(max(plan.mine - plan.kept, 1)), rows, rows],
            *scratch,
            pltpu.SemaphoreType.DMA((2, plan.mine)),
        ],
        compiler_params=pltpu.CompilerParams(vmem_limit_bytes=31 * MIB),
        cost_estimate=pl.CostEstimate(
            flops=2 * 3 * plan.mine * plan.expert_rows * plan.width * plan.hidden,
            bytes_accessed=2 * 2 * plan.mine * plan.width * plan.hidden,
            transcendentals=0,
        ),
        name=name,
    )(*inputs, in_hbm(up_hbm), in_hbm(down_hbm))


def forward(plan, blocks, gate, up_hbm, down_hbm):
    kernel = functools.partial(forward_kernel, plan, len(blocks))
    shape = (plan.mine, plan.expert_rows, plan.hidden)
    scratch = [pltpu.VMEM(shape, F32), pltpu.VMEM(shape, BF16)]
    kept = pltpu.VMEM((plan.kept, plan.hidden, plan.width), BF16)
    shapes = part_shapes(plan, plan.width, 2) + [kept]
    inputs = [*blocks, in_vmem(gate)]
    *parts, kept = expert_call(
        plan, kernel, "forward", inputs, up_hbm, down_hbm, shapes, scratch
    )
    return parts, kept


def backward(plan, blocks, saved, gate, kept, up_hbm, down_hbm):
    kernel = functools.partial(backward_kernel, plan, len(blocks))
    scratch = [
        pltpu.VMEM((plan.rows, plan.meta), BF16),
        pltpu.VMEM((2, plan.mine, plan.expert_rows, plan.hidden), BF16),
    ]
    shapes = part_shapes(plan, plan.half) + part_shapes(plan, plan.sent - plan.half)
    inputs = [*blocks, *saved, in_vmem(gate), in_vmem(kept)]
    parts = expert_call(
        plan, kernel, "backward", inputs, up_hbm, down_hbm, shapes, scratch
    )
    return parts[: len(parts) // 2], parts[len(parts) // 2 :]


def gather_group(plan, block):
    return [block] + [plan.over_expert(block, d) for d in range(1, plan.owners)]


def sum_pair(plan, parts):
    own = [[p] for p in parts[: plan.owners]]
    d = 0
    for piece in parts[plan.owners :]:
        other = plan.over_pair(piece)
        for start in range(0, piece.shape[0], plan.count):
            own[d].append(other[start : start + plan.count])
            d += 1
    return own


def total(terms):
    return sum(t.astype(F32) for t in terms)


def scatter_group(plan, own):
    sent = [total(own[d]).astype(BF16) for d in range(1, plan.owners)]
    return own[0] + [plan.over_expert(x, d, True) for d, x in enumerate(sent, 1)]


def scatter_steps(plan, owns):
    if not plan.paired:
        return [scatter_group(plan, own) for own in owns]
    step = 1
    while step < plan.owners:
        away = [d for d in range(0, plan.owners, step) if d & step]
        for own in owns:
            sent = jnp.concatenate([total(own[d]).astype(BF16) for d in away])
            back = plan.over_expert(sent, step, True)
            for i, d in enumerate(away):
                own[d ^ step].append(back[i * plan.count : (i + 1) * plan.count])
        step *= 2
    return [own[0] for own in owns]


def finish_kernel(plan, count, *refs):
    parts, (routes_ref, out_hbm, score_hbm, out_s, score_s, sems) = refs[:count], refs[count:]
    half, rest = plan.half, plan.width - plan.half
    near = total([part[...] for part in parts[: count // 2]])
    far = total([part[...] for part in parts[count // 2 :]])
    out_s[:, :half] = near.astype(BF16)
    out_s[:, half:] = far[:, :rest].astype(BF16)
    out_copy = pltpu.make_async_copy(out_s, out_hbm, sems.at[0])
    out_copy.start()
    shape = (plan.meta, plan.meta)
    same = jnp.where(iota(shape, 0) == iota(shape, 1), 1.0, 0.0).astype(BF16)
    spread = dot_tb(same, far[:, rest:].astype(BF16))
    experts = plan.experts
    score = spread[:experts] + spread[experts : 2 * experts] + spread[2 * experts : 3 * experts]
    row = iota((experts, plan.count), 0)
    for k in range(plan.top):
        hit = row == routes_ref[k : k + 1, :]
        score_s[k : k + 1, :] = jnp.sum(jnp.where(hit, score, 0.0), axis=0, keepdims=True)
    score_copy = pltpu.make_async_copy(score_s, score_hbm, sems.at[1])
    score_copy.start()
    out_copy.wait()
    score_copy.wait()


def finish_back(plan, parts, routes):
    out, score = pl.pallas_call(
        functools.partial(finish_kernel, plan, len(parts)),
        out_shape=(
            jax.ShapeDtypeStruct((plan.count, plan.width), BF16),
            jax.ShapeDtypeStruct((plan.top, plan.count), F32),
        ),
        in_specs=[vmem()] * (len(parts) + 1),
        out_specs=(hbm(), hbm()),
        scratch_shapes=[
            pltpu.VMEM((plan.count, plan.width), BF16),
            pltpu.VMEM((plan.top, plan.count), F32),
            pltpu.SemaphoreType.DMA((2,)),
        ],
        compiler_params=pltpu.CompilerParams(vmem_limit_bytes=8 * MIB),
        name="finish",
    )(*parts, routes.T)
    return out, score.T


def body(
    tokens,
    routes,
    weights_fwd,
    cotangent,
    routes_back,
    weights_back,
    saved_gate,
    saved_up,
    w_gate,
    w_up,
    w_down,
):
    plan = Plan(tokens, routes, saved_gate, w_gate)
    packed = pack(plan, tokens, routes, weights_fwd)
    packed_back, saved, ready = prepare(
        plan, cotangent, routes_back, weights_back, saved_gate, saved_up, packed
    )
    gate_hbm, up_hbm = jnp.swapaxes(w_gate, 1, 2), jnp.swapaxes(w_up, 1, 2)
    if plan.paired and plan.owners > 1:
        blocks = [packed, plan.over_expert(packed, 1)]
        gate, done = fetch(plan, gate_hbm, blocks[1])
        step = 2
        while step < plan.owners:
            blocks.append(plan.over_expert(jnp.concatenate(blocks) + ready[:1], step))
            step *= 2
    else:
        blocks = gather_group(plan, packed)
        gate, done = fetch(plan, gate_hbm, packed)
    if plan.split > 1:
        blocks.append(plan.over_pair(jnp.concatenate(blocks) + done[:1]))
    blocks_back = gather_group(plan, packed_back)
    parts, kept = forward(plan, blocks, gate, up_hbm, w_down)
    parts, blocks_back = lax.optimization_barrier((parts, blocks_back))
    if plan.split > 1:
        blocks_back = blocks_back + [plan.over_pair(jnp.concatenate(blocks_back))]
        saved[1] = plan.over_pair(saved[1])
    terms = scatter_group(plan, sum_pair(plan, parts))
    parts_back = backward(plan, blocks_back, saved, gate, kept, up_hbm, w_down)
    parts_back, terms = lax.optimization_barrier((parts_back, terms))
    mixed = total(terms).astype(BF16)
    near, far = scatter_steps(plan, [sum_pair(plan, parts) for parts in parts_back])
    input_grad, weight_grad = finish_back(plan, near + far, routes_back)
    return (mixed, input_grad, weight_grad)


def solution(mesh):
    spec = P(("dp", "expert"), None)
    saved = P("dp", None, "expert", None, None)
    weight = P("expert", None, None)
    return jax.shard_map(
        body,
        mesh=mesh,
        in_specs=(spec,) * 6 + (saved,) * 2 + (weight,) * 3,
        out_specs=(spec,) * 3,
        check_vma=False,
    )
```

```python
import functools
import jax
import jax.numpy as jnp
from jax import lax
from jax.experimental import pallas as pl
from jax.experimental.pallas import tpu as pltpu
from jax.sharding import PartitionSpec as P

F32 = jnp.float32
BF16 = jnp.bfloat16
LANES = 128
MIB = 1 << 20


def round_up(value, unit):
    return -(-value // unit) * unit


def dot(a, b):
    return jnp.dot(a, b, preferred_element_type=F32)


def dot_tb(a, b):
    return lax.dot_general(a, b, (((1,), (1,)), ((), ())), preferred_element_type=F32)


def dot_ta(a, b):
    return lax.dot_general(a, b, (((0,), (0,)), ((), ())), preferred_element_type=F32)


def iota(shape, dim):
    return lax.broadcasted_iota(jnp.int32, shape, dim)


def vmem():
    return pl.BlockSpec(memory_space=pltpu.VMEM)


def hbm():
    return pl.BlockSpec(memory_space=pltpu.HBM)


def in_vmem(x):
    return pltpu.with_memory_space_constraint(x, pltpu.VMEM)


def in_hbm(x):
    return pltpu.with_memory_space_constraint(x, pltpu.HBM)


class Plan:
    def __init__(self, tokens, routes, saved_gate, w_gate):
        self.owners = lax.axis_size("expert")
        self.groups = lax.axis_size("dp")
        self.count, self.width = tokens.shape
        self.top = routes.shape[1]
        self.local = w_gate.shape[0]
        self.hidden = w_gate.shape[2]
        self.experts = self.owners * self.local
        self.cap = saved_gate.shape[3]
        self.cap_rows = round_up(self.cap, 8)
        self.split = 2 if self.groups % 2 == 0 and self.local % 2 == 0 else 1
        self.mine = self.local // self.split
        self.meta = round_up(3 * self.experts, LANES)
        self.blocks = self.split * self.owners
        self.source_rows = self.owners * self.cap_rows
        self.expert_rows = self.split * self.source_rows
        self.paired = self.owners & (self.owners - 1) == 0
        self.sent = self.width + self.meta
        self.half = round_up(self.width // 2, LANES)
        self.kept = min(self.mine, 2)
        self.rows = self.mine * self.expert_rows
        self.cols = self.blocks * self.count

    def peer(self, index, step, core):
        bits = self.owners.bit_length() - 1
        if self.owners != 1 << bits:
            return (index + step) % self.owners
        turned = sum(((step >> i) & 1) << (bits - 1 - i) for i in range(bits))
        return index ^ (step + (turned - step) * core)

    def over_expert(self, x, step, back=False):
        pairs = []
        for group in range(self.groups):
            for i in range(self.owners):
                near = group * self.owners + i
                far = self.peer(i, step, group % self.split) + group * self.owners
                pairs.append((near, far) if back else (far, near))
        return lax.ppermute(x, ("dp", "expert"), pairs)

    def over_pair(self, x):
        return lax.ppermute(x, "dp", [(i, i ^ 1) for i in range(self.groups)])


def pack_body(plan, sources, out_ref, routes_ref, factors_ref, sems):
    x_hbm, routes_hbm, factors_hbm = sources
    experts, count = plan.experts, plan.count
    rows = pltpu.make_async_copy(x_hbm, out_ref.at[:, : plan.width], sems.at[0])
    small = [
        pltpu.make_async_copy(routes_hbm, routes_ref, sems.at[1]),
        pltpu.make_async_copy(factors_hbm, factors_ref, sems.at[2]),
    ]
    for copy in (*small, rows):
        copy.start()
    for copy in small:
        copy.wait()
    lane = iota((plan.meta, count), 0)
    chosen = jnp.zeros((plan.meta, count), F32)
    parts = jnp.zeros((plan.meta, count), F32)
    for k in range(plan.top):
        route = routes_ref[k : k + 1, :]
        factor = factors_ref[k : k + 1, :]
        high = factor.astype(BF16).astype(F32)
        low = factor - high
        chosen = chosen + jnp.where(lane == route, 1.0, 0.0)
        parts = parts + jnp.where(lane == route + experts, high, 0.0)
        parts = parts + jnp.where(lane == route + 2 * experts, low, 0.0)
    earlier = jnp.where(iota((count, count), 0) < iota((count, count), 1), 1.0, 0.0)
    before = dot(chosen.astype(BF16), earlier.astype(BF16))
    facts = (chosen * (before + 1.0) + parts).astype(BF16)
    shape = (plan.meta, plan.meta)
    same = jnp.where(iota(shape, 0) == iota(shape, 1), 1.0, 0.0).astype(BF16)
    out_ref[:, plan.width :] = dot_ta(facts, same).astype(BF16)
    rows.wait()


def pack_scratch(plan):
    return [
        pltpu.VMEM((plan.top, plan.count), jnp.int32),
        pltpu.VMEM((plan.top, plan.count), F32),
        pltpu.SemaphoreType.DMA((3,)),
    ]


def pack_kernel(plan, *refs):
    sources, (out_ref, facts_ref), scratch = refs[:3], refs[3:5], refs[5:]
    pack_body(plan, sources, out_ref, *scratch)
    facts_ref[...] = out_ref[:, plan.width :]


def pack(plan, x, routes, factors):
    return pl.pallas_call(
        functools.partial(pack_kernel, plan),
        out_shape=(
            jax.ShapeDtypeStruct((plan.count, plan.sent), BF16),
            jax.ShapeDtypeStruct((plan.count, plan.meta), BF16),
        ),
        in_specs=[hbm()] * 3,
        out_specs=(vmem(), vmem()),
        scratch_shapes=pack_scratch(plan),
        compiler_params=pltpu.CompilerParams(vmem_limit_bytes=4 * MIB),
        name="pack",
    )(in_hbm(x), in_hbm(routes.T), in_hbm(factors.T))


def first_expert(plan):
    core = lax.rem(lax.axis_index("dp"), plan.split)
    return lax.axis_index("expert") * plan.local + core * plan.mine, core * plan.mine


def tables(plan, meta, first):
    me = lax.axis_index("expert")
    core = lax.rem(lax.axis_index("dp"), plan.split)
    row = iota((plan.rows, 1), 0)
    place = row % plan.expert_rows
    expert = first + row // plan.expert_rows
    wanted_slot = (row % plan.cap_rows + 1).astype(F32)
    wanted_block = place // plan.cap_rows
    lane = iota((1, plan.meta), 1)
    pick_slot = jnp.where(lane == expert, 1.0, 0.0).astype(BF16)
    pick_part = (lane == expert + plan.experts) | (lane == expert + 2 * plan.experts)
    slot = dot_tb(pick_slot, meta)
    part = dot_tb(jnp.where(pick_part, 1.0, 0.0).astype(BF16), meta)
    block = iota((1, plan.cols), 1) // plan.count
    group = block // plan.owners
    source = plan.peer(me, block % plan.owners, core ^ group)
    hit = (wanted_block == group * plan.owners + source) & (slot == wanted_slot)
    factor = jnp.sum(jnp.where(hit, part, 0.0), axis=1, keepdims=True)
    return jnp.where(hit, 1.0, 0.0).astype(BF16), factor


def weight_copies(plan, array, slots, sems):
    offset = first_expert(plan)[1]
    return [
        pltpu.make_async_copy(array.at[offset + e], slot, sems.at[e])
        for e, slot in enumerate(slots)
    ]


def weight_slots(plan, *refs):
    return [ref.at[e] for ref in refs for e in range(ref.shape[0])][: plan.mine]


def prepare_kernel(plan, x_hbm, routes_hbm, factors_hbm, gate_hbm, up_hbm, after, *refs):
    packed_ref, done_ref, own_ref = refs[:3]
    other_ref = refs[3] if plan.split > 1 else None
    gate_s, up_s, saved_sems, routes_ref, factors_ref, pack_sems = refs[plan.split + 2 :]
    done_ref[...] = jnp.zeros_like(done_ref)
    saved = [
        pltpu.make_async_copy(gate_hbm, gate_s, saved_sems.at[0]),
        pltpu.make_async_copy(up_hbm, up_s, saved_sems.at[1]),
    ]
    for copy in saved:
        copy.start()
    sources = x_hbm, routes_hbm, factors_hbm
    pack_body(plan, sources, packed_ref, routes_ref, factors_ref, pack_sems)
    _, offset = first_expert(plan)
    shape = (plan.mine * plan.source_rows, gate_s.shape[0])
    row, col = iota(shape, 0), iota(shape, 1)
    slot = row % plan.cap_rows
    source = row % plan.source_rows // plan.cap_rows
    place = (source * plan.cap + slot) * plan.local + row // plan.source_rows
    place = jnp.where(slot < plan.cap, place, -plan.local)

    def pick(start, ref):
        table = jnp.where(col == place + start, 1.0, 0.0).astype(BF16)
        return dot(table, ref[...]).astype(BF16)

    for copy in saved:
        copy.wait()
    own_ref[0] = pick(offset, gate_s)
    own_ref[1] = pick(offset, up_s)
    if other_ref is not None:
        other_ref[0] = pick(plan.mine - offset, gate_s)
        other_ref[1] = pick(plan.mine - offset, up_s)


def prepare(plan, x, routes, factors, saved_gate, saved_up, after):
    flat = (plan.owners * plan.cap * plan.local, plan.hidden)

    def flatten(saved):
        return in_hbm(jnp.swapaxes(saved[0], 1, 2).reshape(flat))

    part = jax.ShapeDtypeStruct((2, plan.mine * plan.source_rows, plan.hidden), BF16)
    packed_shape = jax.ShapeDtypeStruct((plan.count, plan.sent), BF16)
    done_shape = jax.ShapeDtypeStruct((16, plan.sent), BF16)
    out_shape = [packed_shape, done_shape] + [part] * plan.split
    packed, done, *saved = pl.pallas_call(
        functools.partial(prepare_kernel, plan),
        out_shape=out_shape,
        in_specs=[hbm()] * 5 + [pl.BlockSpec(memory_space=pl.ANY)],
        out_specs=[vmem()] * len(out_shape),
        scratch_shapes=[
            pltpu.VMEM(flat, BF16),
            pltpu.VMEM(flat, BF16),
            pltpu.SemaphoreType.DMA((2,)),
            *pack_scratch(plan),
        ],
        compiler_params=pltpu.CompilerParams(vmem_limit_bytes=8 * MIB),
        cost_estimate=pl.CostEstimate(
            flops=0, bytes_accessed=plan.owners * plan.width * plan.sent, transcendentals=0
        ),
        name="prepare",
    )(
        in_hbm(x),
        in_hbm(routes.T),
        in_hbm(factors.T),
        flatten(saved_gate),
        flatten(saved_up),
        after,
    )
    return packed, saved, done


def fetch_kernel(plan, w_hbm, after, also_after, w_ref, done_ref, sems):
    copies = weight_copies(plan, w_hbm, weight_slots(plan, w_ref), sems)
    for copy in copies:
        copy.start()
    done_ref[...] = jnp.zeros_like(done_ref)
    for copy in copies:
        copy.wait()


def fetch(plan, w, after, also_after):
    return pl.pallas_call(
        functools.partial(fetch_kernel, plan),
        out_shape=(
            pltpu.VMEM((plan.mine, plan.hidden, plan.width), BF16),
            jax.ShapeDtypeStruct((16, plan.sent), BF16),
        ),
        in_specs=[hbm()] + [pl.BlockSpec(memory_space=pl.ANY)] * 2,
        out_specs=(vmem(), vmem()),
        scratch_shapes=[pltpu.SemaphoreType.DMA((plan.mine,))],
        compiler_params=pltpu.CompilerParams(vmem_limit_bytes=MIB),
        cost_estimate=pl.CostEstimate(
            flops=0,
            bytes_accessed=2 * plan.mine * plan.hidden * plan.width * 2,
            transcendentals=0,
        ),
        name="fetch",
    )(in_hbm(w), after, also_after)


def arrived(plan, blocks, first, x_s):
    metas = jnp.concatenate([block[:, plan.width :] for block in blocks], axis=0)
    table, factor = tables(plan, metas, first)
    rows = jnp.concatenate([block[:, : plan.width] for block in blocks], axis=0)
    x_s[...] = dot(table, rows).astype(BF16)
    return table, factor


class Queue:
    def __init__(self, copies, ahead):
        self.copies, self.ahead, self.started, self.taken = copies, ahead, 0, 0

    def fill(self):
        limit = min(self.taken + self.ahead, len(self.copies))
        while self.started < limit:
            self.copies[self.started].start()
            self.started += 1

    def take(self):
        self.fill()
        self.copies[self.taken].wait()
        self.taken += 1
        self.fill()


def forward_kernel(plan, count, *refs):
    blocks, refs = refs[:count], refs[count:]
    gate_ref, up_hbm, down_hbm, *refs = refs
    outs, (kept_ref, up_s, down_s, x_s, y_s, gate_s, hidden_s, sems) = refs[:-8], refs[-8:]
    first, _ = first_expert(plan)
    downs = weight_slots(plan, kept_ref, down_s)
    copies = weight_copies(plan, up_hbm, weight_slots(plan, up_s), sems.at[0])
    copies += weight_copies(plan, down_hbm, downs, sems.at[1])
    queue = Queue(copies, 3)
    queue.fill()
    table, factor = arrived(plan, blocks, first, x_s)
    n = plan.expert_rows
    parts = [slice(e * n, (e + 1) * n) for e in range(plan.mine)]
    for e, part in enumerate(parts):
        gate_s[e] = dot_tb(x_s[part, :], gate_ref[e])
    up = None
    for e, part in enumerate(parts):
        queue.take()
        last, up = up, dot_tb(x_s[part, :], up_s[e])
        if e:
            gate = gate_s[e - 1]
            hidden_s[e - 1] = (gate / (1.0 + jnp.exp(-gate)) * last).astype(BF16)
    gate = gate_s[plan.mine - 1]
    hidden_s[plan.mine - 1] = (gate / (1.0 + jnp.exp(-gate)) * up).astype(BF16)
    for e, part in enumerate(parts):
        queue.take()
        out = dot(hidden_s[e], downs[e][...])
        y_s[part, :] = (out * factor[part]).astype(BF16)
    put_rows(outs, slice(None), dot_ta(table, y_s[...]).astype(BF16))


def put_rows(outs, columns, rows):
    start = 0
    for out in outs:
        stop = start + out.shape[0]
        out[:, columns] = rows[start:stop, :]
        start = stop


def backward_kernel(plan, count, *refs):
    blocks, refs = refs[:count], refs[count:]
    saved_ref, other_ref, refs = refs[0], refs[plan.split - 1], refs[plan.split :]
    gate_ref, kept_ref, up_hbm, down_hbm, *refs = refs
    outs, (up_s, down_s, x_s, y_s, score_s, grads_s, sems) = refs[:-7], refs[-7:]
    first, _ = first_expert(plan)
    downs = weight_slots(plan, kept_ref, down_s)
    copies = weight_copies(plan, down_hbm, downs, sems.at[0])[plan.kept :]
    copies += weight_copies(plan, up_hbm, weight_slots(plan, up_s), sems.at[1])
    queue = Queue(copies, 3)
    queue.fill()
    table, factor = arrived(plan, blocks, first, x_s)
    n, held = plan.expert_rows, plan.source_rows
    lane = iota((n, plan.meta), 1)
    parts = [slice(e * n, (e + 1) * n) for e in range(plan.mine)]

    def through_activation(e, grad):
        own = slice(e * held, (e + 1) * held)
        act, up = saved_ref[0, own, :], saved_ref[1, own, :]
        if plan.split > 1:
            act = jnp.concatenate([act, other_ref[0, own, :]], axis=0)
            up = jnp.concatenate([up, other_ref[1, own, :]], axis=0)
        act, up = act.astype(F32), up.astype(F32)
        sig = 1.0 / (1.0 + jnp.exp(-act))
        silu = act * sig
        score = jnp.sum(silu * up * grad, axis=1, keepdims=True)
        grads_s[0, e] = (grad * up * sig * (1.0 + act * (1.0 - sig))).astype(BF16)
        grads_s[1, e] = (grad * silu).astype(BF16)
        expert = first + e
        high = score.astype(BF16).astype(F32)
        middle = (score - high).astype(BF16).astype(F32)
        low = score - high - middle
        spread = jnp.where(lane == expert, high, 0.0)
        spread = jnp.where(lane == expert + plan.experts, middle, spread)
        spread = jnp.where(lane == expert + 2 * plan.experts, low, spread)
        score_s[parts[e], :] = spread.astype(BF16)

    grad = None
    for e, part in enumerate(parts):
        if e >= plan.kept:
            queue.take()
        last, grad = grad, dot_tb(x_s[part, :], downs[e][...])
        if e:
            through_activation(e - 1, last)
    through_activation(plan.mine - 1, grad)
    for e, part in enumerate(parts):
        queue.take()
        result = dot(grads_s[0, e], gate_ref[e]) + dot(grads_s[1, e], up_s[e])
        y_s[part, :] = (result * factor[part]).astype(BF16)
    half, near = plan.half, outs[: len(outs) // 2]
    far = outs[len(outs) // 2 :]
    put_rows(near, slice(0, half), dot_ta(table, y_s[:, :half]).astype(BF16))
    rest = plan.width - half
    put_rows(far, slice(0, rest), dot_ta(table, y_s[:, half:]).astype(BF16))
    scores = dot_ta(table, score_s[...]).astype(BF16)
    put_rows(far, slice(rest, rest + plan.meta), scores)


def part_shapes(plan, width, pieces=1):
    block = jax.ShapeDtypeStruct((plan.count, width), BF16)
    pieces = pieces if plan.owners % pieces == 0 else 1
    rows = plan.owners * plan.count // pieces
    other = jax.ShapeDtypeStruct((rows, width), BF16)
    return [block] * plan.owners + [other] * ((plan.split - 1) * pieces)


def expert_call(plan, kernel, name, inputs, up_hbm, down_hbm, shapes, scratch):
    def weight(count):
        return pltpu.VMEM((count, plan.hidden, plan.width), BF16)

    rows = pltpu.VMEM((plan.rows, plan.width), BF16)
    return pl.pallas_call(
        kernel,
        out_shape=shapes,
        in_specs=[vmem()] * len(inputs) + [hbm()] * 2,
        out_specs=[vmem()] * len(shapes),
        scratch_shapes=[
            *[weight(plan.mine), weight(max(plan.mine - plan.kept, 1)), rows, rows],
            *scratch,
            pltpu.SemaphoreType.DMA((2, plan.mine)),
        ],
        compiler_params=pltpu.CompilerParams(vmem_limit_bytes=31 * MIB),
        cost_estimate=pl.CostEstimate(
            flops=2 * 3 * plan.mine * plan.expert_rows * plan.width * plan.hidden,
            bytes_accessed=2 * 2 * plan.mine * plan.width * plan.hidden,
            transcendentals=0,
        ),
        name=name,
    )(*inputs, in_hbm(up_hbm), in_hbm(down_hbm))


def forward(plan, blocks, gate, up_hbm, down_hbm):
    kernel = functools.partial(forward_kernel, plan, len(blocks))
    shape = (plan.mine, plan.expert_rows, plan.hidden)
    scratch = [pltpu.VMEM(shape, F32), pltpu.VMEM(shape, BF16)]
    kept = pltpu.VMEM((plan.kept, plan.hidden, plan.width), BF16)
    shapes = part_shapes(plan, plan.width, 2) + [kept]
    inputs = [*blocks, in_vmem(gate)]
    *parts, kept = expert_call(
        plan, kernel, "forward", inputs, up_hbm, down_hbm, shapes, scratch
    )
    return parts, kept


def backward(plan, blocks, saved, gate, kept, up_hbm, down_hbm):
    kernel = functools.partial(backward_kernel, plan, len(blocks))
    scratch = [
        pltpu.VMEM((plan.rows, plan.meta), BF16),
        pltpu.VMEM((2, plan.mine, plan.expert_rows, plan.hidden), BF16),
    ]
    shapes = part_shapes(plan, plan.half) + part_shapes(plan, plan.sent - plan.half)
    inputs = [*blocks, *saved, in_vmem(gate), in_vmem(kept)]
    parts = expert_call(
        plan, kernel, "backward", inputs, up_hbm, down_hbm, shapes, scratch
    )
    return parts[: len(parts) // 2], parts[len(parts) // 2 :]


def gather_group(plan, block):
    return [block] + [plan.over_expert(block, d) for d in range(1, plan.owners)]


def sum_pair(plan, parts):
    own = [[p] for p in parts[: plan.owners]]
    d = 0
    for piece in parts[plan.owners :]:
        other = plan.over_pair(piece)
        for start in range(0, piece.shape[0], plan.count):
            own[d].append(other[start : start + plan.count])
            d += 1
    return own


def total(terms):
    return sum(t.astype(F32) for t in terms)


def scatter_group(plan, own):
    sent = [total(own[d]).astype(BF16) for d in range(1, plan.owners)]
    return own[0] + [plan.over_expert(x, d, True) for d, x in enumerate(sent, 1)]


def scatter_steps(plan, owns):
    if not plan.paired:
        return [scatter_group(plan, own) for own in owns]
    step = 1
    while step < plan.owners:
        away = [d for d in range(0, plan.owners, step) if d & step]
        for own in owns:
            sent = jnp.concatenate([total(own[d]).astype(BF16) for d in away])
            back = plan.over_expert(sent, step, True)
            for i, d in enumerate(away):
                own[d ^ step].append(back[i * plan.count : (i + 1) * plan.count])
        step *= 2
    return [own[0] for own in owns]


def finish_kernel(plan, count, *refs):
    parts, (routes_ref, out_hbm, score_hbm, out_s, score_s, sems) = refs[:count], refs[count:]
    half, rest = plan.half, plan.width - plan.half
    near = total([part[...] for part in parts[: count // 2]])
    far = total([part[...] for part in parts[count // 2 :]])
    out_s[:, :half] = near.astype(BF16)
    out_s[:, half:] = far[:, :rest].astype(BF16)
    out_copy = pltpu.make_async_copy(out_s, out_hbm, sems.at[0])
    out_copy.start()
    shape = (plan.meta, plan.meta)
    same = jnp.where(iota(shape, 0) == iota(shape, 1), 1.0, 0.0).astype(BF16)
    spread = dot_tb(same, far[:, rest:].astype(BF16))
    experts = plan.experts
    score = spread[:experts] + spread[experts : 2 * experts] + spread[2 * experts : 3 * experts]
    row = iota((experts, plan.count), 0)
    for k in range(plan.top):
        hit = row == routes_ref[k : k + 1, :]
        score_s[k : k + 1, :] = jnp.sum(jnp.where(hit, score, 0.0), axis=0, keepdims=True)
    score_copy = pltpu.make_async_copy(score_s, score_hbm, sems.at[1])
    score_copy.start()
    out_copy.wait()
    score_copy.wait()


def finish_back(plan, parts, routes):
    out, score = pl.pallas_call(
        functools.partial(finish_kernel, plan, len(parts)),
        out_shape=(
            jax.ShapeDtypeStruct((plan.count, plan.width), BF16),
            jax.ShapeDtypeStruct((plan.top, plan.count), F32),
        ),
        in_specs=[vmem()] * (len(parts) + 1),
        out_specs=(hbm(), hbm()),
        scratch_shapes=[
            pltpu.VMEM((plan.count, plan.width), BF16),
            pltpu.VMEM((plan.top, plan.count), F32),
            pltpu.SemaphoreType.DMA((2,)),
        ],
        compiler_params=pltpu.CompilerParams(vmem_limit_bytes=8 * MIB),
        name="finish",
    )(*parts, routes.T)
    return out, score.T


def body(
    tokens,
    routes,
    weights_fwd,
    cotangent,
    routes_back,
    weights_back,
    saved_gate,
    saved_up,
    w_gate,
    w_up,
    w_down,
):
    plan = Plan(tokens, routes, saved_gate, w_gate)
    packed, facts = pack(plan, tokens, routes, weights_fwd)
    packed_back, saved, ready = prepare(
        plan, cotangent, routes_back, weights_back, saved_gate, saved_up, packed
    )
    if plan.split > 1:
        saved[1] = plan.over_pair(saved[1])
    gate_hbm, up_hbm = jnp.swapaxes(w_gate, 1, 2), jnp.swapaxes(w_up, 1, 2)
    if plan.paired and plan.owners > 1:
        first = plan.over_expert(tokens, 1), plan.over_expert(facts, 1)
        blocks = [packed, jnp.concatenate(first, axis=1)]
        gate, done = fetch(plan, gate_hbm, first[0], saved[-1])
        step = 2
        while step < plan.owners:
            blocks.append(plan.over_expert(jnp.concatenate(blocks) + ready[:1], step))
            step *= 2
    else:
        blocks = gather_group(plan, packed)
        gate, done = fetch(plan, gate_hbm, packed, saved[-1])
    if plan.split > 1:
        blocks.append(plan.over_pair(jnp.concatenate(blocks) + done[:1]))
    blocks_back = gather_group(plan, packed_back)
    parts, kept = forward(plan, blocks, gate, up_hbm, w_down)
    parts, blocks_back = lax.optimization_barrier((parts, blocks_back))
    if plan.split > 1:
        blocks_back = blocks_back + [plan.over_pair(jnp.concatenate(blocks_back))]
    terms = scatter_group(plan, sum_pair(plan, parts))
    parts_back = backward(plan, blocks_back, saved, gate, kept, up_hbm, w_down)
    parts_back, terms = lax.optimization_barrier((parts_back, terms))
    mixed = total(terms).astype(BF16)
    near, far = scatter_steps(plan, [sum_pair(plan, parts) for parts in parts_back])
    input_grad, weight_grad = finish_back(plan, near + far, routes_back)
    return (mixed, input_grad, weight_grad)


def solution(mesh):
    spec = P(("dp", "expert"), None)
    saved = P("dp", None, "expert", None, None)
    weight = P("expert", None, None)
    return jax.shard_map(
        body,
        mesh=mesh,
        in_specs=(spec,) * 6 + (saved,) * 2 + (weight,) * 3,
        out_specs=(spec,) * 3,
        check_vma=False,
    )
```

```python
import functools
import jax
import jax.numpy as jnp
from jax import lax
from jax.experimental import pallas as pl
from jax.experimental.pallas import tpu as pltpu
from jax.sharding import PartitionSpec as P

F32 = jnp.float32
BF16 = jnp.bfloat16
LANES = 128
MIB = 1 << 20


def round_up(value, unit):
    return -(-value // unit) * unit


def dot(a, b):
    return jnp.dot(a, b, preferred_element_type=F32)


def dot_tb(a, b):
    return lax.dot_general(a, b, (((1,), (1,)), ((), ())), preferred_element_type=F32)


def dot_ta(a, b):
    return lax.dot_general(a, b, (((0,), (0,)), ((), ())), preferred_element_type=F32)


def iota(shape, dim):
    return lax.broadcasted_iota(jnp.int32, shape, dim)


def vmem():
    return pl.BlockSpec(memory_space=pltpu.VMEM)


def hbm():
    return pl.BlockSpec(memory_space=pltpu.HBM)


def in_vmem(x):
    return pltpu.with_memory_space_constraint(x, pltpu.VMEM)


def in_hbm(x):
    return pltpu.with_memory_space_constraint(x, pltpu.HBM)


class Plan:
    def __init__(self, tokens, routes, saved_gate, w_gate):
        self.owners = lax.axis_size("expert")
        self.groups = lax.axis_size("dp")
        self.count, self.width = tokens.shape
        self.top = routes.shape[1]
        self.local = w_gate.shape[0]
        self.hidden = w_gate.shape[2]
        self.experts = self.owners * self.local
        self.cap = saved_gate.shape[3]
        self.cap_rows = round_up(self.cap, 8)
        self.split = 2 if self.groups % 2 == 0 and self.local % 2 == 0 else 1
        self.mine = self.local // self.split
        self.meta = round_up(3 * self.experts, LANES)
        self.blocks = self.split * self.owners
        self.source_rows = self.owners * self.cap_rows
        self.expert_rows = self.split * self.source_rows
        self.paired = self.owners & (self.owners - 1) == 0
        self.sent = self.width + self.meta
        self.half = round_up(self.width // 2, LANES)
        self.kept = min(self.mine, 2)
        self.held = 1
        self.rows = self.mine * self.expert_rows
        self.cols = self.blocks * self.count

    def peer(self, index, step, core):
        bits = self.owners.bit_length() - 1
        if self.owners != 1 << bits:
            return (index + step) % self.owners
        turned = sum(((step >> i) & 1) << (bits - 1 - i) for i in range(bits))
        return index ^ (step + (turned - step) * core)

    def over_expert(self, x, step, back=False):
        pairs = []
        for group in range(self.groups):
            for i in range(self.owners):
                near = group * self.owners + i
                far = self.peer(i, step, group % self.split) + group * self.owners
                pairs.append((near, far) if back else (far, near))
        return lax.ppermute(x, ("dp", "expert"), pairs)

    def over_pair(self, x):
        return lax.ppermute(x, "dp", [(i, i ^ 1) for i in range(self.groups)])


def pack_body(plan, sources, out_ref, routes_ref, factors_ref, sems):
    x_hbm, routes_hbm, factors_hbm = sources
    experts, count = plan.experts, plan.count
    rows = pltpu.make_async_copy(x_hbm, out_ref.at[:, : plan.width], sems.at[0])
    small = [
        pltpu.make_async_copy(routes_hbm, routes_ref, sems.at[1]),
        pltpu.make_async_copy(factors_hbm, factors_ref, sems.at[2]),
    ]
    for copy in (*small, rows):
        copy.start()
    for copy in small:
        copy.wait()
    lane = iota((plan.meta, count), 0)
    chosen = jnp.zeros((plan.meta, count), F32)
    parts = jnp.zeros((plan.meta, count), F32)
    for k in range(plan.top):
        route = routes_ref[k : k + 1, :]
        factor = factors_ref[k : k + 1, :]
        high = factor.astype(BF16).astype(F32)
        low = factor - high
        chosen = chosen + jnp.where(lane == route, 1.0, 0.0)
        parts = parts + jnp.where(lane == route + experts, high, 0.0)
        parts = parts + jnp.where(lane == route + 2 * experts, low, 0.0)
    earlier = jnp.where(iota((count, count), 0) < iota((count, count), 1), 1.0, 0.0)
    before = dot(chosen.astype(BF16), earlier.astype(BF16))
    facts = (chosen * (before + 1.0) + parts).astype(BF16)
    shape = (plan.meta, plan.meta)
    same = jnp.where(iota(shape, 0) == iota(shape, 1), 1.0, 0.0).astype(BF16)
    out_ref[:, plan.width :] = dot_ta(facts, same).astype(BF16)
    rows.wait()


def pack_scratch(plan):
    return [
        pltpu.VMEM((plan.top, plan.count), jnp.int32),
        pltpu.VMEM((plan.top, plan.count), F32),
        pltpu.SemaphoreType.DMA((3,)),
    ]


def pack_kernel(plan, *refs):
    pack_body(plan, refs[:3], *refs[3:])


def pack(plan, x, routes, factors):
    return pl.pallas_call(
        functools.partial(pack_kernel, plan),
        out_shape=jax.ShapeDtypeStruct((plan.count, plan.sent), BF16),
        in_specs=[hbm()] * 3,
        out_specs=vmem(),
        scratch_shapes=pack_scratch(plan),
        compiler_params=pltpu.CompilerParams(vmem_limit_bytes=4 * MIB),
        name="pack",
    )(in_hbm(x), in_hbm(routes.T), in_hbm(factors.T))


def first_expert(plan):
    core = lax.rem(lax.axis_index("dp"), plan.split)
    return lax.axis_index("expert") * plan.local + core * plan.mine, core * plan.mine


def tables(plan, meta, first):
    me = lax.axis_index("expert")
    core = lax.rem(lax.axis_index("dp"), plan.split)
    row = iota((plan.rows, 1), 0)
    place = row % plan.expert_rows
    expert = first + row // plan.expert_rows
    wanted_slot = (row % plan.cap_rows + 1).astype(F32)
    wanted_block = place // plan.cap_rows
    lane = iota((1, plan.meta), 1)
    pick_slot = jnp.where(lane == expert, 1.0, 0.0).astype(BF16)
    pick_part = (lane == expert + plan.experts) | (lane == expert + 2 * plan.experts)
    slot = dot_tb(pick_slot, meta)
    part = dot_tb(jnp.where(pick_part, 1.0, 0.0).astype(BF16), meta)
    block = iota((1, plan.cols), 1) // plan.count
    group = block // plan.owners
    source = plan.peer(me, block % plan.owners, core ^ group)
    hit = (wanted_block == group * plan.owners + source) & (slot == wanted_slot)
    factor = jnp.sum(jnp.where(hit, part, 0.0), axis=1, keepdims=True)
    return jnp.where(hit, 1.0, 0.0).astype(BF16), factor


def weight_copies(plan, array, slots, sems):
    offset = first_expert(plan)[1]
    return [
        pltpu.make_async_copy(array.at[offset + e], slot, sems.at[e])
        for e, slot in enumerate(slots)
    ]


def weight_slots(plan, *refs):
    return [ref.at[e] for ref in refs for e in range(ref.shape[0])][: plan.mine]


def prepare_kernel(plan, x_hbm, routes_hbm, factors_hbm, gate_hbm, up_hbm, after, *refs):
    packed_ref, done_ref, own_ref = refs[:3]
    other_ref = refs[3] if plan.split > 1 else None
    gate_s, up_s, saved_sems, routes_ref, factors_ref, pack_sems = refs[plan.split + 2 :]
    done_ref[...] = jnp.zeros_like(done_ref)
    saved = [
        pltpu.make_async_copy(gate_hbm, gate_s, saved_sems.at[0]),
        pltpu.make_async_copy(up_hbm, up_s, saved_sems.at[1]),
    ]
    for copy in saved:
        copy.start()
    sources = x_hbm, routes_hbm, factors_hbm
    pack_body(plan, sources, packed_ref, routes_ref, factors_ref, pack_sems)
    _, offset = first_expert(plan)
    shape = (plan.mine * plan.source_rows, gate_s.shape[0])
    row, col = iota(shape, 0), iota(shape, 1)
    slot = row % plan.cap_rows
    source = row % plan.source_rows // plan.cap_rows
    place = (source * plan.cap + slot) * plan.local + row // plan.source_rows
    place = jnp.where(slot < plan.cap, place, -plan.local)

    def pick(start, ref):
        table = jnp.where(col == place + start, 1.0, 0.0).astype(BF16)
        return dot(table, ref[...]).astype(BF16)

    for copy in saved:
        copy.wait()
    own_ref[0] = pick(offset, gate_s)
    own_ref[1] = pick(offset, up_s)
    if other_ref is not None:
        other_ref[0] = pick(plan.mine - offset, gate_s)
        other_ref[1] = pick(plan.mine - offset, up_s)


def prepare(plan, x, routes, factors, saved_gate, saved_up, after):
    flat = (plan.owners * plan.cap * plan.local, plan.hidden)

    def flatten(saved):
        return in_hbm(jnp.swapaxes(saved[0], 1, 2).reshape(flat))

    part = jax.ShapeDtypeStruct((2, plan.mine * plan.source_rows, plan.hidden), BF16)
    packed_shape = jax.ShapeDtypeStruct((plan.count, plan.sent), BF16)
    done_shape = jax.ShapeDtypeStruct((16, plan.sent), BF16)
    out_shape = [packed_shape, done_shape] + [part] * plan.split
    packed, done, *saved = pl.pallas_call(
        functools.partial(prepare_kernel, plan),
        out_shape=out_shape,
        in_specs=[hbm()] * 5 + [pl.BlockSpec(memory_space=pl.ANY)],
        out_specs=[vmem()] * len(out_shape),
        scratch_shapes=[
            pltpu.VMEM(flat, BF16),
            pltpu.VMEM(flat, BF16),
            pltpu.SemaphoreType.DMA((2,)),
            *pack_scratch(plan),
        ],
        compiler_params=pltpu.CompilerParams(vmem_limit_bytes=8 * MIB),
        cost_estimate=pl.CostEstimate(
            flops=0, bytes_accessed=plan.owners * plan.width * plan.sent, transcendentals=0
        ),
        name="prepare",
    )(
        in_hbm(x),
        in_hbm(routes.T),
        in_hbm(factors.T),
        flatten(saved_gate),
        flatten(saved_up),
        after,
    )
    return packed, saved, done


def fetch_kernel(plan, gate_hbm, up_hbm, after, also_after, *refs):
    gate_ref, held_ref, done_ref, sems = refs
    copies = weight_copies(plan, gate_hbm, weight_slots(plan, gate_ref), sems.at[0])
    copies += weight_copies(plan, up_hbm, weight_slots(plan, held_ref), sems.at[1])
    for copy in copies:
        copy.start()
    done_ref[...] = jnp.zeros_like(done_ref)
    for copy in copies:
        copy.wait()


def fetch(plan, gate_hbm, up_hbm, after, also_after):
    return pl.pallas_call(
        functools.partial(fetch_kernel, plan),
        out_shape=(
            pltpu.VMEM((plan.mine, plan.hidden, plan.width), BF16),
            pltpu.VMEM((plan.held, plan.hidden, plan.width), BF16),
            jax.ShapeDtypeStruct((16, plan.sent), BF16),
        ),
        in_specs=[hbm()] * 2 + [pl.BlockSpec(memory_space=pl.ANY)] * 2,
        out_specs=(vmem(),) * 3,
        scratch_shapes=[pltpu.SemaphoreType.DMA((2, plan.mine))],
        compiler_params=pltpu.CompilerParams(vmem_limit_bytes=MIB),
        cost_estimate=pl.CostEstimate(
            flops=0,
            bytes_accessed=2 * plan.mine * plan.hidden * plan.width * 2,
            transcendentals=0,
        ),
        name="fetch",
    )(in_hbm(gate_hbm), in_hbm(up_hbm), after, also_after)


def arrived(plan, blocks, first, x_s):
    metas = jnp.concatenate([block[:, plan.width :] for block in blocks], axis=0)
    table, factor = tables(plan, metas, first)
    rows = jnp.concatenate([block[:, : plan.width] for block in blocks], axis=0)
    x_s[...] = dot(table, rows).astype(BF16)
    return table, factor


class Queue:
    def __init__(self, copies, ahead):
        self.copies, self.ahead, self.started, self.taken = copies, ahead, 0, 0

    def fill(self):
        limit = min(self.taken + self.ahead, len(self.copies))
        while self.started < limit:
            self.copies[self.started].start()
            self.started += 1

    def take(self):
        self.fill()
        self.copies[self.taken].wait()
        self.taken += 1
        self.fill()


def forward_kernel(plan, count, *refs):
    blocks, refs = refs[:count], refs[count:]
    gate_ref, held_ref, up_hbm, down_hbm, *refs = refs
    outs, (kept_ref, up_s, down_s, x_s, y_s, gate_s, hidden_s, sems) = refs[:-8], refs[-8:]
    first, _ = first_expert(plan)
    downs = weight_slots(plan, kept_ref, down_s)
    ups = weight_slots(plan, held_ref, up_s)
    copies = weight_copies(plan, up_hbm, ups, sems.at[0])[plan.held :]
    copies += weight_copies(plan, down_hbm, downs, sems.at[1])
    queue = Queue(copies, 3)
    queue.fill()
    table, factor = arrived(plan, blocks, first, x_s)
    n = plan.expert_rows
    parts = [slice(e * n, (e + 1) * n) for e in range(plan.mine)]
    for e, part in enumerate(parts):
        gate_s[e] = dot_tb(x_s[part, :], gate_ref[e])
    up = None
    for e, part in enumerate(parts):
        if e >= plan.held:
            queue.take()
        last, up = up, dot_tb(x_s[part, :], ups[e][...])
        if e:
            gate = gate_s[e - 1]
            hidden_s[e - 1] = (gate / (1.0 + jnp.exp(-gate)) * last).astype(BF16)
    gate = gate_s[plan.mine - 1]
    hidden_s[plan.mine - 1] = (gate / (1.0 + jnp.exp(-gate)) * up).astype(BF16)
    for e, part in enumerate(parts):
        queue.take()
        out = dot(hidden_s[e], downs[e][...])
        y_s[part, :] = (out * factor[part]).astype(BF16)
    put_rows(outs, slice(None), dot_ta(table, y_s[...]).astype(BF16))


def put_rows(outs, columns, rows):
    start = 0
    for out in outs:
        stop = start + out.shape[0]
        out[:, columns] = rows[start:stop, :]
        start = stop


def backward_kernel(plan, count, *refs):
    blocks, refs = refs[:count], refs[count:]
    saved_ref, other_ref, refs = refs[0], refs[plan.split - 1], refs[plan.split :]
    gate_ref, held_ref, kept_ref, up_hbm, down_hbm, *refs = refs
    outs, (up_s, down_s, x_s, y_s, score_s, grads_s, sems) = refs[:-7], refs[-7:]
    first, _ = first_expert(plan)
    downs = weight_slots(plan, kept_ref, down_s)
    copies = weight_copies(plan, down_hbm, downs, sems.at[0])[plan.kept :]
    ups = weight_slots(plan, held_ref, up_s)
    copies += weight_copies(plan, up_hbm, ups, sems.at[1])[plan.held :]
    queue = Queue(copies, 3)
    queue.fill()
    table, factor = arrived(plan, blocks, first, x_s)
    n, held = plan.expert_rows, plan.source_rows
    lane = iota((n, plan.meta), 1)
    parts = [slice(e * n, (e + 1) * n) for e in range(plan.mine)]

    def through_activation(e, grad):
        own = slice(e * held, (e + 1) * held)
        act, up = saved_ref[0, own, :], saved_ref[1, own, :]
        if plan.split > 1:
            act = jnp.concatenate([act, other_ref[0, own, :]], axis=0)
            up = jnp.concatenate([up, other_ref[1, own, :]], axis=0)
        act, up = act.astype(F32), up.astype(F32)
        sig = 1.0 / (1.0 + jnp.exp(-act))
        silu = act * sig
        score = jnp.sum(silu * up * grad, axis=1, keepdims=True)
        grads_s[0, e] = (grad * up * sig * (1.0 + act * (1.0 - sig))).astype(BF16)
        grads_s[1, e] = (grad * silu).astype(BF16)
        expert = first + e
        high = score.astype(BF16).astype(F32)
        middle = (score - high).astype(BF16).astype(F32)
        low = score - high - middle
        spread = jnp.where(lane == expert, high, 0.0)
        spread = jnp.where(lane == expert + plan.experts, middle, spread)
        spread = jnp.where(lane == expert + 2 * plan.experts, low, spread)
        score_s[parts[e], :] = spread.astype(BF16)

    grad = None
    for e, part in enumerate(parts):
        if e >= plan.kept:
            queue.take()
        last, grad = grad, dot_tb(x_s[part, :], downs[e][...])
        if e:
            through_activation(e - 1, last)
    through_activation(plan.mine - 1, grad)
    for e, part in enumerate(parts):
        if e >= plan.held:
            queue.take()
        result = dot(grads_s[0, e], gate_ref[e]) + dot(grads_s[1, e], ups[e][...])
        y_s[part, :] = (result * factor[part]).astype(BF16)
    half, near = plan.half, outs[: len(outs) // 2]
    far = outs[len(outs) // 2 :]
    put_rows(near, slice(0, half), dot_ta(table, y_s[:, :half]).astype(BF16))
    rest = plan.width - half
    put_rows(far, slice(0, rest), dot_ta(table, y_s[:, half:]).astype(BF16))
    scores = dot_ta(table, score_s[...]).astype(BF16)
    put_rows(far, slice(rest, rest + plan.meta), scores)


def part_shapes(plan, width, pieces=1):
    block = jax.ShapeDtypeStruct((plan.count, width), BF16)
    pieces = pieces if plan.owners % pieces == 0 else 1
    rows = plan.owners * plan.count // pieces
    other = jax.ShapeDtypeStruct((rows, width), BF16)
    return [block] * plan.owners + [other] * ((plan.split - 1) * pieces)


def expert_call(plan, kernel, name, inputs, up_hbm, down_hbm, shapes, scratch):
    def weight(count):
        return pltpu.VMEM((count, plan.hidden, plan.width), BF16)

    rows = pltpu.VMEM((plan.rows, plan.width), BF16)
    return pl.pallas_call(
        kernel,
        out_shape=shapes,
        in_specs=[vmem()] * len(inputs) + [hbm()] * 2,
        out_specs=[vmem()] * len(shapes),
        scratch_shapes=[
            weight(max(plan.mine - plan.held, 1)),
            weight(max(plan.mine - plan.kept, 1)),
            *[rows, rows],
            *scratch,
            pltpu.SemaphoreType.DMA((2, plan.mine)),
        ],
        compiler_params=pltpu.CompilerParams(vmem_limit_bytes=31 * MIB),
        cost_estimate=pl.CostEstimate(
            flops=2 * 3 * plan.mine * plan.expert_rows * plan.width * plan.hidden,
            bytes_accessed=2 * 2 * plan.mine * plan.width * plan.hidden,
            transcendentals=0,
        ),
        name=name,
    )(*inputs, in_hbm(up_hbm), in_hbm(down_hbm))


def forward(plan, blocks, gate, held, up_hbm, down_hbm):
    kernel = functools.partial(forward_kernel, plan, len(blocks))
    shape = (plan.mine, plan.expert_rows, plan.hidden)
    scratch = [pltpu.VMEM(shape, F32), pltpu.VMEM(shape, BF16)]
    kept = pltpu.VMEM((plan.kept, plan.hidden, plan.width), BF16)
    shapes = part_shapes(plan, plan.width, 2) + [kept]
    inputs = [*blocks, in_vmem(gate), in_vmem(held)]
    *parts, kept = expert_call(
        plan, kernel, "forward", inputs, up_hbm, down_hbm, shapes, scratch
    )
    return parts, kept


def backward(plan, blocks, saved, resident, up_hbm, down_hbm):
    kernel = functools.partial(backward_kernel, plan, len(blocks))
    scratch = [
        pltpu.VMEM((plan.rows, plan.meta), BF16),
        pltpu.VMEM((2, plan.mine, plan.expert_rows, plan.hidden), BF16),
    ]
    shapes = part_shapes(plan, plan.half) + part_shapes(plan, plan.sent - plan.half)
    inputs = [*blocks, *saved, *[in_vmem(w) for w in resident]]
    parts = expert_call(
        plan, kernel, "backward", inputs, up_hbm, down_hbm, shapes, scratch
    )
    return parts[: len(parts) // 2], parts[len(parts) // 2 :]


def gather_group(plan, block):
    return [block] + [plan.over_expert(block, d) for d in range(1, plan.owners)]


def sum_pair(plan, parts):
    own = [[p] for p in parts[: plan.owners]]
    d = 0
    for piece in parts[plan.owners :]:
        other = plan.over_pair(piece)
        for start in range(0, piece.shape[0], plan.count):
            own[d].append(other[start : start + plan.count])
            d += 1
    return own


def total(terms):
    return sum(t.astype(F32) for t in terms)


def scatter_group(plan, own):
    sent = [total(own[d]).astype(BF16) for d in range(1, plan.owners)]
    return own[0] + [plan.over_expert(x, d, True) for d, x in enumerate(sent, 1)]


def scatter_steps(plan, owns):
    if not plan.paired:
        return [scatter_group(plan, own) for own in owns]
    step = 1
    while step < plan.owners:
        away = [d for d in range(0, plan.owners, step) if d & step]
        for own in owns:
            sent = jnp.concatenate([total(own[d]).astype(BF16) for d in away])
            back = plan.over_expert(sent, step, True)
            for i, d in enumerate(away):
                own[d ^ step].append(back[i * plan.count : (i + 1) * plan.count])
        step *= 2
    return [own[0] for own in owns]


def finish_kernel(plan, count, *refs):
    parts, (routes_ref, out_hbm, score_hbm, out_s, score_s, sems) = refs[:count], refs[count:]
    half, rest = plan.half, plan.width - plan.half
    near = total([part[...] for part in parts[: count // 2]])
    far = total([part[...] for part in parts[count // 2 :]])
    out_s[:, :half] = near.astype(BF16)
    out_s[:, half:] = far[:, :rest].astype(BF16)
    out_copy = pltpu.make_async_copy(out_s, out_hbm, sems.at[0])
    out_copy.start()
    shape = (plan.meta, plan.meta)
    same = jnp.where(iota(shape, 0) == iota(shape, 1), 1.0, 0.0).astype(BF16)
    spread = dot_tb(same, far[:, rest:].astype(BF16))
    experts = plan.experts
    score = spread[:experts] + spread[experts : 2 * experts] + spread[2 * experts : 3 * experts]
    row = iota((experts, plan.count), 0)
    for k in range(plan.top):
        hit = row == routes_ref[k : k + 1, :]
        score_s[k : k + 1, :] = jnp.sum(jnp.where(hit, score, 0.0), axis=0, keepdims=True)
    score_copy = pltpu.make_async_copy(score_s, score_hbm, sems.at[1])
    score_copy.start()
    out_copy.wait()
    score_copy.wait()


def finish_back(plan, parts, routes):
    out, score = pl.pallas_call(
        functools.partial(finish_kernel, plan, len(parts)),
        out_shape=(
            jax.ShapeDtypeStruct((plan.count, plan.width), BF16),
            jax.ShapeDtypeStruct((plan.top, plan.count), F32),
        ),
        in_specs=[vmem()] * (len(parts) + 1),
        out_specs=(hbm(), hbm()),
        scratch_shapes=[
            pltpu.VMEM((plan.count, plan.width), BF16),
            pltpu.VMEM((plan.top, plan.count), F32),
            pltpu.SemaphoreType.DMA((2,)),
        ],
        compiler_params=pltpu.CompilerParams(vmem_limit_bytes=8 * MIB),
        name="finish",
    )(*parts, routes.T)
    return out, score.T


def body(
    tokens,
    routes,
    weights_fwd,
    cotangent,
    routes_back,
    weights_back,
    saved_gate,
    saved_up,
    w_gate,
    w_up,
    w_down,
):
    plan = Plan(tokens, routes, saved_gate, w_gate)
    packed = pack(plan, tokens, routes, weights_fwd)
    packed_back, saved, ready = prepare(
        plan, cotangent, routes_back, weights_back, saved_gate, saved_up, packed
    )
    if plan.split > 1:
        saved[1] = plan.over_pair(saved[1])
    gate_hbm, up_hbm = jnp.swapaxes(w_gate, 1, 2), jnp.swapaxes(w_up, 1, 2)
    if plan.paired and plan.owners > 1:
        blocks = [packed, plan.over_expert(packed, 1)]
        gate, held, done = fetch(plan, gate_hbm, up_hbm, blocks[1], saved[-1])
        step = 2
        while step < plan.owners:
            blocks.append(plan.over_expert(jnp.concatenate(blocks) + ready[:1], step))
            step *= 2
    else:
        blocks = gather_group(plan, packed)
        gate, held, done = fetch(plan, gate_hbm, up_hbm, packed, saved[-1])
    if plan.split > 1:
        blocks.append(plan.over_pair(jnp.concatenate(blocks) + done[:1]))
    blocks_back = gather_group(plan, packed_back)
    parts, kept = forward(plan, blocks, gate, held, up_hbm, w_down)
    parts, blocks_back = lax.optimization_barrier((parts, blocks_back))
    if plan.split > 1:
        blocks_back = blocks_back + [plan.over_pair(jnp.concatenate(blocks_back))]
    terms = scatter_group(plan, sum_pair(plan, parts))
    parts_back = backward(plan, blocks_back, saved, (gate, held, kept), up_hbm, w_down)
    parts_back, terms = lax.optimization_barrier((parts_back, terms))
    mixed = total(terms).astype(BF16)
    near, far = scatter_steps(plan, [sum_pair(plan, parts) for parts in parts_back])
    input_grad, weight_grad = finish_back(plan, near + far, routes_back)
    return (mixed, input_grad, weight_grad)


def solution(mesh):
    spec = P(("dp", "expert"), None)
    saved = P("dp", None, "expert", None, None)
    weight = P("expert", None, None)
    return jax.shard_map(
        body,
        mesh=mesh,
        in_specs=(spec,) * 6 + (saved,) * 2 + (weight,) * 3,
        out_specs=(spec,) * 3,
        check_vma=False,
    )
```

```python
import functools
import jax
import jax.numpy as jnp
from jax import lax
from jax.experimental import pallas as pl
from jax.experimental.pallas import tpu as pltpu
from jax.sharding import PartitionSpec as P

F32 = jnp.float32
BF16 = jnp.bfloat16
LANES = 128
MIB = 1 << 20


def round_up(value, unit):
    return -(-value // unit) * unit


def dot(a, b):
    return jnp.dot(a, b, preferred_element_type=F32)


def dot_tb(a, b):
    return lax.dot_general(a, b, (((1,), (1,)), ((), ())), preferred_element_type=F32)


def dot_ta(a, b):
    return lax.dot_general(a, b, (((0,), (0,)), ((), ())), preferred_element_type=F32)


def iota(shape, dim):
    return lax.broadcasted_iota(jnp.int32, shape, dim)


def vmem():
    return pl.BlockSpec(memory_space=pltpu.VMEM)


def hbm():
    return pl.BlockSpec(memory_space=pltpu.HBM)


def in_vmem(x):
    return pltpu.with_memory_space_constraint(x, pltpu.VMEM)


def in_hbm(x):
    return pltpu.with_memory_space_constraint(x, pltpu.HBM)


class Plan:
    def __init__(self, tokens, routes, saved_gate, w_gate):
        self.owners = lax.axis_size("expert")
        self.groups = lax.axis_size("dp")
        self.count, self.width = tokens.shape
        self.top = routes.shape[1]
        self.local = w_gate.shape[0]
        self.hidden = w_gate.shape[2]
        self.experts = self.owners * self.local
        self.cap = saved_gate.shape[3]
        self.cap_rows = round_up(self.cap, 8)
        self.split = 2 if self.groups % 2 == 0 and self.local % 2 == 0 else 1
        self.mine = self.local // self.split
        self.meta = round_up(3 * self.experts, LANES)
        self.blocks = self.split * self.owners
        self.source_rows = self.owners * self.cap_rows
        self.expert_rows = self.split * self.source_rows
        self.paired = self.owners & (self.owners - 1) == 0
        self.sent = self.width + self.meta
        self.half = round_up(self.width // 2, LANES)
        self.kept = min(self.mine, 2)
        self.held = 1
        self.rows = self.mine * self.expert_rows
        self.cols = self.blocks * self.count

    def peer(self, index, step, core):
        bits = self.owners.bit_length() - 1
        if self.owners != 1 << bits:
            return (index + step) % self.owners
        turned = sum(((step >> i) & 1) << (bits - 1 - i) for i in range(bits))
        return index ^ (step + (turned - step) * core)

    def over_expert(self, x, step, back=False):
        pairs = []
        for group in range(self.groups):
            for i in range(self.owners):
                near = group * self.owners + i
                far = self.peer(i, step, group % self.split) + group * self.owners
                pairs.append((near, far) if back else (far, near))
        return lax.ppermute(x, ("dp", "expert"), pairs)

    def over_pair(self, x):
        return lax.ppermute(x, "dp", [(i, i ^ 1) for i in range(self.groups)])


def pack_body(plan, sources, out_ref, routes_ref, factors_ref, sems):
    x_hbm, routes_hbm, factors_hbm = sources
    experts, count = plan.experts, plan.count
    rows = pltpu.make_async_copy(x_hbm, out_ref.at[:, : plan.width], sems.at[0])
    small = [
        pltpu.make_async_copy(routes_hbm, routes_ref, sems.at[1]),
        pltpu.make_async_copy(factors_hbm, factors_ref, sems.at[2]),
    ]
    for copy in (*small, rows):
        copy.start()
    for copy in small:
        copy.wait()
    lane = iota((plan.meta, count), 0)
    chosen = jnp.zeros((plan.meta, count), F32)
    parts = jnp.zeros((plan.meta, count), F32)
    for k in range(plan.top):
        route = routes_ref[k : k + 1, :]
        factor = factors_ref[k : k + 1, :]
        high = factor.astype(BF16).astype(F32)
        low = factor - high
        chosen = chosen + jnp.where(lane == route, 1.0, 0.0)
        parts = parts + jnp.where(lane == route + experts, high, 0.0)
        parts = parts + jnp.where(lane == route + 2 * experts, low, 0.0)
    earlier = jnp.where(iota((count, count), 0) < iota((count, count), 1), 1.0, 0.0)
    before = dot(chosen.astype(BF16), earlier.astype(BF16))
    facts = (chosen * (before + 1.0) + parts).astype(BF16)
    shape = (plan.meta, plan.meta)
    same = jnp.where(iota(shape, 0) == iota(shape, 1), 1.0, 0.0).astype(BF16)
    out_ref[:, plan.width :] = dot_ta(facts, same).astype(BF16)
    rows.wait()


def pack_scratch(plan):
    return [
        pltpu.VMEM((plan.top, plan.count), jnp.int32),
        pltpu.VMEM((plan.top, plan.count), F32),
        pltpu.SemaphoreType.DMA((3,)),
    ]


def pack_kernel(plan, *refs):
    pack_body(plan, refs[:3], *refs[3:])


def pack(plan, x, routes, factors):
    return pl.pallas_call(
        functools.partial(pack_kernel, plan),
        out_shape=jax.ShapeDtypeStruct((plan.count, plan.sent), BF16),
        in_specs=[hbm()] * 3,
        out_specs=vmem(),
        scratch_shapes=pack_scratch(plan),
        compiler_params=pltpu.CompilerParams(vmem_limit_bytes=4 * MIB),
        name="pack",
    )(in_hbm(x), in_hbm(routes.T), in_hbm(factors.T))


def first_expert(plan):
    core = lax.rem(lax.axis_index("dp"), plan.split)
    return lax.axis_index("expert") * plan.local + core * plan.mine, core * plan.mine


def tables(plan, meta, first):
    me = lax.axis_index("expert")
    core = lax.rem(lax.axis_index("dp"), plan.split)
    row = iota((plan.rows, 1), 0)
    place = row % plan.expert_rows
    expert = first + row // plan.expert_rows
    wanted_slot = (row % plan.cap_rows + 1).astype(F32)
    wanted_block = place // plan.cap_rows
    lane = iota((1, plan.meta), 1)
    pick_slot = jnp.where(lane == expert, 1.0, 0.0).astype(BF16)
    pick_part = (lane == expert + plan.experts) | (lane == expert + 2 * plan.experts)
    slot = dot_tb(pick_slot, meta)
    part = dot_tb(jnp.where(pick_part, 1.0, 0.0).astype(BF16), meta)
    block = iota((1, plan.cols), 1) // plan.count
    group = block // plan.owners
    source = plan.peer(me, block % plan.owners, core ^ group)
    hit = (wanted_block == group * plan.owners + source) & (slot == wanted_slot)
    factor = jnp.sum(jnp.where(hit, part, 0.0), axis=1, keepdims=True)
    return jnp.where(hit, 1.0, 0.0).astype(BF16), factor


def weight_copies(plan, array, slots, sems):
    offset = first_expert(plan)[1]
    return [
        pltpu.make_async_copy(array.at[offset + e], slot, sems.at[e])
        for e, slot in enumerate(slots)
    ]


def weight_slots(plan, *refs):
    return [ref.at[e] for ref in refs for e in range(ref.shape[0])][: plan.mine]


def prepare_kernel(plan, x_hbm, routes_hbm, factors_hbm, gate_hbm, up_hbm, after, *refs):
    packed_ref, done_ref, own_ref = refs[:3]
    other_ref = refs[3] if plan.split > 1 else None
    gate_s, up_s, saved_sems, routes_ref, factors_ref, pack_sems = refs[plan.split + 2 :]
    done_ref[...] = jnp.zeros_like(done_ref)
    saved = [
        pltpu.make_async_copy(gate_hbm, gate_s, saved_sems.at[0]),
        pltpu.make_async_copy(up_hbm, up_s, saved_sems.at[1]),
    ]
    for copy in saved:
        copy.start()
    sources = x_hbm, routes_hbm, factors_hbm
    pack_body(plan, sources, packed_ref, routes_ref, factors_ref, pack_sems)
    _, offset = first_expert(plan)
    shape = (plan.mine * plan.source_rows, gate_s.shape[0])
    row, col = iota(shape, 0), iota(shape, 1)
    slot = row % plan.cap_rows
    source = row % plan.source_rows // plan.cap_rows
    place = (source * plan.cap + slot) * plan.local + row // plan.source_rows
    place = jnp.where(slot < plan.cap, place, -plan.local)

    def pick(start, ref):
        table = jnp.where(col == place + start, 1.0, 0.0).astype(BF16)
        return dot(table, ref[...]).astype(BF16)

    for copy in saved:
        copy.wait()
    own_ref[0] = pick(offset, gate_s)
    own_ref[1] = pick(offset, up_s)
    if other_ref is not None:
        other_ref[0] = pick(plan.mine - offset, gate_s)
        other_ref[1] = pick(plan.mine - offset, up_s)


def prepare(plan, x, routes, factors, saved_gate, saved_up, after):
    flat = (plan.owners * plan.cap * plan.local, plan.hidden)

    def flatten(saved):
        return in_hbm(jnp.swapaxes(saved[0], 1, 2).reshape(flat))

    part = jax.ShapeDtypeStruct((2, plan.mine * plan.source_rows, plan.hidden), BF16)
    packed_shape = jax.ShapeDtypeStruct((plan.count, plan.sent), BF16)
    done_shape = jax.ShapeDtypeStruct((16, plan.sent), BF16)
    out_shape = [packed_shape, done_shape] + [part] * plan.split
    packed, done, *saved = pl.pallas_call(
        functools.partial(prepare_kernel, plan),
        out_shape=out_shape,
        in_specs=[hbm()] * 5 + [pl.BlockSpec(memory_space=pl.ANY)],
        out_specs=[vmem()] * len(out_shape),
        scratch_shapes=[
            pltpu.VMEM(flat, BF16),
            pltpu.VMEM(flat, BF16),
            pltpu.SemaphoreType.DMA((2,)),
            *pack_scratch(plan),
        ],
        compiler_params=pltpu.CompilerParams(vmem_limit_bytes=8 * MIB),
        cost_estimate=pl.CostEstimate(
            flops=0, bytes_accessed=plan.owners * plan.width * plan.sent, transcendentals=0
        ),
        name="prepare",
    )(
        in_hbm(x),
        in_hbm(routes.T),
        in_hbm(factors.T),
        flatten(saved_gate),
        flatten(saved_up),
        after,
    )
    return packed, saved, done


def fetch_kernel(plan, gate_hbm, up_hbm, after, also_after, *refs):
    gate_ref, held_ref, done_ref, sems = refs
    copies = weight_copies(plan, gate_hbm, weight_slots(plan, gate_ref), sems.at[0])
    copies += weight_copies(plan, up_hbm, weight_slots(plan, held_ref), sems.at[1])
    for copy in copies:
        copy.start()
    done_ref[...] = jnp.zeros_like(done_ref)
    for copy in copies:
        copy.wait()


def fetch(plan, gate_hbm, up_hbm, after, also_after):
    return pl.pallas_call(
        functools.partial(fetch_kernel, plan),
        out_shape=(
            pltpu.VMEM((plan.mine, plan.hidden, plan.width), BF16),
            pltpu.VMEM((plan.held, plan.hidden, plan.width), BF16),
            jax.ShapeDtypeStruct((16, plan.sent), BF16),
        ),
        in_specs=[hbm()] * 2 + [pl.BlockSpec(memory_space=pl.ANY)] * 2,
        out_specs=(vmem(),) * 3,
        scratch_shapes=[pltpu.SemaphoreType.DMA((2, plan.mine))],
        compiler_params=pltpu.CompilerParams(vmem_limit_bytes=MIB),
        cost_estimate=pl.CostEstimate(
            flops=0,
            bytes_accessed=2 * plan.mine * plan.hidden * plan.width * 2,
            transcendentals=0,
        ),
        name="fetch",
    )(in_hbm(gate_hbm), in_hbm(up_hbm), after, also_after)


def arrived(plan, blocks, first, x_s):
    metas = jnp.concatenate([block[:, plan.width :] for block in blocks], axis=0)
    table, factor = tables(plan, metas, first)
    rows = jnp.concatenate([block[:, : plan.width] for block in blocks], axis=0)
    x_s[...] = dot(table, rows).astype(BF16)
    return table, factor


class Queue:
    def __init__(self, copies, ahead):
        self.copies, self.ahead, self.started, self.taken = copies, ahead, 0, 0

    def fill(self):
        limit = min(self.taken + self.ahead, len(self.copies))
        while self.started < limit:
            self.copies[self.started].start()
            self.started += 1

    def take(self):
        self.fill()
        self.copies[self.taken].wait()
        self.taken += 1
        self.fill()


def forward_kernel(plan, count, *refs):
    blocks, refs = refs[:count], refs[count:]
    gate_ref, held_ref, up_hbm, down_hbm, *refs = refs
    outs, (kept_ref, up_s, down_s, x_s, y_s, gate_s, hidden_s, sems) = refs[:-8], refs[-8:]
    first, _ = first_expert(plan)
    downs = weight_slots(plan, kept_ref, down_s)
    ups = weight_slots(plan, held_ref, up_s)
    copies = weight_copies(plan, up_hbm, ups, sems.at[0])[plan.held :]
    copies += weight_copies(plan, down_hbm, downs, sems.at[1])
    queue = Queue(copies, 3)
    queue.fill()
    table, factor = arrived(plan, blocks, first, x_s)
    n = plan.expert_rows
    parts = [slice(e * n, (e + 1) * n) for e in range(plan.mine)]
    for e, part in enumerate(parts):
        gate_s[e] = dot_tb(x_s[part, :], gate_ref[e])
    up = None
    for e, part in enumerate(parts):
        if e >= plan.held:
            queue.take()
        last, up = up, dot_tb(x_s[part, :], ups[e][...])
        if e:
            gate = gate_s[e - 1]
            hidden_s[e - 1] = (gate / (1.0 + jnp.exp(-gate)) * last).astype(BF16)
    gate = gate_s[plan.mine - 1]
    hidden_s[plan.mine - 1] = (gate / (1.0 + jnp.exp(-gate)) * up).astype(BF16)
    for e, part in enumerate(parts):
        queue.take()
        out = dot(hidden_s[e], downs[e][...])
        y_s[part, :] = (out * factor[part]).astype(BF16)
    put_rows(outs, slice(None), dot_ta(table, y_s[...]).astype(BF16))


def put_rows(outs, columns, rows):
    start = 0
    for out in outs:
        stop = start + out.shape[0]
        out[:, columns] = rows[start:stop, :]
        start = stop


def backward_kernel(plan, count, *refs):
    blocks, refs = refs[:count], refs[count:]
    saved_ref, other_ref, refs = refs[0], refs[plan.split - 1], refs[plan.split :]
    gate_ref, held_ref, kept_ref, up_hbm, down_hbm, *refs = refs
    outs, (up_s, down_s, x_s, y_s, score_s, grads_s, sems) = refs[:-7], refs[-7:]
    first, _ = first_expert(plan)
    downs = weight_slots(plan, kept_ref, down_s)
    copies = weight_copies(plan, down_hbm, downs, sems.at[0])[plan.kept :]
    ups = weight_slots(plan, held_ref, up_s)
    copies += weight_copies(plan, up_hbm, ups, sems.at[1])[plan.held :]
    queue = Queue(copies, 3)
    queue.fill()
    table, factor = arrived(plan, blocks, first, x_s)
    n, held = plan.expert_rows, plan.source_rows
    lane = iota((n, plan.meta), 1)
    parts = [slice(e * n, (e + 1) * n) for e in range(plan.mine)]

    def through_activation(e, grad):
        own = slice(e * held, (e + 1) * held)
        act, up = saved_ref[0, own, :], saved_ref[1, own, :]
        if plan.split > 1:
            act = jnp.concatenate([act, other_ref[0, own, :]], axis=0)
            up = jnp.concatenate([up, other_ref[1, own, :]], axis=0)
        act, up = act.astype(F32), up.astype(F32)
        sig = 1.0 / (1.0 + jnp.exp(-act))
        silu = act * sig
        score = jnp.sum(silu * up * grad, axis=1, keepdims=True)
        grads_s[0, e] = (grad * up * sig * (1.0 + act * (1.0 - sig))).astype(BF16)
        grads_s[1, e] = (grad * silu).astype(BF16)
        expert = first + e
        high = score.astype(BF16).astype(F32)
        middle = (score - high).astype(BF16).astype(F32)
        low = score - high - middle
        spread = jnp.where(lane == expert, high, 0.0)
        spread = jnp.where(lane == expert + plan.experts, middle, spread)
        spread = jnp.where(lane == expert + 2 * plan.experts, low, spread)
        score_s[parts[e], :] = spread.astype(BF16)

    grad = None
    for e, part in enumerate(parts):
        if e >= plan.kept:
            queue.take()
        last, grad = grad, dot_tb(x_s[part, :], downs[e][...])
        if e:
            through_activation(e - 1, last)
    through_activation(plan.mine - 1, grad)
    for e, part in enumerate(parts):
        if e >= plan.held:
            queue.take()
        result = dot(grads_s[0, e], gate_ref[e]) + dot(grads_s[1, e], ups[e][...])
        y_s[part, :] = (result * factor[part]).astype(BF16)
    half, near = plan.half, outs[: len(outs) // 2]
    far = outs[len(outs) // 2 :]
    put_rows(near, slice(0, half), dot_ta(table, y_s[:, :half]).astype(BF16))
    rest = plan.width - half
    put_rows(far, slice(0, rest), dot_ta(table, y_s[:, half:]).astype(BF16))
    scores = dot_ta(table, score_s[...]).astype(BF16)
    put_rows(far, slice(rest, rest + plan.meta), scores)


def part_shapes(plan, width, pieces=1):
    block = jax.ShapeDtypeStruct((plan.count, width), BF16)
    pieces = pieces if plan.owners % pieces == 0 else 1
    rows = plan.owners * plan.count // pieces
    other = jax.ShapeDtypeStruct((rows, width), BF16)
    return [block] * plan.owners + [other] * ((plan.split - 1) * pieces)


def expert_call(plan, kernel, name, inputs, up_hbm, down_hbm, shapes, scratch):
    def weight(count):
        return pltpu.VMEM((count, plan.hidden, plan.width), BF16)

    rows = pltpu.VMEM((plan.rows, plan.width), BF16)
    return pl.pallas_call(
        kernel,
        out_shape=shapes,
        in_specs=[vmem()] * len(inputs) + [hbm()] * 2,
        out_specs=[vmem()] * len(shapes),
        scratch_shapes=[
            weight(max(plan.mine - plan.held, 1)),
            weight(max(plan.mine - plan.kept, 1)),
            *[rows, rows],
            *scratch,
            pltpu.SemaphoreType.DMA((2, plan.mine)),
        ],
        compiler_params=pltpu.CompilerParams(vmem_limit_bytes=26 * MIB),
        cost_estimate=pl.CostEstimate(
            flops=2 * 3 * plan.mine * plan.expert_rows * plan.width * plan.hidden,
            bytes_accessed=2 * 2 * plan.mine * plan.width * plan.hidden,
            transcendentals=0,
        ),
        name=name,
    )(*inputs, in_hbm(up_hbm), in_hbm(down_hbm))


def forward(plan, blocks, gate, held, up_hbm, down_hbm):
    kernel = functools.partial(forward_kernel, plan, len(blocks))
    shape = (plan.mine, plan.expert_rows, plan.hidden)
    scratch = [pltpu.VMEM(shape, F32), pltpu.VMEM(shape, BF16)]
    kept = pltpu.VMEM((plan.kept, plan.hidden, plan.width), BF16)
    shapes = part_shapes(plan, plan.width, 2) + [kept]
    inputs = [*blocks, in_vmem(gate), in_vmem(held)]
    *parts, kept = expert_call(
        plan, kernel, "forward", inputs, up_hbm, down_hbm, shapes, scratch
    )
    return parts, kept


def backward(plan, blocks, saved, resident, up_hbm, down_hbm):
    kernel = functools.partial(backward_kernel, plan, len(blocks))
    scratch = [
        pltpu.VMEM((plan.rows, plan.meta), BF16),
        pltpu.VMEM((2, plan.mine, plan.expert_rows, plan.hidden), BF16),
    ]
    shapes = part_shapes(plan, plan.half) + part_shapes(plan, plan.sent - plan.half)
    inputs = [*blocks, *saved, *[in_vmem(w) for w in resident]]
    parts = expert_call(
        plan, kernel, "backward", inputs, up_hbm, down_hbm, shapes, scratch
    )
    return parts[: len(parts) // 2], parts[len(parts) // 2 :]


def gather_group(plan, block):
    return [block] + [plan.over_expert(block, d) for d in range(1, plan.owners)]


def sum_pair(plan, parts):
    own = [[p] for p in parts[: plan.owners]]
    d = 0
    for piece in parts[plan.owners :]:
        other = plan.over_pair(piece)
        for start in range(0, piece.shape[0], plan.count):
            own[d].append(other[start : start + plan.count])
            d += 1
    return own


def total(terms):
    return sum(t.astype(F32) for t in terms)


def scatter_group(plan, own):
    sent = [total(own[d]).astype(BF16) for d in range(1, plan.owners)]
    return own[0] + [plan.over_expert(x, d, True) for d, x in enumerate(sent, 1)]


def scatter_steps(plan, owns):
    if not plan.paired:
        return [scatter_group(plan, own) for own in owns]
    step = 1
    while step < plan.owners:
        away = [d for d in range(0, plan.owners, step) if d & step]
        for own in owns:
            sent = jnp.concatenate([total(own[d]).astype(BF16) for d in away])
            back = plan.over_expert(sent, step, True)
            for i, d in enumerate(away):
                own[d ^ step].append(back[i * plan.count : (i + 1) * plan.count])
        step *= 2
    return [own[0] for own in owns]


def finish_kernel(plan, count, *refs):
    parts, (routes_ref, out_hbm, score_hbm, out_s, score_s, sems) = refs[:count], refs[count:]
    half, rest = plan.half, plan.width - plan.half
    near = total([part[...] for part in parts[: count // 2]])
    far = total([part[...] for part in parts[count // 2 :]])
    out_s[:, :half] = near.astype(BF16)
    out_s[:, half:] = far[:, :rest].astype(BF16)
    out_copy = pltpu.make_async_copy(out_s, out_hbm, sems.at[0])
    out_copy.start()
    shape = (plan.meta, plan.meta)
    same = jnp.where(iota(shape, 0) == iota(shape, 1), 1.0, 0.0).astype(BF16)
    spread = dot_tb(same, far[:, rest:].astype(BF16))
    experts = plan.experts
    score = spread[:experts] + spread[experts : 2 * experts] + spread[2 * experts : 3 * experts]
    row = iota((experts, plan.count), 0)
    for k in range(plan.top):
        hit = row == routes_ref[k : k + 1, :]
        score_s[k : k + 1, :] = jnp.sum(jnp.where(hit, score, 0.0), axis=0, keepdims=True)
    score_copy = pltpu.make_async_copy(score_s, score_hbm, sems.at[1])
    score_copy.start()
    out_copy.wait()
    score_copy.wait()


def finish_back(plan, parts, routes):
    out, score = pl.pallas_call(
        functools.partial(finish_kernel, plan, len(parts)),
        out_shape=(
            jax.ShapeDtypeStruct((plan.count, plan.width), BF16),
            jax.ShapeDtypeStruct((plan.top, plan.count), F32),
        ),
        in_specs=[vmem()] * (len(parts) + 1),
        out_specs=(hbm(), hbm()),
        scratch_shapes=[
            pltpu.VMEM((plan.count, plan.width), BF16),
            pltpu.VMEM((plan.top, plan.count), F32),
            pltpu.SemaphoreType.DMA((2,)),
        ],
        compiler_params=pltpu.CompilerParams(vmem_limit_bytes=8 * MIB),
        name="finish",
    )(*parts, routes.T)
    return out, score.T


def body(
    tokens,
    routes,
    weights_fwd,
    cotangent,
    routes_back,
    weights_back,
    saved_gate,
    saved_up,
    w_gate,
    w_up,
    w_down,
):
    plan = Plan(tokens, routes, saved_gate, w_gate)
    packed = pack(plan, tokens, routes, weights_fwd)
    packed_back, saved, ready = prepare(
        plan, cotangent, routes_back, weights_back, saved_gate, saved_up, packed
    )
    if plan.split > 1:
        saved[1] = plan.over_pair(saved[1])
    gate_hbm, up_hbm = jnp.swapaxes(w_gate, 1, 2), jnp.swapaxes(w_up, 1, 2)
    if plan.paired and plan.owners > 1:
        blocks = [packed, plan.over_expert(packed, 1)]
        gate, held, done = fetch(plan, gate_hbm, up_hbm, blocks[1], saved[-1])
        step = 2
        while step < plan.owners:
            blocks.append(plan.over_expert(jnp.concatenate(blocks) + ready[:1], step))
            step *= 2
    else:
        blocks = gather_group(plan, packed)
        gate, held, done = fetch(plan, gate_hbm, up_hbm, packed, saved[-1])
    if plan.split > 1:
        blocks.append(plan.over_pair(jnp.concatenate(blocks) + done[:1]))
    blocks_back = gather_group(plan, packed_back)
    parts, kept = forward(plan, blocks, gate, held, up_hbm, w_down)
    parts, blocks_back = lax.optimization_barrier((parts, blocks_back))
    if plan.split > 1:
        blocks_back = blocks_back + [plan.over_pair(jnp.concatenate(blocks_back))]
    terms = scatter_group(plan, sum_pair(plan, parts))
    parts_back = backward(plan, blocks_back, saved, (gate, held, kept), up_hbm, w_down)
    parts_back, terms = lax.optimization_barrier((parts_back, terms))
    mixed = total(terms).astype(BF16)
    near, far = scatter_steps(plan, [sum_pair(plan, parts) for parts in parts_back])
    input_grad, weight_grad = finish_back(plan, near + far, routes_back)
    return (mixed, input_grad, weight_grad)


def solution(mesh):
    spec = P(("dp", "expert"), None)
    saved = P("dp", None, "expert", None, None)
    weight = P("expert", None, None)
    return jax.shard_map(
        body,
        mesh=mesh,
        in_specs=(spec,) * 6 + (saved,) * 2 + (weight,) * 3,
        out_specs=(spec,) * 3,
        check_vma=False,
    )
```

```python
import functools
import jax
import jax.numpy as jnp
from jax import lax
from jax.experimental import pallas as pl
from jax.experimental.pallas import tpu as pltpu
from jax.sharding import PartitionSpec as P

F32 = jnp.float32
BF16 = jnp.bfloat16
LANES = 128
MIB = 1 << 20


def round_up(value, unit):
    return -(-value // unit) * unit


def dot(a, b):
    return jnp.dot(a, b, preferred_element_type=F32)


def dot_tb(a, b):
    return lax.dot_general(a, b, (((1,), (1,)), ((), ())), preferred_element_type=F32)


def dot_ta(a, b):
    return lax.dot_general(a, b, (((0,), (0,)), ((), ())), preferred_element_type=F32)


def iota(shape, dim):
    return lax.broadcasted_iota(jnp.int32, shape, dim)


def vmem():
    return pl.BlockSpec(memory_space=pltpu.VMEM)


def hbm():
    return pl.BlockSpec(memory_space=pltpu.HBM)


def in_vmem(x):
    return pltpu.with_memory_space_constraint(x, pltpu.VMEM)


def in_hbm(x):
    return pltpu.with_memory_space_constraint(x, pltpu.HBM)


class Plan:
    def __init__(self, tokens, routes, saved_gate, w_gate):
        self.owners = lax.axis_size("expert")
        self.groups = lax.axis_size("dp")
        self.count, self.width = tokens.shape
        self.top = routes.shape[1]
        self.local = w_gate.shape[0]
        self.hidden = w_gate.shape[2]
        self.experts = self.owners * self.local
        self.cap = saved_gate.shape[3]
        self.cap_rows = round_up(self.cap, 8)
        self.split = 2 if self.groups % 2 == 0 and self.local % 2 == 0 else 1
        self.mine = self.local // self.split
        self.meta = round_up(3 * self.experts, LANES)
        self.blocks = self.split * self.owners
        self.source_rows = self.owners * self.cap_rows
        self.expert_rows = self.split * self.source_rows
        self.paired = self.owners & (self.owners - 1) == 0
        self.sent = self.width + self.meta
        self.half = round_up(self.width // 2, LANES)
        self.kept = min(self.mine, 2)
        self.rows = self.mine * self.expert_rows
        self.cols = self.blocks * self.count

    def peer(self, index, step, core):
        bits = self.owners.bit_length() - 1
        if self.owners != 1 << bits:
            return (index + step) % self.owners
        turned = sum(((step >> i) & 1) << (bits - 1 - i) for i in range(bits))
        return index ^ (step + (turned - step) * core)

    def over_expert(self, x, step, back=False):
        pairs = []
        for group in range(self.groups):
            for i in range(self.owners):
                near = group * self.owners + i
                far = self.peer(i, step, group % self.split) + group * self.owners
                pairs.append((near, far) if back else (far, near))
        return lax.ppermute(x, ("dp", "expert"), pairs)

    def over_pair(self, x):
        return lax.ppermute(x, "dp", [(i, i ^ 1) for i in range(self.groups)])


def pack_body(plan, sources, out_ref, routes_ref, factors_ref, sems):
    x_hbm, routes_hbm, factors_hbm = sources
    experts, count = plan.experts, plan.count
    rows = pltpu.make_async_copy(x_hbm, out_ref.at[:, : plan.width], sems.at[0])
    small = [
        pltpu.make_async_copy(routes_hbm, routes_ref, sems.at[1]),
        pltpu.make_async_copy(factors_hbm, factors_ref, sems.at[2]),
    ]
    for copy in (*small, rows):
        copy.start()
    for copy in small:
        copy.wait()
    lane = iota((plan.meta, count), 0)
    chosen = jnp.zeros((plan.meta, count), F32)
    parts = jnp.zeros((plan.meta, count), F32)
    for k in range(plan.top):
        route = routes_ref[k : k + 1, :]
        factor = factors_ref[k : k + 1, :]
        high = factor.astype(BF16).astype(F32)
        low = factor - high
        chosen = chosen + jnp.where(lane == route, 1.0, 0.0)
        parts = parts + jnp.where(lane == route + experts, high, 0.0)
        parts = parts + jnp.where(lane == route + 2 * experts, low, 0.0)
    earlier = jnp.where(iota((count, count), 0) < iota((count, count), 1), 1.0, 0.0)
    before = dot(chosen.astype(BF16), earlier.astype(BF16))
    facts = (chosen * (before + 1.0) + parts).astype(BF16)
    shape = (plan.meta, plan.meta)
    same = jnp.where(iota(shape, 0) == iota(shape, 1), 1.0, 0.0).astype(BF16)
    out_ref[:, plan.width :] = dot_ta(facts, same).astype(BF16)
    rows.wait()


def pack_scratch(plan):
    return [
        pltpu.VMEM((plan.top, plan.count), jnp.int32),
        pltpu.VMEM((plan.top, plan.count), F32),
        pltpu.SemaphoreType.DMA((3,)),
    ]


def pack_kernel(plan, *refs):
    pack_body(plan, refs[:3], *refs[3:])


def pack(plan, x, routes, factors):
    return pl.pallas_call(
        functools.partial(pack_kernel, plan),
        out_shape=jax.ShapeDtypeStruct((plan.count, plan.sent), BF16),
        in_specs=[hbm()] * 3,
        out_specs=vmem(),
        scratch_shapes=pack_scratch(plan),
        compiler_params=pltpu.CompilerParams(vmem_limit_bytes=4 * MIB),
        name="pack",
    )(in_hbm(x), in_hbm(routes.T), in_hbm(factors.T))


def first_expert(plan):
    core = lax.rem(lax.axis_index("dp"), plan.split)
    return lax.axis_index("expert") * plan.local + core * plan.mine, core * plan.mine


def tables(plan, meta, first):
    me = lax.axis_index("expert")
    core = lax.rem(lax.axis_index("dp"), plan.split)
    row = iota((plan.rows, 1), 0)
    place = row % plan.expert_rows
    expert = first + row // plan.expert_rows
    wanted_slot = (row % plan.cap_rows + 1).astype(F32)
    wanted_block = place // plan.cap_rows
    lane = iota((1, plan.meta), 1)
    pick_slot = jnp.where(lane == expert, 1.0, 0.0).astype(BF16)
    pick_part = (lane == expert + plan.experts) | (lane == expert + 2 * plan.experts)
    slot = dot_tb(pick_slot, meta)
    part = dot_tb(jnp.where(pick_part, 1.0, 0.0).astype(BF16), meta)
    block = iota((1, plan.cols), 1) // plan.count
    group = block // plan.owners
    source = plan.peer(me, block % plan.owners, core ^ group)
    hit = (wanted_block == group * plan.owners + source) & (slot == wanted_slot)
    factor = jnp.sum(jnp.where(hit, part, 0.0), axis=1, keepdims=True)
    return jnp.where(hit, 1.0, 0.0).astype(BF16), factor


def weight_copies(plan, array, slots, sems):
    offset = first_expert(plan)[1]
    return [
        pltpu.make_async_copy(array.at[offset + e], slot, sems.at[e])
        for e, slot in enumerate(slots)
    ]


def weight_slots(plan, *refs):
    return [ref.at[e] for ref in refs for e in range(ref.shape[0])][: plan.mine]


def prepare_kernel(plan, x_hbm, routes_hbm, factors_hbm, gate_hbm, up_hbm, after, *refs):
    packed_ref, done_ref, own_ref = refs[:3]
    other_ref = refs[3] if plan.split > 1 else None
    gate_s, up_s, saved_sems, routes_ref, factors_ref, pack_sems = refs[plan.split + 2 :]
    done_ref[...] = jnp.zeros_like(done_ref)
    saved = [
        pltpu.make_async_copy(gate_hbm, gate_s, saved_sems.at[0]),
        pltpu.make_async_copy(up_hbm, up_s, saved_sems.at[1]),
    ]
    for copy in saved:
        copy.start()
    sources = x_hbm, routes_hbm, factors_hbm
    pack_body(plan, sources, packed_ref, routes_ref, factors_ref, pack_sems)
    _, offset = first_expert(plan)
    shape = (plan.mine * plan.source_rows, gate_s.shape[0])
    row, col = iota(shape, 0), iota(shape, 1)
    slot = row % plan.cap_rows
    source = row % plan.source_rows // plan.cap_rows
    place = (source * plan.cap + slot) * plan.local + row // plan.source_rows
    place = jnp.where(slot < plan.cap, place, -plan.local)

    def pick(start, ref):
        table = jnp.where(col == place + start, 1.0, 0.0).astype(BF16)
        return dot(table, ref[...]).astype(BF16)

    for copy in saved:
        copy.wait()
    own_ref[0] = pick(offset, gate_s)
    own_ref[1] = pick(offset, up_s)
    if other_ref is not None:
        other_ref[0] = pick(plan.mine - offset, gate_s)
        other_ref[1] = pick(plan.mine - offset, up_s)


def prepare(plan, x, routes, factors, saved_gate, saved_up, after):
    flat = (plan.owners * plan.cap * plan.local, plan.hidden)

    def flatten(saved):
        return in_hbm(jnp.swapaxes(saved[0], 1, 2).reshape(flat))

    part = jax.ShapeDtypeStruct((2, plan.mine * plan.source_rows, plan.hidden), BF16)
    packed_shape = jax.ShapeDtypeStruct((plan.count, plan.sent), BF16)
    done_shape = jax.ShapeDtypeStruct((16, plan.sent), BF16)
    out_shape = [packed_shape, done_shape] + [part] * plan.split
    packed, done, *saved = pl.pallas_call(
        functools.partial(prepare_kernel, plan),
        out_shape=out_shape,
        in_specs=[hbm()] * 5 + [pl.BlockSpec(memory_space=pl.ANY)],
        out_specs=[vmem()] * len(out_shape),
        scratch_shapes=[
            pltpu.VMEM(flat, BF16),
            pltpu.VMEM(flat, BF16),
            pltpu.SemaphoreType.DMA((2,)),
            *pack_scratch(plan),
        ],
        compiler_params=pltpu.CompilerParams(vmem_limit_bytes=8 * MIB),
        cost_estimate=pl.CostEstimate(
            flops=0, bytes_accessed=plan.owners * plan.width * plan.sent, transcendentals=0
        ),
        name="prepare",
    )(
        in_hbm(x),
        in_hbm(routes.T),
        in_hbm(factors.T),
        flatten(saved_gate),
        flatten(saved_up),
        after,
    )
    return packed, saved, done


def fetch_kernel(plan, w_hbm, after, also_after, w_ref, done_ref, sems):
    copies = weight_copies(plan, w_hbm, weight_slots(plan, w_ref), sems)
    for copy in copies:
        copy.start()
    done_ref[...] = jnp.zeros_like(done_ref)
    for copy in copies:
        copy.wait()


def fetch(plan, w, after, also_after):
    return pl.pallas_call(
        functools.partial(fetch_kernel, plan),
        out_shape=(
            pltpu.VMEM((plan.mine, plan.hidden, plan.width), BF16),
            jax.ShapeDtypeStruct((16, plan.sent), BF16),
        ),
        in_specs=[hbm()] + [pl.BlockSpec(memory_space=pl.ANY)] * 2,
        out_specs=(vmem(), vmem()),
        scratch_shapes=[pltpu.SemaphoreType.DMA((plan.mine,))],
        compiler_params=pltpu.CompilerParams(vmem_limit_bytes=MIB),
        cost_estimate=pl.CostEstimate(
            flops=0,
            bytes_accessed=2 * plan.mine * plan.hidden * plan.width * 2,
            transcendentals=0,
        ),
        name="fetch",
    )(in_hbm(w), after, also_after)


def arrived(plan, blocks, first, x_s):
    metas = jnp.concatenate([block[:, plan.width :] for block in blocks], axis=0)
    table, factor = tables(plan, metas, first)
    rows = jnp.concatenate([block[:, : plan.width] for block in blocks], axis=0)
    x_s[...] = dot(table, rows).astype(BF16)
    return table, factor


class Queue:
    def __init__(self, copies, ahead):
        self.copies, self.ahead, self.started, self.taken = copies, ahead, 0, 0

    def fill(self):
        limit = min(self.taken + self.ahead, len(self.copies))
        while self.started < limit:
            self.copies[self.started].start()
            self.started += 1

    def take(self, count):
        self.fill()
        for _ in range(count):
            self.copies[self.taken].wait()
            self.taken += 1
        self.fill()


def forward_kernel(plan, count, *refs):
    blocks, refs = refs[:count], refs[count:]
    gate_ref, up_hbm, down_hbm, *refs = refs
    outs, (kept_ref, up_s, down_s, x_s, y_s, gate_s, hidden_s, sems) = refs[:-8], refs[-8:]
    first, _ = first_expert(plan)
    downs = weight_slots(plan, kept_ref, down_s)
    copies = weight_copies(plan, up_hbm, weight_slots(plan, up_s), sems.at[0])
    copies += weight_copies(plan, down_hbm, downs, sems.at[1])
    queue = Queue(copies, 4)
    queue.fill()
    table, factor = arrived(plan, blocks, first, x_s)
    n = plan.expert_rows
    parts = [slice(e * n, (e + 1) * n) for e in range(plan.mine)]
    for e, part in enumerate(parts):
        gate_s[e] = dot_tb(x_s[part, :], gate_ref[e])
    up = None
    for e, part in enumerate(parts):
        if e % 2 == 0:
            queue.take(min(2, plan.mine - e))
        last, up = up, dot_tb(x_s[part, :], up_s[e])
        if e:
            gate = gate_s[e - 1]
            hidden_s[e - 1] = (gate / (1.0 + jnp.exp(-gate)) * last).astype(BF16)
    gate = gate_s[plan.mine - 1]
    hidden_s[plan.mine - 1] = (gate / (1.0 + jnp.exp(-gate)) * up).astype(BF16)
    for e, part in enumerate(parts):
        if e % 2 == 0:
            queue.take(min(2, plan.mine - e))
        out = dot(hidden_s[e], downs[e][...])
        y_s[part, :] = (out * factor[part]).astype(BF16)
    put_rows(outs, slice(None), dot_ta(table, y_s[...]).astype(BF16))


def put_rows(outs, columns, rows):
    start = 0
    for out in outs:
        stop = start + out.shape[0]
        out[:, columns] = rows[start:stop, :]
        start = stop


def backward_kernel(plan, count, *refs):
    blocks, refs = refs[:count], refs[count:]
    saved_ref, other_ref, refs = refs[0], refs[plan.split - 1], refs[plan.split :]
    gate_ref, kept_ref, up_hbm, down_hbm, *refs = refs
    outs, (up_s, down_s, x_s, y_s, score_s, grads_s, sems) = refs[:-7], refs[-7:]
    first, _ = first_expert(plan)
    downs = weight_slots(plan, kept_ref, down_s)
    copies = weight_copies(plan, down_hbm, downs, sems.at[0])[plan.kept :]
    copies += weight_copies(plan, up_hbm, weight_slots(plan, up_s), sems.at[1])
    queue = Queue(copies, 4)
    queue.fill()
    table, factor = arrived(plan, blocks, first, x_s)
    n, held = plan.expert_rows, plan.source_rows
    lane = iota((n, plan.meta), 1)
    parts = [slice(e * n, (e + 1) * n) for e in range(plan.mine)]

    def through_activation(e, grad):
        own = slice(e * held, (e + 1) * held)
        act, up = saved_ref[0, own, :], saved_ref[1, own, :]
        if plan.split > 1:
            act = jnp.concatenate([act, other_ref[0, own, :]], axis=0)
            up = jnp.concatenate([up, other_ref[1, own, :]], axis=0)
        act, up = act.astype(F32), up.astype(F32)
        sig = 1.0 / (1.0 + jnp.exp(-act))
        silu = act * sig
        score = jnp.sum(silu * up * grad, axis=1, keepdims=True)
        grads_s[0, e] = (grad * up * sig * (1.0 + act * (1.0 - sig))).astype(BF16)
        grads_s[1, e] = (grad * silu).astype(BF16)
        expert = first + e
        high = score.astype(BF16).astype(F32)
        middle = (score - high).astype(BF16).astype(F32)
        low = score - high - middle
        spread = jnp.where(lane == expert, high, 0.0)
        spread = jnp.where(lane == expert + plan.experts, middle, spread)
        spread = jnp.where(lane == expert + 2 * plan.experts, low, spread)
        score_s[parts[e], :] = spread.astype(BF16)

    grad = None
    for e, part in enumerate(parts):
        if e == plan.kept:
            queue.take(plan.mine - plan.kept)
        last, grad = grad, dot_tb(x_s[part, :], downs[e][...])
        if e:
            through_activation(e - 1, last)
    through_activation(plan.mine - 1, grad)
    for e, part in enumerate(parts):
        if e % 2 == 0:
            queue.take(min(2, plan.mine - e))
        result = dot(grads_s[0, e], gate_ref[e]) + dot(grads_s[1, e], up_s[e])
        y_s[part, :] = (result * factor[part]).astype(BF16)
    half, near = plan.half, outs[: len(outs) // 2]
    far = outs[len(outs) // 2 :]
    put_rows(near, slice(0, half), dot_ta(table, y_s[:, :half]).astype(BF16))
    rest = plan.width - half
    put_rows(far, slice(0, rest), dot_ta(table, y_s[:, half:]).astype(BF16))
    scores = dot_ta(table, score_s[...]).astype(BF16)
    put_rows(far, slice(rest, rest + plan.meta), scores)


def part_shapes(plan, width, pieces=1):
    block = jax.ShapeDtypeStruct((plan.count, width), BF16)
    pieces = pieces if plan.owners % pieces == 0 else 1
    rows = plan.owners * plan.count // pieces
    other = jax.ShapeDtypeStruct((rows, width), BF16)
    return [block] * plan.owners + [other] * ((plan.split - 1) * pieces)


def expert_call(plan, kernel, name, inputs, up_hbm, down_hbm, shapes, scratch):
    def weight(count):
        return pltpu.VMEM((count, plan.hidden, plan.width), BF16)

    rows = pltpu.VMEM((plan.rows, plan.width), BF16)
    return pl.pallas_call(
        kernel,
        out_shape=shapes,
        in_specs=[vmem()] * len(inputs) + [hbm()] * 2,
        out_specs=[vmem()] * len(shapes),
        scratch_shapes=[
            *[weight(plan.mine), weight(max(plan.mine - plan.kept, 1)), rows, rows],
            *scratch,
            pltpu.SemaphoreType.DMA((2, plan.mine)),
        ],
        compiler_params=pltpu.CompilerParams(vmem_limit_bytes=31 * MIB),
        cost_estimate=pl.CostEstimate(
            flops=2 * 3 * plan.mine * plan.expert_rows * plan.width * plan.hidden,
            bytes_accessed=2 * 2 * plan.mine * plan.width * plan.hidden,
            transcendentals=0,
        ),
        name=name,
    )(*inputs, in_hbm(up_hbm), in_hbm(down_hbm))


def forward(plan, blocks, gate, up_hbm, down_hbm):
    kernel = functools.partial(forward_kernel, plan, len(blocks))
    shape = (plan.mine, plan.expert_rows, plan.hidden)
    scratch = [pltpu.VMEM(shape, F32), pltpu.VMEM(shape, BF16)]
    kept = pltpu.VMEM((plan.kept, plan.hidden, plan.width), BF16)
    shapes = part_shapes(plan, plan.width, 2) + [kept]
    inputs = [*blocks, in_vmem(gate)]
    *parts, kept = expert_call(
        plan, kernel, "forward", inputs, up_hbm, down_hbm, shapes, scratch
    )
    return parts, kept


def backward(plan, blocks, saved, gate, kept, up_hbm, down_hbm):
    kernel = functools.partial(backward_kernel, plan, len(blocks))
    scratch = [
        pltpu.VMEM((plan.rows, plan.meta), BF16),
        pltpu.VMEM((2, plan.mine, plan.expert_rows, plan.hidden), BF16),
    ]
    shapes = part_shapes(plan, plan.half) + part_shapes(plan, plan.sent - plan.half)
    inputs = [*blocks, *saved, in_vmem(gate), in_vmem(kept)]
    parts = expert_call(
        plan, kernel, "backward", inputs, up_hbm, down_hbm, shapes, scratch
    )
    return parts[: len(parts) // 2], parts[len(parts) // 2 :]


def gather_group(plan, block):
    return [block] + [plan.over_expert(block, d) for d in range(1, plan.owners)]


def sum_pair(plan, parts):
    own = [[p] for p in parts[: plan.owners]]
    d = 0
    for piece in parts[plan.owners :]:
        other = plan.over_pair(piece)
        for start in range(0, piece.shape[0], plan.count):
            own[d].append(other[start : start + plan.count])
            d += 1
    return own


def total(terms):
    return sum(t.astype(F32) for t in terms)


def scatter_group(plan, own):
    sent = [total(own[d]).astype(BF16) for d in range(1, plan.owners)]
    return own[0] + [plan.over_expert(x, d, True) for d, x in enumerate(sent, 1)]


def scatter_steps(plan, owns):
    if not plan.paired:
        return [scatter_group(plan, own) for own in owns]
    step = 1
    while step < plan.owners:
        away = [d for d in range(0, plan.owners, step) if d & step]
        for own in owns:
            sent = jnp.concatenate([total(own[d]).astype(BF16) for d in away])
            back = plan.over_expert(sent, step, True)
            for i, d in enumerate(away):
                own[d ^ step].append(back[i * plan.count : (i + 1) * plan.count])
        step *= 2
    return [own[0] for own in owns]


def finish_kernel(plan, count, *refs):
    parts, (routes_ref, out_hbm, score_hbm, out_s, score_s, sems) = refs[:count], refs[count:]
    half, rest = plan.half, plan.width - plan.half
    near = total([part[...] for part in parts[: count // 2]])
    far = total([part[...] for part in parts[count // 2 :]])
    out_s[:, :half] = near.astype(BF16)
    out_s[:, half:] = far[:, :rest].astype(BF16)
    out_copy = pltpu.make_async_copy(out_s, out_hbm, sems.at[0])
    out_copy.start()
    shape = (plan.meta, plan.meta)
    same = jnp.where(iota(shape, 0) == iota(shape, 1), 1.0, 0.0).astype(BF16)
    spread = dot_tb(same, far[:, rest:].astype(BF16))
    experts = plan.experts
    score = spread[:experts] + spread[experts : 2 * experts] + spread[2 * experts : 3 * experts]
    row = iota((experts, plan.count), 0)
    for k in range(plan.top):
        hit = row == routes_ref[k : k + 1, :]
        score_s[k : k + 1, :] = jnp.sum(jnp.where(hit, score, 0.0), axis=0, keepdims=True)
    score_copy = pltpu.make_async_copy(score_s, score_hbm, sems.at[1])
    score_copy.start()
    out_copy.wait()
    score_copy.wait()


def finish_back(plan, parts, routes):
    out, score = pl.pallas_call(
        functools.partial(finish_kernel, plan, len(parts)),
        out_shape=(
            jax.ShapeDtypeStruct((plan.count, plan.width), BF16),
            jax.ShapeDtypeStruct((plan.top, plan.count), F32),
        ),
        in_specs=[vmem()] * (len(parts) + 1),
        out_specs=(hbm(), hbm()),
        scratch_shapes=[
            pltpu.VMEM((plan.count, plan.width), BF16),
            pltpu.VMEM((plan.top, plan.count), F32),
            pltpu.SemaphoreType.DMA((2,)),
        ],
        compiler_params=pltpu.CompilerParams(vmem_limit_bytes=8 * MIB),
        name="finish",
    )(*parts, routes.T)
    return out, score.T


def body(
    tokens,
    routes,
    weights_fwd,
    cotangent,
    routes_back,
    weights_back,
    saved_gate,
    saved_up,
    w_gate,
    w_up,
    w_down,
):
    plan = Plan(tokens, routes, saved_gate, w_gate)
    packed = pack(plan, tokens, routes, weights_fwd)
    packed_back, saved, ready = prepare(
        plan, cotangent, routes_back, weights_back, saved_gate, saved_up, packed
    )
    if plan.split > 1:
        saved[1] = plan.over_pair(saved[1])
    gate_hbm, up_hbm = jnp.swapaxes(w_gate, 1, 2), jnp.swapaxes(w_up, 1, 2)
    if plan.paired and plan.owners > 1:
        blocks = [packed, plan.over_expert(packed, 1)]
        gate, done = fetch(plan, gate_hbm, blocks[1], saved[-1])
        step = 2
        while step < plan.owners:
            blocks.append(plan.over_expert(jnp.concatenate(blocks) + ready[:1], step))
            step *= 2
    else:
        blocks = gather_group(plan, packed)
        gate, done = fetch(plan, gate_hbm, packed, saved[-1])
    if plan.split > 1:
        blocks.append(plan.over_pair(jnp.concatenate(blocks) + done[:1]))
    blocks_back = gather_group(plan, packed_back)
    parts, kept = forward(plan, blocks, gate, up_hbm, w_down)
    parts, blocks_back = lax.optimization_barrier((parts, blocks_back))
    if plan.split > 1:
        blocks_back = blocks_back + [plan.over_pair(jnp.concatenate(blocks_back))]
    terms = scatter_group(plan, sum_pair(plan, parts))
    parts_back = backward(plan, blocks_back, saved, gate, kept, up_hbm, w_down)
    parts_back, terms = lax.optimization_barrier((parts_back, terms))
    mixed = total(terms).astype(BF16)
    near, far = scatter_steps(plan, [sum_pair(plan, parts) for parts in parts_back])
    input_grad, weight_grad = finish_back(plan, near + far, routes_back)
    return (mixed, input_grad, weight_grad)


def solution(mesh):
    spec = P(("dp", "expert"), None)
    saved = P("dp", None, "expert", None, None)
    weight = P("expert", None, None)
    return jax.shard_map(
        body,
        mesh=mesh,
        in_specs=(spec,) * 6 + (saved,) * 2 + (weight,) * 3,
        out_specs=(spec,) * 3,
        check_vma=False,
    )
```

```python
import functools
import jax
import jax.numpy as jnp
from jax import lax
from jax.experimental import pallas as pl
from jax.experimental.pallas import tpu as pltpu
from jax.sharding import PartitionSpec as P

F32 = jnp.float32
BF16 = jnp.bfloat16
LANES = 128
MIB = 1 << 20


def round_up(value, unit):
    return -(-value // unit) * unit


def dot(a, b):
    return jnp.dot(a, b, preferred_element_type=F32)


def dot_tb(a, b):
    return lax.dot_general(a, b, (((1,), (1,)), ((), ())), preferred_element_type=F32)


def dot_ta(a, b):
    return lax.dot_general(a, b, (((0,), (0,)), ((), ())), preferred_element_type=F32)


def iota(shape, dim):
    return lax.broadcasted_iota(jnp.int32, shape, dim)


def vmem():
    return pl.BlockSpec(memory_space=pltpu.VMEM)


def hbm():
    return pl.BlockSpec(memory_space=pltpu.HBM)


def in_vmem(x):
    return pltpu.with_memory_space_constraint(x, pltpu.VMEM)


def in_hbm(x):
    return pltpu.with_memory_space_constraint(x, pltpu.HBM)


class Plan:
    def __init__(self, tokens, routes, saved_gate, w_gate):
        self.owners = lax.axis_size("expert")
        self.groups = lax.axis_size("dp")
        self.count, self.width = tokens.shape
        self.top = routes.shape[1]
        self.local = w_gate.shape[0]
        self.hidden = w_gate.shape[2]
        self.experts = self.owners * self.local
        self.cap = saved_gate.shape[3]
        self.cap_rows = round_up(self.cap, 8)
        self.split = 2 if self.groups % 2 == 0 and self.local % 2 == 0 else 1
        self.mine = self.local // self.split
        self.meta = round_up(3 * self.experts, LANES)
        self.blocks = self.split * self.owners
        self.source_rows = self.owners * self.cap_rows
        self.expert_rows = self.split * self.source_rows
        self.paired = self.owners & (self.owners - 1) == 0
        self.sent = self.width + self.meta
        self.half = round_up(self.width // 2, LANES)
        self.kept = min(self.mine, 2)
        self.rows = self.mine * self.expert_rows
        self.cols = self.blocks * self.count

    def peer(self, index, step, core):
        bits = self.owners.bit_length() - 1
        if self.owners != 1 << bits:
            return (index + step) % self.owners
        turned = sum(((step >> i) & 1) << (bits - 1 - i) for i in range(bits))
        return index ^ (step + (turned - step) * core)

    def over_expert(self, x, step, back=False):
        pairs = []
        for group in range(self.groups):
            for i in range(self.owners):
                near = group * self.owners + i
                far = self.peer(i, step, group % self.split) + group * self.owners
                pairs.append((near, far) if back else (far, near))
        return lax.ppermute(x, ("dp", "expert"), pairs)

    def over_pair(self, x):
        return lax.ppermute(x, "dp", [(i, i ^ 1) for i in range(self.groups)])


def pack_body(plan, sources, out_ref, routes_ref, factors_ref, sems):
    x_hbm, routes_hbm, factors_hbm = sources
    experts, count = plan.experts, plan.count
    rows = pltpu.make_async_copy(x_hbm, out_ref.at[:, : plan.width], sems.at[0])
    small = [
        pltpu.make_async_copy(routes_hbm, routes_ref, sems.at[1]),
        pltpu.make_async_copy(factors_hbm, factors_ref, sems.at[2]),
    ]
    for copy in (*small, rows):
        copy.start()
    for copy in small:
        copy.wait()
    lane = iota((plan.meta, count), 0)
    chosen = jnp.zeros((plan.meta, count), F32)
    parts = jnp.zeros((plan.meta, count), F32)
    for k in range(plan.top):
        route = routes_ref[k : k + 1, :]
        factor = factors_ref[k : k + 1, :]
        high = factor.astype(BF16).astype(F32)
        low = factor - high
        chosen = chosen + jnp.where(lane == route, 1.0, 0.0)
        parts = parts + jnp.where(lane == route + experts, high, 0.0)
        parts = parts + jnp.where(lane == route + 2 * experts, low, 0.0)
    earlier = jnp.where(iota((count, count), 0) < iota((count, count), 1), 1.0, 0.0)
    before = dot(chosen.astype(BF16), earlier.astype(BF16))
    facts = (chosen * (before + 1.0) + parts).astype(BF16)
    shape = (plan.meta, plan.meta)
    same = jnp.where(iota(shape, 0) == iota(shape, 1), 1.0, 0.0).astype(BF16)
    out_ref[:, plan.width :] = dot_ta(facts, same).astype(BF16)
    rows.wait()


def pack_scratch(plan):
    return [
        pltpu.VMEM((plan.top, plan.count), jnp.int32),
        pltpu.VMEM((plan.top, plan.count), F32),
        pltpu.SemaphoreType.DMA((3,)),
    ]


def pack_kernel(plan, *refs):
    pack_body(plan, refs[:3], *refs[3:])


def pack(plan, x, routes, factors):
    return pl.pallas_call(
        functools.partial(pack_kernel, plan),
        out_shape=jax.ShapeDtypeStruct((plan.count, plan.sent), BF16),
        in_specs=[hbm()] * 3,
        out_specs=vmem(),
        scratch_shapes=pack_scratch(plan),
        compiler_params=pltpu.CompilerParams(vmem_limit_bytes=4 * MIB),
        name="pack",
    )(in_hbm(x), in_hbm(routes.T), in_hbm(factors.T))


def first_expert(plan):
    core = lax.rem(lax.axis_index("dp"), plan.split)
    return lax.axis_index("expert") * plan.local + core * plan.mine, core * plan.mine


def tables(plan, meta, first):
    me = lax.axis_index("expert")
    core = lax.rem(lax.axis_index("dp"), plan.split)
    row = iota((plan.rows, 1), 0)
    place = row % plan.expert_rows
    expert = first + row // plan.expert_rows
    wanted_slot = (row % plan.cap_rows + 1).astype(F32)
    wanted_block = place // plan.cap_rows
    lane = iota((1, plan.meta), 1)
    pick_slot = jnp.where(lane == expert, 1.0, 0.0).astype(BF16)
    pick_part = (lane == expert + plan.experts) | (lane == expert + 2 * plan.experts)
    slot = dot_tb(pick_slot, meta)
    part = dot_tb(jnp.where(pick_part, 1.0, 0.0).astype(BF16), meta)
    block = iota((1, plan.cols), 1) // plan.count
    group = block // plan.owners
    source = plan.peer(me, block % plan.owners, core ^ group)
    hit = (wanted_block == group * plan.owners + source) & (slot == wanted_slot)
    factor = jnp.sum(jnp.where(hit, part, 0.0), axis=1, keepdims=True)
    return jnp.where(hit, 1.0, 0.0).astype(BF16), factor


def weight_copies(plan, array, slots, sems):
    offset = first_expert(plan)[1]
    return [
        pltpu.make_async_copy(array.at[offset + e], slot, sems.at[e])
        for e, slot in enumerate(slots)
    ]


def weight_slots(plan, *refs):
    return [ref.at[e] for ref in refs for e in range(ref.shape[0])][: plan.mine]


def prepare_kernel(plan, x_hbm, routes_hbm, factors_hbm, gate_hbm, up_hbm, after, *refs):
    packed_ref, done_ref, own_ref = refs[:3]
    other_ref = refs[3] if plan.split > 1 else None
    gate_s, up_s, saved_sems, routes_ref, factors_ref, pack_sems = refs[plan.split + 2 :]
    done_ref[...] = jnp.zeros_like(done_ref)
    saved = [
        pltpu.make_async_copy(gate_hbm, gate_s, saved_sems.at[0]),
        pltpu.make_async_copy(up_hbm, up_s, saved_sems.at[1]),
    ]
    for copy in saved:
        copy.start()
    sources = x_hbm, routes_hbm, factors_hbm
    pack_body(plan, sources, packed_ref, routes_ref, factors_ref, pack_sems)
    _, offset = first_expert(plan)
    shape = (plan.mine * plan.source_rows, gate_s.shape[0])
    row, col = iota(shape, 0), iota(shape, 1)
    slot = row % plan.cap_rows
    source = row % plan.source_rows // plan.cap_rows
    place = (source * plan.cap + slot) * plan.local + row // plan.source_rows
    place = jnp.where(slot < plan.cap, place, -plan.local)

    def pick(start, ref):
        table = jnp.where(col == place + start, 1.0, 0.0).astype(BF16)
        return dot(table, ref[...]).astype(BF16)

    for copy in saved:
        copy.wait()
    own_ref[0] = pick(offset, gate_s)
    own_ref[1] = pick(offset, up_s)
    if other_ref is not None:
        other_ref[0] = pick(plan.mine - offset, gate_s)
        other_ref[1] = pick(plan.mine - offset, up_s)


def prepare(plan, x, routes, factors, saved_gate, saved_up, after):
    flat = (plan.owners * plan.cap * plan.local, plan.hidden)

    def flatten(saved):
        return in_hbm(jnp.swapaxes(saved[0], 1, 2).reshape(flat))

    part = jax.ShapeDtypeStruct((2, plan.mine * plan.source_rows, plan.hidden), BF16)
    packed_shape = jax.ShapeDtypeStruct((plan.count, plan.sent), BF16)
    done_shape = jax.ShapeDtypeStruct((16, plan.sent), BF16)
    out_shape = [packed_shape, done_shape] + [part] * plan.split
    packed, done, *saved = pl.pallas_call(
        functools.partial(prepare_kernel, plan),
        out_shape=out_shape,
        in_specs=[hbm()] * 5 + [pl.BlockSpec(memory_space=pl.ANY)],
        out_specs=[vmem()] * len(out_shape),
        scratch_shapes=[
            pltpu.VMEM(flat, BF16),
            pltpu.VMEM(flat, BF16),
            pltpu.SemaphoreType.DMA((2,)),
            *pack_scratch(plan),
        ],
        compiler_params=pltpu.CompilerParams(vmem_limit_bytes=8 * MIB),
        cost_estimate=pl.CostEstimate(
            flops=0, bytes_accessed=plan.owners * plan.width * plan.sent, transcendentals=0
        ),
        name="prepare",
    )(
        in_hbm(x),
        in_hbm(routes.T),
        in_hbm(factors.T),
        flatten(saved_gate),
        flatten(saved_up),
        after,
    )
    return packed, saved, done


def fetch_kernel(plan, w_hbm, after, also_after, w_ref, done_ref, sems):
    copies = weight_copies(plan, w_hbm, weight_slots(plan, w_ref), sems)
    for copy in copies:
        copy.start()
    done_ref[...] = jnp.zeros_like(done_ref)
    for copy in copies:
        copy.wait()


def fetch(plan, w, after, also_after):
    return pl.pallas_call(
        functools.partial(fetch_kernel, plan),
        out_shape=(
            pltpu.VMEM((plan.mine, plan.hidden, plan.width), BF16),
            jax.ShapeDtypeStruct((16, plan.sent), BF16),
        ),
        in_specs=[hbm()] + [pl.BlockSpec(memory_space=pl.ANY)] * 2,
        out_specs=(vmem(), vmem()),
        scratch_shapes=[pltpu.SemaphoreType.DMA((plan.mine,))],
        compiler_params=pltpu.CompilerParams(vmem_limit_bytes=MIB),
        cost_estimate=pl.CostEstimate(
            flops=0,
            bytes_accessed=2 * plan.mine * plan.hidden * plan.width * 2,
            transcendentals=0,
        ),
        name="fetch",
    )(in_hbm(w), after, also_after)


def arrived(plan, blocks, first, x_s):
    metas = jnp.concatenate([block[:, plan.width :] for block in blocks], axis=0)
    table, factor = tables(plan, metas, first)
    rows = jnp.concatenate([block[:, : plan.width] for block in blocks], axis=0)
    x_s[...] = dot(table, rows).astype(BF16)
    return table, factor


class Queue:
    def __init__(self, copies, ahead):
        self.copies, self.ahead, self.started, self.taken = copies, ahead, 0, 0

    def fill(self):
        limit = min(self.taken + self.ahead, len(self.copies))
        while self.started < limit:
            self.copies[self.started].start()
            self.started += 1

    def take(self, count):
        self.fill()
        for _ in range(count):
            self.copies[self.taken].wait()
            self.taken += 1
        self.fill()


def forward_kernel(plan, count, *refs):
    blocks, refs = refs[:count], refs[count:]
    gate_ref, up_hbm, down_hbm, *refs = refs
    outs, (kept_ref, up_s, down_s, x_s, y_s, gate_s, hidden_s, sems) = refs[:-8], refs[-8:]
    first, _ = first_expert(plan)
    downs = weight_slots(plan, kept_ref, down_s)
    copies = weight_copies(plan, up_hbm, weight_slots(plan, up_s), sems.at[0])
    copies += weight_copies(plan, down_hbm, downs, sems.at[1])
    queue = Queue(copies, 4)
    queue.fill()
    table, factor = arrived(plan, blocks, first, x_s)
    n = plan.expert_rows
    parts = [slice(e * n, (e + 1) * n) for e in range(plan.mine)]
    for e, part in enumerate(parts):
        gate_s[e] = dot_tb(x_s[part, :], gate_ref[e])
    up = None
    for e, part in enumerate(parts):
        if e % 2 == 0:
            queue.take(min(2, plan.mine - e))
        last, up = up, dot_tb(x_s[part, :], up_s[e])
        if e:
            gate = gate_s[e - 1]
            hidden_s[e - 1] = (gate / (1.0 + jnp.exp(-gate)) * last).astype(BF16)
    gate = gate_s[plan.mine - 1]
    hidden_s[plan.mine - 1] = (gate / (1.0 + jnp.exp(-gate)) * up).astype(BF16)
    for e, part in enumerate(parts):
        if e % 2 == 0:
            queue.take(min(2, plan.mine - e))
        out = dot(hidden_s[e], downs[e][...])
        y_s[part, :] = (out * factor[part]).astype(BF16)
    put_rows(outs, slice(None), dot_ta(table, y_s[...]).astype(BF16))


def put_rows(outs, columns, rows):
    start = 0
    for out in outs:
        stop = start + out.shape[0]
        out[:, columns] = rows[start:stop, :]
        start = stop


def backward_kernel(plan, count, *refs):
    blocks, refs = refs[:count], refs[count:]
    saved_ref, other_ref, refs = refs[0], refs[plan.split - 1], refs[plan.split :]
    gate_ref, kept_ref, up_hbm, down_hbm, *refs = refs
    outs, (up_s, down_s, x_s, y_s, score_s, grads_s, sems) = refs[:-7], refs[-7:]
    first, _ = first_expert(plan)
    downs = weight_slots(plan, kept_ref, down_s)
    copies = weight_copies(plan, down_hbm, downs, sems.at[0])[plan.kept :]
    copies += weight_copies(plan, up_hbm, weight_slots(plan, up_s), sems.at[1])
    queue = Queue(copies, 4)
    queue.fill()
    table, factor = arrived(plan, blocks, first, x_s)
    n, held = plan.expert_rows, plan.source_rows
    lane = iota((n, plan.meta), 1)
    parts = [slice(e * n, (e + 1) * n) for e in range(plan.mine)]

    def through_activation(e, grad):
        own = slice(e * held, (e + 1) * held)
        act, up = saved_ref[0, own, :], saved_ref[1, own, :]
        if plan.split > 1:
            act = jnp.concatenate([act, other_ref[0, own, :]], axis=0)
            up = jnp.concatenate([up, other_ref[1, own, :]], axis=0)
        act, up = act.astype(F32), up.astype(F32)
        sig = 1.0 / (1.0 + jnp.exp(-act))
        silu = act * sig
        score = jnp.sum(silu * up * grad, axis=1, keepdims=True)
        grads_s[0, e] = (grad * up * sig * (1.0 + act * (1.0 - sig))).astype(BF16)
        grads_s[1, e] = (grad * silu).astype(BF16)
        expert = first + e
        high = score.astype(BF16).astype(F32)
        middle = (score - high).astype(BF16).astype(F32)
        low = score - high - middle
        spread = jnp.where(lane == expert, high, 0.0)
        spread = jnp.where(lane == expert + plan.experts, middle, spread)
        spread = jnp.where(lane == expert + 2 * plan.experts, low, spread)
        score_s[parts[e], :] = spread.astype(BF16)

    grad = None
    for e, part in enumerate(parts):
        if e == plan.kept:
            queue.take(plan.mine - plan.kept)
        last, grad = grad, dot_tb(x_s[part, :], downs[e][...])
        if e:
            through_activation(e - 1, last)
    through_activation(plan.mine - 1, grad)
    for e, part in enumerate(parts):
        if e % 2 == 0:
            queue.take(min(2, plan.mine - e))
        result = dot(grads_s[0, e], gate_ref[e]) + dot(grads_s[1, e], up_s[e])
        y_s[part, :] = (result * factor[part]).astype(BF16)
    half, near = plan.half, outs[: len(outs) // 2]
    far = outs[len(outs) // 2 :]
    put_rows(near, slice(0, half), dot_ta(table, y_s[:, :half]).astype(BF16))
    rest = plan.width - half
    put_rows(far, slice(0, rest), dot_ta(table, y_s[:, half:]).astype(BF16))
    scores = dot_ta(table, score_s[...]).astype(BF16)
    put_rows(far, slice(rest, rest + plan.meta), scores)


def part_shapes(plan, width, pieces=1):
    block = jax.ShapeDtypeStruct((plan.count, width), BF16)
    pieces = pieces if plan.owners % pieces == 0 else 1
    rows = plan.owners * plan.count // pieces
    other = jax.ShapeDtypeStruct((rows, width), BF16)
    return [block] * plan.owners + [other] * ((plan.split - 1) * pieces)


def expert_call(plan, kernel, name, inputs, up_hbm, down_hbm, shapes, scratch):
    def weight(count):
        return pltpu.VMEM((count, plan.hidden, plan.width), BF16)

    rows = pltpu.VMEM((plan.rows, plan.width), BF16)
    return pl.pallas_call(
        kernel,
        out_shape=shapes,
        in_specs=[vmem()] * len(inputs) + [hbm()] * 2,
        out_specs=[vmem()] * len(shapes),
        scratch_shapes=[
            *[weight(plan.mine), weight(max(plan.mine - plan.kept, 1)), rows, rows],
            *scratch,
            pltpu.SemaphoreType.DMA((2, plan.mine)),
        ],
        compiler_params=pltpu.CompilerParams(vmem_limit_bytes=31 * MIB),
        cost_estimate=pl.CostEstimate(
            flops=2 * 3 * plan.mine * plan.expert_rows * plan.width * plan.hidden,
            bytes_accessed=2 * 2 * plan.mine * plan.width * plan.hidden,
            transcendentals=0,
        ),
        name=name,
    )(*inputs, in_hbm(up_hbm), in_hbm(down_hbm))


def forward(plan, blocks, gate, up_hbm, down_hbm):
    kernel = functools.partial(forward_kernel, plan, len(blocks))
    shape = (plan.mine, plan.expert_rows, plan.hidden)
    scratch = [pltpu.VMEM(shape, F32), pltpu.VMEM(shape, BF16)]
    kept = pltpu.VMEM((plan.kept, plan.hidden, plan.width), BF16)
    shapes = part_shapes(plan, plan.width, 2) + [kept]
    inputs = [*blocks, in_vmem(gate)]
    *parts, kept = expert_call(
        plan, kernel, "forward", inputs, up_hbm, down_hbm, shapes, scratch
    )
    return parts, kept


def backward(plan, blocks, saved, gate, kept, up_hbm, down_hbm):
    kernel = functools.partial(backward_kernel, plan, len(blocks))
    scratch = [
        pltpu.VMEM((plan.rows, plan.meta), BF16),
        pltpu.VMEM((2, plan.mine, plan.expert_rows, plan.hidden), BF16),
    ]
    shapes = part_shapes(plan, plan.half) + part_shapes(plan, plan.sent - plan.half)
    inputs = [*blocks, *saved, in_vmem(gate), in_vmem(kept)]
    parts = expert_call(
        plan, kernel, "backward", inputs, up_hbm, down_hbm, shapes, scratch
    )
    return parts[: len(parts) // 2], parts[len(parts) // 2 :]


def gather_group(plan, block):
    return [block] + [plan.over_expert(block, d) for d in range(1, plan.owners)]


def sum_pair(plan, parts):
    own = [[p] for p in parts[: plan.owners]]
    d = 0
    for piece in parts[plan.owners :]:
        other = plan.over_pair(piece)
        for start in range(0, piece.shape[0], plan.count):
            own[d].append(other[start : start + plan.count])
            d += 1
    return own


def total(terms):
    return sum(t.astype(F32) for t in terms)


def scatter_group(plan, own):
    sent = [total(own[d]).astype(BF16) for d in range(1, plan.owners)]
    return own[0] + [plan.over_expert(x, d, True) for d, x in enumerate(sent, 1)]


def away(plan, step):
    return [d for d in range(0, plan.owners, step) if d & step]


def send_step(plan, own, step):
    sent = [total(own[d]).astype(BF16) for d in away(plan, step)]
    return plan.over_expert(jnp.concatenate(sent), step, True)


def take_step(plan, own, step, back):
    kept = [list(terms) for terms in own]
    for i, d in enumerate(away(plan, step)):
        kept[d ^ step].append(back[i * plan.count : (i + 1) * plan.count])
    return kept


def exchange(plan, own, step):
    return take_step(plan, own, step, send_step(plan, own, step))


def finish_kernel(plan, count, *refs):
    parts, (routes_ref, out_hbm, score_hbm, out_s, score_s, sems) = refs[:count], refs[count:]
    half, rest = plan.half, plan.width - plan.half
    near = total([part[...] for part in parts[: count // 2]])
    far = total([part[...] for part in parts[count // 2 :]])
    out_s[:, :half] = near.astype(BF16)
    out_s[:, half:] = far[:, :rest].astype(BF16)
    out_copy = pltpu.make_async_copy(out_s, out_hbm, sems.at[0])
    out_copy.start()
    shape = (plan.meta, plan.meta)
    same = jnp.where(iota(shape, 0) == iota(shape, 1), 1.0, 0.0).astype(BF16)
    spread = dot_tb(same, far[:, rest:].astype(BF16))
    experts = plan.experts
    score = spread[:experts] + spread[experts : 2 * experts] + spread[2 * experts : 3 * experts]
    row = iota((experts, plan.count), 0)
    for k in range(plan.top):
        hit = row == routes_ref[k : k + 1, :]
        score_s[k : k + 1, :] = jnp.sum(jnp.where(hit, score, 0.0), axis=0, keepdims=True)
    score_copy = pltpu.make_async_copy(score_s, score_hbm, sems.at[1])
    score_copy.start()
    out_copy.wait()
    score_copy.wait()


def finish_back(plan, parts, routes):
    out, score = pl.pallas_call(
        functools.partial(finish_kernel, plan, len(parts)),
        out_shape=(
            jax.ShapeDtypeStruct((plan.count, plan.width), BF16),
            jax.ShapeDtypeStruct((plan.top, plan.count), F32),
        ),
        in_specs=[vmem()] * (len(parts) + 1),
        out_specs=(hbm(), hbm()),
        scratch_shapes=[
            pltpu.VMEM((plan.count, plan.width), BF16),
            pltpu.VMEM((plan.top, plan.count), F32),
            pltpu.SemaphoreType.DMA((2,)),
        ],
        compiler_params=pltpu.CompilerParams(vmem_limit_bytes=8 * MIB),
        name="finish",
    )(*parts, routes.T)
    return out, score.T


def body(
    tokens,
    routes,
    weights_fwd,
    cotangent,
    routes_back,
    weights_back,
    saved_gate,
    saved_up,
    w_gate,
    w_up,
    w_down,
):
    plan = Plan(tokens, routes, saved_gate, w_gate)
    packed = pack(plan, tokens, routes, weights_fwd)
    packed_back, saved, ready = prepare(
        plan, cotangent, routes_back, weights_back, saved_gate, saved_up, packed
    )
    if plan.split > 1:
        saved[1] = plan.over_pair(saved[1])
    gate_hbm, up_hbm = jnp.swapaxes(w_gate, 1, 2), jnp.swapaxes(w_up, 1, 2)
    if plan.paired and plan.owners > 1:
        blocks = [packed, plan.over_expert(packed, 1)]
        gate, done = fetch(plan, gate_hbm, blocks[1], saved[-1])
        step = 2
        while step < plan.owners:
            blocks.append(plan.over_expert(jnp.concatenate(blocks) + ready[:1], step))
            step *= 2
    else:
        blocks = gather_group(plan, packed)
        gate, done = fetch(plan, gate_hbm, packed, saved[-1])
    if plan.split > 1:
        blocks.append(plan.over_pair(jnp.concatenate(blocks) + done[:1]))
    blocks_back = gather_group(plan, packed_back)
    parts, kept = forward(plan, blocks, gate, up_hbm, w_down)
    parts, blocks_back = lax.optimization_barrier((parts, blocks_back))
    if plan.split > 1:
        blocks_back = blocks_back + [plan.over_pair(jnp.concatenate(blocks_back))]
    own = sum_pair(plan, parts)
    steps = [1 << i for i in range(plan.owners.bit_length() - 1)] if plan.paired else []
    back = send_step(plan, own, 1) if steps else scatter_group(plan, own)
    parts_back = backward(plan, blocks_back, saved, gate, kept, up_hbm, w_down)
    parts_back, back = lax.optimization_barrier((parts_back, back))
    near, far = [sum_pair(plan, half) for half in parts_back]
    if steps:
        own = take_step(plan, own, 1, back)
        for step in steps[1:-1]:
            own = exchange(plan, own, step)
        back = send_step(plan, own, steps[-1])
        near_back, far_back = send_step(plan, near, 1), send_step(plan, far, 1)
        near_back, back = lax.optimization_barrier((near_back, back))
        own = take_step(plan, own, steps[-1], back)
        near, far = take_step(plan, near, 1, near_back), take_step(plan, far, 1, far_back)
        for step in steps[1:]:
            near, far = exchange(plan, near, step), exchange(plan, far, step)
    else:
        own, near, far = [back], [scatter_group(plan, near)], [scatter_group(plan, far)]
    mixed = total(own[0]).astype(BF16)
    input_grad, weight_grad = finish_back(plan, near[0] + far[0], routes_back)
    return (mixed, input_grad, weight_grad)


def solution(mesh):
    spec = P(("dp", "expert"), None)
    saved = P("dp", None, "expert", None, None)
    weight = P("expert", None, None)
    return jax.shard_map(
        body,
        mesh=mesh,
        in_specs=(spec,) * 6 + (saved,) * 2 + (weight,) * 3,
        out_specs=(spec,) * 3,
        check_vma=False,
    )
```

```python
import functools
import jax
import jax.numpy as jnp
from jax import lax
from jax.experimental import pallas as pl
from jax.experimental.pallas import tpu as pltpu
from jax.sharding import PartitionSpec as P

F32 = jnp.float32
BF16 = jnp.bfloat16
LANES = 128
MIB = 1 << 20


def round_up(value, unit):
    return -(-value // unit) * unit


def dot(a, b):
    return jnp.dot(a, b, preferred_element_type=F32)


def dot_tb(a, b):
    return lax.dot_general(a, b, (((1,), (1,)), ((), ())), preferred_element_type=F32)


def dot_ta(a, b):
    return lax.dot_general(a, b, (((0,), (0,)), ((), ())), preferred_element_type=F32)


def iota(shape, dim):
    return lax.broadcasted_iota(jnp.int32, shape, dim)


def vmem():
    return pl.BlockSpec(memory_space=pltpu.VMEM)


def hbm():
    return pl.BlockSpec(memory_space=pltpu.HBM)


def in_vmem(x):
    return pltpu.with_memory_space_constraint(x, pltpu.VMEM)


def in_hbm(x):
    return pltpu.with_memory_space_constraint(x, pltpu.HBM)


class Plan:
    def __init__(self, tokens, routes, saved_gate, w_gate):
        self.owners = lax.axis_size("expert")
        self.groups = lax.axis_size("dp")
        self.count, self.width = tokens.shape
        self.top = routes.shape[1]
        self.local = w_gate.shape[0]
        self.hidden = w_gate.shape[2]
        self.experts = self.owners * self.local
        self.cap = saved_gate.shape[3]
        self.cap_rows = round_up(self.cap, 8)
        self.split = 2 if self.groups % 2 == 0 and self.local % 2 == 0 else 1
        self.mine = self.local // self.split
        self.meta = round_up(3 * self.experts, LANES)
        self.blocks = self.split * self.owners
        self.source_rows = self.owners * self.cap_rows
        self.expert_rows = self.split * self.source_rows
        self.paired = self.owners & (self.owners - 1) == 0
        self.sent = self.width + self.meta
        self.half = round_up(self.width // 2, LANES)
        self.kept = min(self.mine, 2)
        self.rows = self.mine * self.expert_rows
        self.cols = self.blocks * self.count

    def peer(self, index, step, core):
        bits = self.owners.bit_length() - 1
        if self.owners != 1 << bits:
            return (index + step) % self.owners
        turned = sum(((step >> i) & 1) << (bits - 1 - i) for i in range(bits))
        return index ^ (step + (turned - step) * core)

    def over_expert(self, x, step, back=False):
        pairs = []
        for group in range(self.groups):
            for i in range(self.owners):
                near = group * self.owners + i
                far = self.peer(i, step, group % self.split) + group * self.owners
                pairs.append((near, far) if back else (far, near))
        return lax.ppermute(x, ("dp", "expert"), pairs)

    def over_pair(self, x):
        return lax.ppermute(x, "dp", [(i, i ^ 1) for i in range(self.groups)])


def pack_body(plan, sources, out_ref, routes_ref, factors_ref, sems):
    x_hbm, routes_hbm, factors_hbm = sources
    experts, count = plan.experts, plan.count
    rows = pltpu.make_async_copy(x_hbm, out_ref.at[:, : plan.width], sems.at[0])
    small = [
        pltpu.make_async_copy(routes_hbm, routes_ref, sems.at[1]),
        pltpu.make_async_copy(factors_hbm, factors_ref, sems.at[2]),
    ]
    for copy in (*small, rows):
        copy.start()
    for copy in small:
        copy.wait()
    lane = iota((plan.meta, count), 0)
    chosen = jnp.zeros((plan.meta, count), F32)
    parts = jnp.zeros((plan.meta, count), F32)
    for k in range(plan.top):
        route = routes_ref[k : k + 1, :]
        factor = factors_ref[k : k + 1, :]
        high = factor.astype(BF16).astype(F32)
        low = factor - high
        chosen = chosen + jnp.where(lane == route, 1.0, 0.0)
        parts = parts + jnp.where(lane == route + experts, high, 0.0)
        parts = parts + jnp.where(lane == route + 2 * experts, low, 0.0)
    earlier = jnp.where(iota((count, count), 0) < iota((count, count), 1), 1.0, 0.0)
    before = dot(chosen.astype(BF16), earlier.astype(BF16))
    facts = (chosen * (before + 1.0) + parts).astype(BF16)
    shape = (plan.meta, plan.meta)
    same = jnp.where(iota(shape, 0) == iota(shape, 1), 1.0, 0.0).astype(BF16)
    out_ref[:, plan.width :] = dot_ta(facts, same).astype(BF16)
    rows.wait()


def pack_scratch(plan):
    return [
        pltpu.VMEM((plan.top, plan.count), jnp.int32),
        pltpu.VMEM((plan.top, plan.count), F32),
        pltpu.SemaphoreType.DMA((3,)),
    ]


def pack_kernel(plan, *refs):
    pack_body(plan, refs[:3], *refs[3:])


def pack(plan, x, routes, factors):
    return pl.pallas_call(
        functools.partial(pack_kernel, plan),
        out_shape=jax.ShapeDtypeStruct((plan.count, plan.sent), BF16),
        in_specs=[hbm()] * 3,
        out_specs=vmem(),
        scratch_shapes=pack_scratch(plan),
        compiler_params=pltpu.CompilerParams(vmem_limit_bytes=4 * MIB),
        name="pack",
    )(in_hbm(x), in_hbm(routes.T), in_hbm(factors.T))


def first_expert(plan):
    core = lax.rem(lax.axis_index("dp"), plan.split)
    return lax.axis_index("expert") * plan.local + core * plan.mine, core * plan.mine


def tables(plan, meta, first):
    me = lax.axis_index("expert")
    core = lax.rem(lax.axis_index("dp"), plan.split)
    row = iota((plan.rows, 1), 0)
    place = row % plan.expert_rows
    expert = first + row // plan.expert_rows
    wanted_slot = (row % plan.cap_rows + 1).astype(F32)
    wanted_block = place // plan.cap_rows
    lane = iota((1, plan.meta), 1)
    pick_slot = jnp.where(lane == expert, 1.0, 0.0).astype(BF16)
    pick_part = (lane == expert + plan.experts) | (lane == expert + 2 * plan.experts)
    slot = dot_tb(pick_slot, meta)
    part = dot_tb(jnp.where(pick_part, 1.0, 0.0).astype(BF16), meta)
    block = iota((1, plan.cols), 1) // plan.count
    group = block // plan.owners
    source = plan.peer(me, block % plan.owners, core ^ group)
    hit = (wanted_block == group * plan.owners + source) & (slot == wanted_slot)
    factor = jnp.sum(jnp.where(hit, part, 0.0), axis=1, keepdims=True)
    return jnp.where(hit, 1.0, 0.0).astype(BF16), factor


def weight_copies(plan, array, slots, sems):
    offset = first_expert(plan)[1]
    return [
        pltpu.make_async_copy(array.at[offset + e], slot, sems.at[e])
        for e, slot in enumerate(slots)
    ]


def weight_slots(plan, *refs):
    return [ref.at[e] for ref in refs for e in range(ref.shape[0])][: plan.mine]


def prepare_kernel(plan, x_hbm, routes_hbm, factors_hbm, gate_hbm, up_hbm, after, *refs):
    packed_ref, done_ref, own_ref = refs[:3]
    other_ref = refs[3] if plan.split > 1 else None
    gate_s, up_s, saved_sems, routes_ref, factors_ref, pack_sems = refs[plan.split + 2 :]
    done_ref[...] = jnp.zeros_like(done_ref)
    saved = [
        pltpu.make_async_copy(gate_hbm, gate_s, saved_sems.at[0]),
        pltpu.make_async_copy(up_hbm, up_s, saved_sems.at[1]),
    ]
    for copy in saved:
        copy.start()
    sources = x_hbm, routes_hbm, factors_hbm
    pack_body(plan, sources, packed_ref, routes_ref, factors_ref, pack_sems)
    _, offset = first_expert(plan)
    shape = (plan.mine * plan.source_rows, gate_s.shape[0])
    row, col = iota(shape, 0), iota(shape, 1)
    slot = row % plan.cap_rows
    source = row % plan.source_rows // plan.cap_rows
    place = (source * plan.cap + slot) * plan.local + row // plan.source_rows
    place = jnp.where(slot < plan.cap, place, -plan.local)

    def pick(start, ref):
        table = jnp.where(col == place + start, 1.0, 0.0).astype(BF16)
        return dot(table, ref[...]).astype(BF16)

    for copy in saved:
        copy.wait()
    own_ref[0] = pick(offset, gate_s)
    own_ref[1] = pick(offset, up_s)
    if other_ref is not None:
        other_ref[0] = pick(plan.mine - offset, gate_s)
        other_ref[1] = pick(plan.mine - offset, up_s)


def prepare(plan, x, routes, factors, saved_gate, saved_up, after):
    flat = (plan.owners * plan.cap * plan.local, plan.hidden)

    def flatten(saved):
        return in_hbm(jnp.swapaxes(saved[0], 1, 2).reshape(flat))

    part = jax.ShapeDtypeStruct((2, plan.mine * plan.source_rows, plan.hidden), BF16)
    packed_shape = jax.ShapeDtypeStruct((plan.count, plan.sent), BF16)
    done_shape = jax.ShapeDtypeStruct((16, plan.sent), BF16)
    out_shape = [packed_shape, done_shape] + [part] * plan.split
    packed, done, *saved = pl.pallas_call(
        functools.partial(prepare_kernel, plan),
        out_shape=out_shape,
        in_specs=[hbm()] * 5 + [pl.BlockSpec(memory_space=pl.ANY)],
        out_specs=[vmem()] * len(out_shape),
        scratch_shapes=[
            pltpu.VMEM(flat, BF16),
            pltpu.VMEM(flat, BF16),
            pltpu.SemaphoreType.DMA((2,)),
            *pack_scratch(plan),
        ],
        compiler_params=pltpu.CompilerParams(vmem_limit_bytes=8 * MIB),
        cost_estimate=pl.CostEstimate(
            flops=0, bytes_accessed=plan.owners * plan.width * plan.sent, transcendentals=0
        ),
        name="prepare",
    )(
        in_hbm(x),
        in_hbm(routes.T),
        in_hbm(factors.T),
        flatten(saved_gate),
        flatten(saved_up),
        after,
    )
    return packed, saved, done


def fetch_kernel(plan, w_hbm, after, also_after, w_ref, done_ref, sems):
    copies = weight_copies(plan, w_hbm, weight_slots(plan, w_ref), sems)
    for copy in copies:
        copy.start()
    done_ref[...] = jnp.zeros_like(done_ref)
    for copy in copies:
        copy.wait()


def fetch(plan, w, after, also_after):
    return pl.pallas_call(
        functools.partial(fetch_kernel, plan),
        out_shape=(
            pltpu.VMEM((plan.mine, plan.hidden, plan.width), BF16),
            jax.ShapeDtypeStruct((16, plan.sent), BF16),
        ),
        in_specs=[hbm()] + [pl.BlockSpec(memory_space=pl.ANY)] * 2,
        out_specs=(vmem(), vmem()),
        scratch_shapes=[pltpu.SemaphoreType.DMA((plan.mine,))],
        compiler_params=pltpu.CompilerParams(vmem_limit_bytes=MIB),
        cost_estimate=pl.CostEstimate(
            flops=0,
            bytes_accessed=2 * plan.mine * plan.hidden * plan.width * 2,
            transcendentals=0,
        ),
        name="fetch",
    )(in_hbm(w), after, also_after)


def arrived(plan, blocks, first, x_s):
    metas = jnp.concatenate([block[:, plan.width :] for block in blocks], axis=0)
    table, factor = tables(plan, metas, first)
    rows = jnp.concatenate([block[:, : plan.width] for block in blocks], axis=0)
    x_s[...] = dot(table, rows).astype(BF16)
    return table, factor


class Queue:
    def __init__(self, copies, ahead):
        self.copies, self.ahead, self.started, self.taken = copies, ahead, 0, 0

    def fill(self):
        limit = min(self.taken + self.ahead, len(self.copies))
        while self.started < limit:
            self.copies[self.started].start()
            self.started += 1

    def take(self, count):
        self.fill()
        for _ in range(count):
            self.copies[self.taken].wait()
            self.taken += 1
        self.fill()


def forward_kernel(plan, count, *refs):
    blocks, refs = refs[:count], refs[count:]
    gate_ref, up_hbm, down_hbm, *refs = refs
    outs, (kept_ref, up_s, down_s, x_s, y_s, gate_s, hidden_s, sems) = refs[:-8], refs[-8:]
    first, _ = first_expert(plan)
    downs = weight_slots(plan, kept_ref, down_s)
    copies = weight_copies(plan, up_hbm, weight_slots(plan, up_s), sems.at[0])
    copies += weight_copies(plan, down_hbm, downs, sems.at[1])
    queue = Queue(copies, 4)
    queue.fill()
    table, factor = arrived(plan, blocks, first, x_s)
    n = plan.expert_rows
    parts = [slice(e * n, (e + 1) * n) for e in range(plan.mine)]
    for e, part in enumerate(parts):
        gate_s[e] = dot_tb(x_s[part, :], gate_ref[e])
    up = None
    for e, part in enumerate(parts):
        if e % 2 == 0:
            queue.take(min(2, plan.mine - e))
        last, up = up, dot_tb(x_s[part, :], up_s[e])
        if e:
            gate = gate_s[e - 1]
            hidden_s[e - 1] = (gate / (1.0 + jnp.exp(-gate)) * last).astype(BF16)
    gate = gate_s[plan.mine - 1]
    hidden_s[plan.mine - 1] = (gate / (1.0 + jnp.exp(-gate)) * up).astype(BF16)
    for e, part in enumerate(parts):
        if e % 2 == 0:
            queue.take(min(2, plan.mine - e))
        out = dot(hidden_s[e], downs[e][...])
        y_s[part, :] = (out * factor[part]).astype(BF16)
    put_rows(outs, slice(None), dot_ta(table, y_s[...]).astype(BF16))


def put_rows(outs, columns, rows):
    start = 0
    for out in outs:
        stop = start + out.shape[0]
        out[:, columns] = rows[start:stop, :]
        start = stop


def backward_kernel(plan, count, *refs):
    blocks, refs = refs[:count], refs[count:]
    saved_ref, other_ref, refs = refs[0], refs[plan.split - 1], refs[plan.split :]
    gate_ref, kept_ref, up_hbm, down_hbm, *refs = refs
    outs, (up_s, down_s, x_s, y_s, score_s, grads_s, sems) = refs[:-7], refs[-7:]
    first, _ = first_expert(plan)
    downs = weight_slots(plan, kept_ref, down_s)
    copies = weight_copies(plan, down_hbm, downs, sems.at[0])[plan.kept :]
    copies += weight_copies(plan, up_hbm, weight_slots(plan, up_s), sems.at[1])
    queue = Queue(copies, 3)
    queue.fill()
    table, factor = arrived(plan, blocks, first, x_s)
    n, held = plan.expert_rows, plan.source_rows
    lane = iota((n, plan.meta), 1)
    parts = [slice(e * n, (e + 1) * n) for e in range(plan.mine)]

    def through_activation(e, grad):
        own = slice(e * held, (e + 1) * held)
        act, up = saved_ref[0, own, :], saved_ref[1, own, :]
        if plan.split > 1:
            act = jnp.concatenate([act, other_ref[0, own, :]], axis=0)
            up = jnp.concatenate([up, other_ref[1, own, :]], axis=0)
        act, up = act.astype(F32), up.astype(F32)
        sig = 1.0 / (1.0 + jnp.exp(-act))
        silu = act * sig
        score = jnp.sum(silu * up * grad, axis=1, keepdims=True)
        grads_s[0, e] = (grad * up * sig * (1.0 + act * (1.0 - sig))).astype(BF16)
        grads_s[1, e] = (grad * silu).astype(BF16)
        expert = first + e
        high = score.astype(BF16).astype(F32)
        middle = (score - high).astype(BF16).astype(F32)
        low = score - high - middle
        spread = jnp.where(lane == expert, high, 0.0)
        spread = jnp.where(lane == expert + plan.experts, middle, spread)
        spread = jnp.where(lane == expert + 2 * plan.experts, low, spread)
        score_s[parts[e], :] = spread.astype(BF16)

    grad = None
    for e, part in enumerate(parts):
        if e >= plan.kept:
            queue.take(1)
        last, grad = grad, dot_tb(x_s[part, :], downs[e][...])
        if e:
            through_activation(e - 1, last)
    through_activation(plan.mine - 1, grad)
    for e, part in enumerate(parts):
        queue.take(1)
        result = dot(grads_s[0, e], gate_ref[e]) + dot(grads_s[1, e], up_s[e])
        y_s[part, :] = (result * factor[part]).astype(BF16)
    half, near = plan.half, outs[: len(outs) // 2]
    far = outs[len(outs) // 2 :]
    put_rows(near, slice(0, half), dot_ta(table, y_s[:, :half]).astype(BF16))
    rest = plan.width - half
    put_rows(far, slice(0, rest), dot_ta(table, y_s[:, half:]).astype(BF16))
    scores = dot_ta(table, score_s[...]).astype(BF16)
    put_rows(far, slice(rest, rest + plan.meta), scores)


def part_shapes(plan, width, pieces=1):
    block = jax.ShapeDtypeStruct((plan.count, width), BF16)
    pieces = pieces if plan.owners % pieces == 0 else 1
    rows = plan.owners * plan.count // pieces
    other = jax.ShapeDtypeStruct((rows, width), BF16)
    return [block] * plan.owners + [other] * ((plan.split - 1) * pieces)


def expert_call(plan, kernel, name, inputs, up_hbm, down_hbm, shapes, scratch):
    def weight(count):
        return pltpu.VMEM((count, plan.hidden, plan.width), BF16)

    rows = pltpu.VMEM((plan.rows, plan.width), BF16)
    return pl.pallas_call(
        kernel,
        out_shape=shapes,
        in_specs=[vmem()] * len(inputs) + [hbm()] * 2,
        out_specs=[vmem()] * len(shapes),
        scratch_shapes=[
            *[weight(plan.mine), weight(max(plan.mine - plan.kept, 1)), rows, rows],
            *scratch,
            pltpu.SemaphoreType.DMA((2, plan.mine)),
        ],
        compiler_params=pltpu.CompilerParams(vmem_limit_bytes=31 * MIB),
        cost_estimate=pl.CostEstimate(
            flops=2 * 3 * plan.mine * plan.expert_rows * plan.width * plan.hidden,
            bytes_accessed=2 * 2 * plan.mine * plan.width * plan.hidden,
            transcendentals=0,
        ),
        name=name,
    )(*inputs, in_hbm(up_hbm), in_hbm(down_hbm))


def forward(plan, blocks, gate, up_hbm, down_hbm):
    kernel = functools.partial(forward_kernel, plan, len(blocks))
    shape = (plan.mine, plan.expert_rows, plan.hidden)
    scratch = [pltpu.VMEM(shape, F32), pltpu.VMEM(shape, BF16)]
    kept = pltpu.VMEM((plan.kept, plan.hidden, plan.width), BF16)
    shapes = part_shapes(plan, plan.width, 2) + [kept]
    inputs = [*blocks, in_vmem(gate)]
    *parts, kept = expert_call(
        plan, kernel, "forward", inputs, up_hbm, down_hbm, shapes, scratch
    )
    return parts, kept


def backward(plan, blocks, saved, gate, kept, up_hbm, down_hbm):
    kernel = functools.partial(backward_kernel, plan, len(blocks))
    scratch = [
        pltpu.VMEM((plan.rows, plan.meta), BF16),
        pltpu.VMEM((2, plan.mine, plan.expert_rows, plan.hidden), BF16),
    ]
    shapes = part_shapes(plan, plan.half) + part_shapes(plan, plan.sent - plan.half)
    inputs = [*blocks, *saved, in_vmem(gate), in_vmem(kept)]
    parts = expert_call(
        plan, kernel, "backward", inputs, up_hbm, down_hbm, shapes, scratch
    )
    return parts[: len(parts) // 2], parts[len(parts) // 2 :]


def gather_group(plan, block):
    return [block] + [plan.over_expert(block, d) for d in range(1, plan.owners)]


def sum_pair(plan, parts):
    own = [[p] for p in parts[: plan.owners]]
    d = 0
    for piece in parts[plan.owners :]:
        other = plan.over_pair(piece)
        for start in range(0, piece.shape[0], plan.count):
            own[d].append(other[start : start + plan.count])
            d += 1
    return own


def total(terms):
    return sum(t.astype(F32) for t in terms)


def scatter_group(plan, own):
    sent = [total(own[d]).astype(BF16) for d in range(1, plan.owners)]
    return own[0] + [plan.over_expert(x, d, True) for d, x in enumerate(sent, 1)]


def away(plan, step):
    return [d for d in range(0, plan.owners, step) if d & step]


def send_step(plan, own, step):
    sent = [total(own[d]).astype(BF16) for d in away(plan, step)]
    return plan.over_expert(jnp.concatenate(sent), step, True)


def take_step(plan, own, step, back):
    kept = [list(terms) for terms in own]
    for i, d in enumerate(away(plan, step)):
        kept[d ^ step].append(back[i * plan.count : (i + 1) * plan.count])
    return kept


def exchange(plan, own, step):
    return take_step(plan, own, step, send_step(plan, own, step))


def finish_kernel(plan, count, *refs):
    parts, (routes_ref, out_hbm, score_hbm, out_s, score_s, sems) = refs[:count], refs[count:]
    half, rest = plan.half, plan.width - plan.half
    near = total([part[...] for part in parts[: count // 2]])
    far = total([part[...] for part in parts[count // 2 :]])
    out_s[:, :half] = near.astype(BF16)
    out_s[:, half:] = far[:, :rest].astype(BF16)
    out_copy = pltpu.make_async_copy(out_s, out_hbm, sems.at[0])
    out_copy.start()
    shape = (plan.meta, plan.meta)
    same = jnp.where(iota(shape, 0) == iota(shape, 1), 1.0, 0.0).astype(BF16)
    spread = dot_tb(same, far[:, rest:].astype(BF16))
    experts = plan.experts
    score = spread[:experts] + spread[experts : 2 * experts] + spread[2 * experts : 3 * experts]
    row = iota((experts, plan.count), 0)
    for k in range(plan.top):
        hit = row == routes_ref[k : k + 1, :]
        score_s[k : k + 1, :] = jnp.sum(jnp.where(hit, score, 0.0), axis=0, keepdims=True)
    score_copy = pltpu.make_async_copy(score_s, score_hbm, sems.at[1])
    score_copy.start()
    out_copy.wait()
    score_copy.wait()


def finish_back(plan, parts, routes):
    out, score = pl.pallas_call(
        functools.partial(finish_kernel, plan, len(parts)),
        out_shape=(
            jax.ShapeDtypeStruct((plan.count, plan.width), BF16),
            jax.ShapeDtypeStruct((plan.top, plan.count), F32),
        ),
        in_specs=[vmem()] * (len(parts) + 1),
        out_specs=(hbm(), hbm()),
        scratch_shapes=[
            pltpu.VMEM((plan.count, plan.width), BF16),
            pltpu.VMEM((plan.top, plan.count), F32),
            pltpu.SemaphoreType.DMA((2,)),
        ],
        compiler_params=pltpu.CompilerParams(vmem_limit_bytes=8 * MIB),
        name="finish",
    )(*parts, routes.T)
    return out, score.T


def body(
    tokens,
    routes,
    weights_fwd,
    cotangent,
    routes_back,
    weights_back,
    saved_gate,
    saved_up,
    w_gate,
    w_up,
    w_down,
):
    plan = Plan(tokens, routes, saved_gate, w_gate)
    packed = pack(plan, tokens, routes, weights_fwd)
    packed_back, saved, ready = prepare(
        plan, cotangent, routes_back, weights_back, saved_gate, saved_up, packed
    )
    if plan.split > 1:
        saved[1] = plan.over_pair(saved[1])
    gate_hbm, up_hbm = jnp.swapaxes(w_gate, 1, 2), jnp.swapaxes(w_up, 1, 2)
    if plan.paired and plan.owners > 1:
        blocks = [packed, plan.over_expert(packed, 1)]
        gate, done = fetch(plan, gate_hbm, blocks[1], saved[-1])
        step = 2
        while step < plan.owners:
            blocks.append(plan.over_expert(jnp.concatenate(blocks) + ready[:1], step))
            step *= 2
    else:
        blocks = gather_group(plan, packed)
        gate, done = fetch(plan, gate_hbm, packed, saved[-1])
    if plan.split > 1:
        blocks.append(plan.over_pair(jnp.concatenate(blocks) + done[:1]))
    blocks_back = gather_group(plan, packed_back)
    parts, kept = forward(plan, blocks, gate, up_hbm, w_down)
    parts, blocks_back = lax.optimization_barrier((parts, blocks_back))
    if plan.split > 1:
        blocks_back = blocks_back + [plan.over_pair(jnp.concatenate(blocks_back))]
    own = sum_pair(plan, parts)
    steps = [1 << i for i in range(plan.owners.bit_length() - 1)] if plan.paired else []
    back = send_step(plan, own, 1) if steps else scatter_group(plan, own)
    parts_back = backward(plan, blocks_back, saved, gate, kept, up_hbm, w_down)
    parts_back, back = lax.optimization_barrier((parts_back, back))
    near, far = [sum_pair(plan, half) for half in parts_back]
    if steps:
        own = take_step(plan, own, 1, back)
        for step in steps[1:-1]:
            own = exchange(plan, own, step)
        back = send_step(plan, own, steps[-1])
        near_back, far_back = send_step(plan, near, 1), send_step(plan, far, 1)
        near_back, back = lax.optimization_barrier((near_back, back))
        own = take_step(plan, own, steps[-1], back)
        near, far = take_step(plan, near, 1, near_back), take_step(plan, far, 1, far_back)
        for step in steps[1:]:
            near, far = exchange(plan, near, step), exchange(plan, far, step)
    else:
        own, near, far = [back], [scatter_group(plan, near)], [scatter_group(plan, far)]
    mixed = total(own[0]).astype(BF16)
    input_grad, weight_grad = finish_back(plan, near[0] + far[0], routes_back)
    return (mixed, input_grad, weight_grad)


def solution(mesh):
    spec = P(("dp", "expert"), None)
    saved = P("dp", None, "expert", None, None)
    weight = P("expert", None, None)
    return jax.shard_map(
        body,
        mesh=mesh,
        in_specs=(spec,) * 6 + (saved,) * 2 + (weight,) * 3,
        out_specs=(spec,) * 3,
        check_vma=False,
    )
```

```python
import functools
import jax
import jax.numpy as jnp
from jax import lax
from jax.experimental import pallas as pl
from jax.experimental.pallas import tpu as pltpu
from jax.sharding import PartitionSpec as P

F32 = jnp.float32
BF16 = jnp.bfloat16
LANES = 128
MIB = 1 << 20


def round_up(value, unit):
    return -(-value // unit) * unit


def dot(a, b):
    return jnp.dot(a, b, preferred_element_type=F32)


def dot_tb(a, b):
    return lax.dot_general(a, b, (((1,), (1,)), ((), ())), preferred_element_type=F32)


def dot_ta(a, b):
    return lax.dot_general(a, b, (((0,), (0,)), ((), ())), preferred_element_type=F32)


def iota(shape, dim):
    return lax.broadcasted_iota(jnp.int32, shape, dim)


def vmem():
    return pl.BlockSpec(memory_space=pltpu.VMEM)


def hbm():
    return pl.BlockSpec(memory_space=pltpu.HBM)


def in_vmem(x):
    return pltpu.with_memory_space_constraint(x, pltpu.VMEM)


def in_hbm(x):
    return pltpu.with_memory_space_constraint(x, pltpu.HBM)


class Plan:
    def __init__(self, tokens, routes, saved_gate, w_gate):
        self.owners = lax.axis_size("expert")
        self.groups = lax.axis_size("dp")
        self.count, self.width = tokens.shape
        self.top = routes.shape[1]
        self.local = w_gate.shape[0]
        self.hidden = w_gate.shape[2]
        self.experts = self.owners * self.local
        self.cap = saved_gate.shape[3]
        self.cap_rows = round_up(self.cap, 8)
        self.split = 2 if self.groups % 2 == 0 and self.local % 2 == 0 else 1
        self.mine = self.local // self.split
        self.meta = round_up(3 * self.experts, LANES)
        self.blocks = self.split * self.owners
        self.source_rows = self.owners * self.cap_rows
        self.expert_rows = self.split * self.source_rows
        self.paired = self.owners & (self.owners - 1) == 0
        self.sent = self.width + self.meta
        self.half = round_up(self.width // 2, LANES)
        self.kept = min(self.mine, 2)
        self.order = [*range(1, self.owners, 2), *range(0, self.owners, 2)]
        self.rows = self.mine * self.expert_rows
        self.cols = self.blocks * self.count

    def peer(self, index, step, core):
        bits = self.owners.bit_length() - 1
        if self.owners != 1 << bits:
            return (index + step) % self.owners
        turned = sum(((step >> i) & 1) << (bits - 1 - i) for i in range(bits))
        return index ^ (step + (turned - step) * core)

    def over_expert(self, x, step, back=False):
        pairs = []
        for group in range(self.groups):
            for i in range(self.owners):
                near = group * self.owners + i
                far = self.peer(i, step, group % self.split) + group * self.owners
                pairs.append((near, far) if back else (far, near))
        return lax.ppermute(x, ("dp", "expert"), pairs)

    def over_pair(self, x):
        return lax.ppermute(x, "dp", [(i, i ^ 1) for i in range(self.groups)])


def pack_body(plan, sources, out_ref, routes_ref, factors_ref, sems):
    x_hbm, routes_hbm, factors_hbm = sources
    experts, count = plan.experts, plan.count
    rows = pltpu.make_async_copy(x_hbm, out_ref.at[:, : plan.width], sems.at[0])
    small = [
        pltpu.make_async_copy(routes_hbm, routes_ref, sems.at[1]),
        pltpu.make_async_copy(factors_hbm, factors_ref, sems.at[2]),
    ]
    for copy in (*small, rows):
        copy.start()
    for copy in small:
        copy.wait()
    lane = iota((plan.meta, count), 0)
    chosen = jnp.zeros((plan.meta, count), F32)
    parts = jnp.zeros((plan.meta, count), F32)
    for k in range(plan.top):
        route = routes_ref[k : k + 1, :]
        factor = factors_ref[k : k + 1, :]
        high = factor.astype(BF16).astype(F32)
        low = factor - high
        chosen = chosen + jnp.where(lane == route, 1.0, 0.0)
        parts = parts + jnp.where(lane == route + experts, high, 0.0)
        parts = parts + jnp.where(lane == route + 2 * experts, low, 0.0)
    earlier = jnp.where(iota((count, count), 0) < iota((count, count), 1), 1.0, 0.0)
    before = dot(chosen.astype(BF16), earlier.astype(BF16))
    facts = (chosen * (before + 1.0) + parts).astype(BF16)
    shape = (plan.meta, plan.meta)
    same = jnp.where(iota(shape, 0) == iota(shape, 1), 1.0, 0.0).astype(BF16)
    out_ref[:, plan.width :] = dot_ta(facts, same).astype(BF16)
    rows.wait()


def pack_scratch(plan):
    return [
        pltpu.VMEM((plan.top, plan.count), jnp.int32),
        pltpu.VMEM((plan.top, plan.count), F32),
        pltpu.SemaphoreType.DMA((3,)),
    ]


def pack_kernel(plan, *refs):
    pack_body(plan, refs[:3], *refs[3:])


def pack(plan, x, routes, factors):
    return pl.pallas_call(
        functools.partial(pack_kernel, plan),
        out_shape=jax.ShapeDtypeStruct((plan.count, plan.sent), BF16),
        in_specs=[hbm()] * 3,
        out_specs=vmem(),
        scratch_shapes=pack_scratch(plan),
        compiler_params=pltpu.CompilerParams(vmem_limit_bytes=4 * MIB),
        name="pack",
    )(in_hbm(x), in_hbm(routes.T), in_hbm(factors.T))


def first_expert(plan):
    core = lax.rem(lax.axis_index("dp"), plan.split)
    return lax.axis_index("expert") * plan.local + core * plan.mine, core * plan.mine


def tables(plan, meta, first):
    me = lax.axis_index("expert")
    core = lax.rem(lax.axis_index("dp"), plan.split)
    row = iota((plan.rows, 1), 0)
    place = row % plan.expert_rows
    expert = first + row // plan.expert_rows
    wanted_slot = (row % plan.cap_rows + 1).astype(F32)
    wanted_block = place // plan.cap_rows
    lane = iota((1, plan.meta), 1)
    pick_slot = jnp.where(lane == expert, 1.0, 0.0).astype(BF16)
    pick_part = (lane == expert + plan.experts) | (lane == expert + 2 * plan.experts)
    slot = dot_tb(pick_slot, meta)
    part = dot_tb(jnp.where(pick_part, 1.0, 0.0).astype(BF16), meta)
    block = iota((1, plan.cols), 1) // plan.count
    group = block // plan.owners
    source = plan.peer(me, block % plan.owners, core ^ group)
    hit = (wanted_block == group * plan.owners + source) & (slot == wanted_slot)
    factor = jnp.sum(jnp.where(hit, part, 0.0), axis=1, keepdims=True)
    return jnp.where(hit, 1.0, 0.0).astype(BF16), factor


def weight_copies(plan, array, slots, sems):
    offset = first_expert(plan)[1]
    return [
        pltpu.make_async_copy(array.at[offset + e], slot, sems.at[e])
        for e, slot in enumerate(slots)
    ]


def weight_slots(plan, *refs):
    return [ref.at[e] for ref in refs for e in range(ref.shape[0])][: plan.mine]


def prepare_kernel(plan, x_hbm, routes_hbm, factors_hbm, gate_hbm, up_hbm, after, *refs):
    packed_ref, done_ref, own_ref = refs[:3]
    other_ref = refs[3] if plan.split > 1 else None
    gate_s, up_s, saved_sems, routes_ref, factors_ref, pack_sems = refs[plan.split + 2 :]
    done_ref[...] = jnp.zeros_like(done_ref)
    saved = [
        pltpu.make_async_copy(gate_hbm, gate_s, saved_sems.at[0]),
        pltpu.make_async_copy(up_hbm, up_s, saved_sems.at[1]),
    ]
    for copy in saved:
        copy.start()
    sources = x_hbm, routes_hbm, factors_hbm
    pack_body(plan, sources, packed_ref, routes_ref, factors_ref, pack_sems)
    _, offset = first_expert(plan)
    shape = (plan.mine * plan.source_rows, gate_s.shape[0])
    row, col = iota(shape, 0), iota(shape, 1)
    slot = row % plan.cap_rows
    source = row % plan.source_rows // plan.cap_rows
    place = (source * plan.cap + slot) * plan.local + row // plan.source_rows
    place = jnp.where(slot < plan.cap, place, -plan.local)

    def pick(start, ref):
        table = jnp.where(col == place + start, 1.0, 0.0).astype(BF16)
        return dot(table, ref[...]).astype(BF16)

    for copy in saved:
        copy.wait()
    own_ref[0] = pick(offset, gate_s)
    own_ref[1] = pick(offset, up_s)
    if other_ref is not None:
        other_ref[0] = pick(plan.mine - offset, gate_s)
        other_ref[1] = pick(plan.mine - offset, up_s)


def prepare(plan, x, routes, factors, saved_gate, saved_up, after):
    flat = (plan.owners * plan.cap * plan.local, plan.hidden)

    def flatten(saved):
        return in_hbm(jnp.swapaxes(saved[0], 1, 2).reshape(flat))

    part = jax.ShapeDtypeStruct((2, plan.mine * plan.source_rows, plan.hidden), BF16)
    packed_shape = jax.ShapeDtypeStruct((plan.count, plan.sent), BF16)
    done_shape = jax.ShapeDtypeStruct((16, plan.sent), BF16)
    out_shape = [packed_shape, done_shape] + [part] * plan.split
    packed, done, *saved = pl.pallas_call(
        functools.partial(prepare_kernel, plan),
        out_shape=out_shape,
        in_specs=[hbm()] * 5 + [pl.BlockSpec(memory_space=pl.ANY)],
        out_specs=[vmem()] * len(out_shape),
        scratch_shapes=[
            pltpu.VMEM(flat, BF16),
            pltpu.VMEM(flat, BF16),
            pltpu.SemaphoreType.DMA((2,)),
            *pack_scratch(plan),
        ],
        compiler_params=pltpu.CompilerParams(vmem_limit_bytes=8 * MIB),
        cost_estimate=pl.CostEstimate(
            flops=0, bytes_accessed=plan.owners * plan.width * plan.sent, transcendentals=0
        ),
        name="prepare",
    )(
        in_hbm(x),
        in_hbm(routes.T),
        in_hbm(factors.T),
        flatten(saved_gate),
        flatten(saved_up),
        after,
    )
    return packed, saved, done


def fetch_kernel(plan, w_hbm, after, also_after, w_ref, done_ref, sems):
    copies = weight_copies(plan, w_hbm, weight_slots(plan, w_ref), sems)
    for copy in copies:
        copy.start()
    done_ref[...] = jnp.zeros_like(done_ref)
    for copy in copies:
        copy.wait()


def fetch(plan, w, after, also_after):
    return pl.pallas_call(
        functools.partial(fetch_kernel, plan),
        out_shape=(
            pltpu.VMEM((plan.mine, plan.hidden, plan.width), BF16),
            jax.ShapeDtypeStruct((16, plan.sent), BF16),
        ),
        in_specs=[hbm()] + [pl.BlockSpec(memory_space=pl.ANY)] * 2,
        out_specs=(vmem(), vmem()),
        scratch_shapes=[pltpu.SemaphoreType.DMA((plan.mine,))],
        compiler_params=pltpu.CompilerParams(vmem_limit_bytes=MIB),
        cost_estimate=pl.CostEstimate(
            flops=0,
            bytes_accessed=2 * plan.mine * plan.hidden * plan.width * 2,
            transcendentals=0,
        ),
        name="fetch",
    )(in_hbm(w), after, also_after)


def arrived(plan, blocks, first, x_s):
    metas = jnp.concatenate([block[:, plan.width :] for block in blocks], axis=0)
    table, factor = tables(plan, metas, first)
    rows = jnp.concatenate([block[:, : plan.width] for block in blocks], axis=0)
    x_s[...] = dot(table, rows).astype(BF16)
    return table, factor


class Queue:
    def __init__(self, copies, ahead):
        self.copies, self.ahead, self.started, self.taken = copies, ahead, 0, 0

    def fill(self):
        limit = min(self.taken + self.ahead, len(self.copies))
        while self.started < limit:
            self.copies[self.started].start()
            self.started += 1

    def take(self, count):
        self.fill()
        for _ in range(count):
            self.copies[self.taken].wait()
            self.taken += 1
        self.fill()


def forward_kernel(plan, count, *refs):
    blocks, refs = refs[:count], refs[count:]
    gate_ref, up_hbm, down_hbm, *refs = refs
    outs, (kept_ref, up_s, down_s, x_s, y_s, gate_s, hidden_s, sems) = refs[:-8], refs[-8:]
    first, _ = first_expert(plan)
    downs = weight_slots(plan, kept_ref, down_s)
    copies = weight_copies(plan, up_hbm, weight_slots(plan, up_s), sems.at[0])
    copies += weight_copies(plan, down_hbm, downs, sems.at[1])
    queue = Queue(copies, 4)
    queue.fill()
    table, factor = arrived(plan, blocks, first, x_s)
    n = plan.expert_rows
    parts = [slice(e * n, (e + 1) * n) for e in range(plan.mine)]
    for e, part in enumerate(parts):
        gate_s[e] = dot_tb(x_s[part, :], gate_ref[e])
    up = None
    for e, part in enumerate(parts):
        if e % 2 == 0:
            queue.take(min(2, plan.mine - e))
        last, up = up, dot_tb(x_s[part, :], up_s[e])
        if e:
            gate = gate_s[e - 1]
            hidden_s[e - 1] = (gate / (1.0 + jnp.exp(-gate)) * last).astype(BF16)
    gate = gate_s[plan.mine - 1]
    hidden_s[plan.mine - 1] = (gate / (1.0 + jnp.exp(-gate)) * up).astype(BF16)
    for e, part in enumerate(parts):
        if e % 2 == 0:
            queue.take(min(2, plan.mine - e))
        out = dot(hidden_s[e], downs[e][...])
        y_s[part, :] = (out * factor[part]).astype(BF16)
    mixed = dot_ta(table, y_s[...]).astype(BF16)
    order = [*range(plan.owners), *[plan.owners + d for d in plan.order]]
    order = order[: plan.blocks]
    mixed = [mixed[b * plan.count : (b + 1) * plan.count, :] for b in order]
    put_rows(outs, slice(None), jnp.concatenate(mixed, axis=0))


def put_rows(outs, columns, rows):
    start = 0
    for out in outs:
        stop = start + out.shape[0]
        out[:, columns] = rows[start:stop, :]
        start = stop


def backward_kernel(plan, count, *refs):
    blocks, refs = refs[:count], refs[count:]
    saved_ref, other_ref, refs = refs[0], refs[plan.split - 1], refs[plan.split :]
    gate_ref, kept_ref, up_hbm, down_hbm, *refs = refs
    outs, (up_s, down_s, x_s, y_s, score_s, grads_s, sems) = refs[:-7], refs[-7:]
    first, _ = first_expert(plan)
    downs = weight_slots(plan, kept_ref, down_s)
    copies = weight_copies(plan, down_hbm, downs, sems.at[0])[plan.kept :]
    copies += weight_copies(plan, up_hbm, weight_slots(plan, up_s), sems.at[1])
    queue = Queue(copies, 3)
    queue.fill()
    table, factor = arrived(plan, blocks, first, x_s)
    n, held = plan.expert_rows, plan.source_rows
    lane = iota((n, plan.meta), 1)
    parts = [slice(e * n, (e + 1) * n) for e in range(plan.mine)]

    def through_activation(e, grad):
        own = slice(e * held, (e + 1) * held)
        act, up = saved_ref[0, own, :], saved_ref[1, own, :]
        if plan.split > 1:
            act = jnp.concatenate([act, other_ref[0, own, :]], axis=0)
            up = jnp.concatenate([up, other_ref[1, own, :]], axis=0)
        act, up = act.astype(F32), up.astype(F32)
        sig = 1.0 / (1.0 + jnp.exp(-act))
        silu = act * sig
        score = jnp.sum(silu * up * grad, axis=1, keepdims=True)
        grads_s[0, e] = (grad * up * sig * (1.0 + act * (1.0 - sig))).astype(BF16)
        grads_s[1, e] = (grad * silu).astype(BF16)
        expert = first + e
        high = score.astype(BF16).astype(F32)
        middle = (score - high).astype(BF16).astype(F32)
        low = score - high - middle
        spread = jnp.where(lane == expert, high, 0.0)
        spread = jnp.where(lane == expert + plan.experts, middle, spread)
        spread = jnp.where(lane == expert + 2 * plan.experts, low, spread)
        score_s[parts[e], :] = spread.astype(BF16)

    grad = None
    for e, part in enumerate(parts):
        if e >= plan.kept:
            queue.take(1)
        last, grad = grad, dot_tb(x_s[part, :], downs[e][...])
        if e:
            through_activation(e - 1, last)
    through_activation(plan.mine - 1, grad)
    for e, part in enumerate(parts):
        queue.take(1)
        result = dot(grads_s[0, e], gate_ref[e]) + dot(grads_s[1, e], up_s[e])
        y_s[part, :] = (result * factor[part]).astype(BF16)
    half, near = plan.half, outs[: len(outs) // 2]
    far = outs[len(outs) // 2 :]
    put_rows(near, slice(0, half), dot_ta(table, y_s[:, :half]).astype(BF16))
    rest = plan.width - half
    put_rows(far, slice(0, rest), dot_ta(table, y_s[:, half:]).astype(BF16))
    scores = dot_ta(table, score_s[...]).astype(BF16)
    put_rows(far, slice(rest, rest + plan.meta), scores)


def part_shapes(plan, width, pieces=1):
    block = jax.ShapeDtypeStruct((plan.count, width), BF16)
    pieces = pieces if plan.owners % pieces == 0 else 1
    rows = plan.owners * plan.count // pieces
    other = jax.ShapeDtypeStruct((rows, width), BF16)
    return [block] * plan.owners + [other] * ((plan.split - 1) * pieces)


def expert_call(plan, kernel, name, inputs, up_hbm, down_hbm, shapes, scratch):
    def weight(count):
        return pltpu.VMEM((count, plan.hidden, plan.width), BF16)

    rows = pltpu.VMEM((plan.rows, plan.width), BF16)
    return pl.pallas_call(
        kernel,
        out_shape=shapes,
        in_specs=[vmem()] * len(inputs) + [hbm()] * 2,
        out_specs=[vmem()] * len(shapes),
        scratch_shapes=[
            *[weight(plan.mine), weight(max(plan.mine - plan.kept, 1)), rows, rows],
            *scratch,
            pltpu.SemaphoreType.DMA((2, plan.mine)),
        ],
        compiler_params=pltpu.CompilerParams(vmem_limit_bytes=31 * MIB),
        cost_estimate=pl.CostEstimate(
            flops=2 * 3 * plan.mine * plan.expert_rows * plan.width * plan.hidden,
            bytes_accessed=2 * 2 * plan.mine * plan.width * plan.hidden,
            transcendentals=0,
        ),
        name=name,
    )(*inputs, in_hbm(up_hbm), in_hbm(down_hbm))


def forward(plan, blocks, gate, up_hbm, down_hbm):
    kernel = functools.partial(forward_kernel, plan, len(blocks))
    shape = (plan.mine, plan.expert_rows, plan.hidden)
    scratch = [pltpu.VMEM(shape, F32), pltpu.VMEM(shape, BF16)]
    kept = pltpu.VMEM((plan.kept, plan.hidden, plan.width), BF16)
    shapes = part_shapes(plan, plan.width, 2) + [kept]
    inputs = [*blocks, in_vmem(gate)]
    *parts, kept = expert_call(
        plan, kernel, "forward", inputs, up_hbm, down_hbm, shapes, scratch
    )
    return parts, kept


def backward(plan, blocks, saved, gate, kept, up_hbm, down_hbm):
    kernel = functools.partial(backward_kernel, plan, len(blocks))
    scratch = [
        pltpu.VMEM((plan.rows, plan.meta), BF16),
        pltpu.VMEM((2, plan.mine, plan.expert_rows, plan.hidden), BF16),
    ]
    shapes = part_shapes(plan, plan.half) + part_shapes(plan, plan.sent - plan.half)
    inputs = [*blocks, *saved, in_vmem(gate), in_vmem(kept)]
    parts = expert_call(
        plan, kernel, "backward", inputs, up_hbm, down_hbm, shapes, scratch
    )
    return parts[: len(parts) // 2], parts[len(parts) // 2 :]


def gather_group(plan, block):
    return [block] + [plan.over_expert(block, d) for d in range(1, plan.owners)]


def sum_pair(plan, parts, order=None):
    own = [[p] for p in parts[: plan.owners]]
    order = iter(order or range(plan.owners))
    for piece in parts[plan.owners :]:
        other = plan.over_pair(piece)
        for start in range(0, piece.shape[0], plan.count):
            own[next(order)].append(other[start : start + plan.count])
    return own


def total(terms):
    return sum(t.astype(F32) for t in terms)


def scatter_group(plan, own):
    sent = [total(own[d]).astype(BF16) for d in range(1, plan.owners)]
    return own[0] + [plan.over_expert(x, d, True) for d, x in enumerate(sent, 1)]


def away(plan, step):
    return [d for d in range(0, plan.owners, step) if d & step]


def send_step(plan, own, step):
    sent = [total(own[d]).astype(BF16) for d in away(plan, step)]
    return plan.over_expert(jnp.concatenate(sent), step, True)


def take_step(plan, own, step, back):
    kept = [list(terms) for terms in own]
    for i, d in enumerate(away(plan, step)):
        kept[d ^ step].append(back[i * plan.count : (i + 1) * plan.count])
    return kept


def exchange(plan, own, step):
    return take_step(plan, own, step, send_step(plan, own, step))


def finish_kernel(plan, count, *refs):
    parts, (routes_ref, out_hbm, score_hbm, out_s, score_s, sems) = refs[:count], refs[count:]
    half, rest = plan.half, plan.width - plan.half
    near = total([part[...] for part in parts[: count // 2]])
    far = total([part[...] for part in parts[count // 2 :]])
    out_s[:, :half] = near.astype(BF16)
    out_s[:, half:] = far[:, :rest].astype(BF16)
    out_copy = pltpu.make_async_copy(out_s, out_hbm, sems.at[0])
    out_copy.start()
    shape = (plan.meta, plan.meta)
    same = jnp.where(iota(shape, 0) == iota(shape, 1), 1.0, 0.0).astype(BF16)
    spread = dot_tb(same, far[:, rest:].astype(BF16))
    experts = plan.experts
    score = spread[:experts] + spread[experts : 2 * experts] + spread[2 * experts : 3 * experts]
    row = iota((experts, plan.count), 0)
    for k in range(plan.top):
        hit = row == routes_ref[k : k + 1, :]
        score_s[k : k + 1, :] = jnp.sum(jnp.where(hit, score, 0.0), axis=0, keepdims=True)
    score_copy = pltpu.make_async_copy(score_s, score_hbm, sems.at[1])
    score_copy.start()
    out_copy.wait()
    score_copy.wait()


def finish_back(plan, parts, routes):
    out, score = pl.pallas_call(
        functools.partial(finish_kernel, plan, len(parts)),
        out_shape=(
            jax.ShapeDtypeStruct((plan.count, plan.width), BF16),
            jax.ShapeDtypeStruct((plan.top, plan.count), F32),
        ),
        in_specs=[vmem()] * (len(parts) + 1),
        out_specs=(hbm(), hbm()),
        scratch_shapes=[
            pltpu.VMEM((plan.count, plan.width), BF16),
            pltpu.VMEM((plan.top, plan.count), F32),
            pltpu.SemaphoreType.DMA((2,)),
        ],
        compiler_params=pltpu.CompilerParams(vmem_limit_bytes=8 * MIB),
        name="finish",
    )(*parts, routes.T)
    return out, score.T


def body(
    tokens,
    routes,
    weights_fwd,
    cotangent,
    routes_back,
    weights_back,
    saved_gate,
    saved_up,
    w_gate,
    w_up,
    w_down,
):
    plan = Plan(tokens, routes, saved_gate, w_gate)
    packed = pack(plan, tokens, routes, weights_fwd)
    packed_back, saved, ready = prepare(
        plan, cotangent, routes_back, weights_back, saved_gate, saved_up, packed
    )
    if plan.split > 1:
        saved[1] = plan.over_pair(saved[1])
    gate_hbm, up_hbm = jnp.swapaxes(w_gate, 1, 2), jnp.swapaxes(w_up, 1, 2)
    if plan.paired and plan.owners > 1:
        blocks = [packed, plan.over_expert(packed, 1)]
        gate, done = fetch(plan, gate_hbm, blocks[1], saved[-1])
        step = 2
        while step < plan.owners:
            blocks.append(plan.over_expert(jnp.concatenate(blocks) + ready[:1], step))
            step *= 2
    else:
        blocks = gather_group(plan, packed)
        gate, done = fetch(plan, gate_hbm, packed, saved[-1])
    if plan.split > 1:
        blocks.append(plan.over_pair(jnp.concatenate(blocks) + done[:1]))
    blocks_back = gather_group(plan, packed_back)
    parts, kept = forward(plan, blocks, gate, up_hbm, w_down)
    parts, blocks_back = lax.optimization_barrier((parts, blocks_back))
    if plan.split > 1:
        blocks_back = blocks_back + [plan.over_pair(jnp.concatenate(blocks_back))]
    own = sum_pair(plan, parts, plan.order)
    steps = [1 << i for i in range(plan.owners.bit_length() - 1)] if plan.paired else []
    back = send_step(plan, own, 1) if steps else scatter_group(plan, own)
    parts_back = backward(plan, blocks_back, saved, gate, kept, up_hbm, w_down)
    parts_back, back = lax.optimization_barrier((parts_back, back))
    near, far = [sum_pair(plan, half) for half in parts_back]
    if steps:
        own = take_step(plan, own, 1, back)
        for step in steps[1:-1]:
            own = exchange(plan, own, step)
        back = send_step(plan, own, steps[-1])
        near_back, far_back = send_step(plan, near, 1), send_step(plan, far, 1)
        near_back, back = lax.optimization_barrier((near_back, back))
        own = take_step(plan, own, steps[-1], back)
        near, far = take_step(plan, near, 1, near_back), take_step(plan, far, 1, far_back)
        for step in steps[1:]:
            near, far = exchange(plan, near, step), exchange(plan, far, step)
    else:
        own, near, far = [back], [scatter_group(plan, near)], [scatter_group(plan, far)]
    mixed = total(own[0]).astype(BF16)
    input_grad, weight_grad = finish_back(plan, near[0] + far[0], routes_back)
    return (mixed, input_grad, weight_grad)


def solution(mesh):
    spec = P(("dp", "expert"), None)
    saved = P("dp", None, "expert", None, None)
    weight = P("expert", None, None)
    return jax.shard_map(
        body,
        mesh=mesh,
        in_specs=(spec,) * 6 + (saved,) * 2 + (weight,) * 3,
        out_specs=(spec,) * 3,
        check_vma=False,
    )
```
